32 devices in a mesh: cube: 4 (over x, core), tile: 8 (over z, y).
Axes of the slice: x: 2, y: 2, z: 4, core: 2. Of those that a mesh axis runs over, the one named last changes fastest.
Arguments:
- leaf_fronts: float32 [32, 1024, 4, 2048], P(None, 'cube', None, 'tile'), as said below
- middle_fronts: float32 [16, 1024, 4, 2048], P(None, 'cube', None, 'tile'), as said below
- root_front: float32 [8, 1024, 4, 2048], P(None, 'cube', None, 'tile'), as said below
- leaf_scatter: int32 [4, 32, 256], replicated, may hold values from 0 to 255, each once within a row
- middle_scatter: int32 [2, 32, 256], replicated, may hold values from 0 to 255, each once within a row
- leaf_orders: int32 [4], replicated, may hold values from 4096 to 8192, as said below
- middle_orders: int32 [2], replicated, may hold values from 4096 to 8192, as said below
Outputs:
- leaf_panel: bfloat16 [32, 4, 256, 256], P(None, 'cube', 'tile')
- middle_panel: bfloat16 [16, 4, 256, 256], P(None, 'cube', 'tile')
- root_panel: bfloat16 [8, 4, 256, 256], P(None, 'cube', 'tile')
- root_schur: bfloat16 [8, 1024, 4, 2048], P(None, 'cube', None, 'tile')
The draws below stay inside these ranges and needn't reach their ends.
Inputs may be any that keep to these rules, and one draw needn't show every extreme that they name: `leaf_fronts`: each front is symmetric and positive definite. `middle_fronts`: each front is symmetric and positive definite. `root_front`: the front is symmetric and positive definite. `leaf_orders`: some front of the level has all 8192 rows live. `middle_orders`: some front of the level has all 8192 rows live.
All inputs are finite; a program needn't handle non-finite values.
Results may differ from the reference program's by a relative error of at most 0.0052.
Values may be sent and summed in bfloat16 or wider, within the bound.
No kernel may reach another device: no remote copies, remote signals or barrier semaphores. Data moves between devices by JAX's collectives and lax.ppermute only.
A program may use at most 256 MiB of HBM per device.

```python
import math
import jax
import jax.numpy as jnp
from jax import lax

PANEL = 256
NTILES = 32
ORDER = 8192
N_CUBE = 4
N_TILE = 8


pivot_diagonal = 8.0


def stored_layout_drawn(natural, fronts):
    groups = N_CUBE // fronts
    rows_per = NTILES // groups
    col_tiles = NTILES // N_TILE
    blocks = natural.reshape(fronts, rows_per, groups, PANEL, col_tiles, N_TILE, PANEL)
    blocks = jnp.transpose(blocks, (1, 0, 2, 3, 4, 5, 6))
    return blocks.reshape(rows_per, N_CUBE * PANEL, col_tiles, N_TILE * PANEL)


def place_pivot(pivot_block, side_block, rest_block, pivot_tile):
    cut_row = pivot_tile * PANEL
    upper_rows = jnp.concatenate([rest_block[:cut_row, :cut_row], side_block[:cut_row], rest_block[:cut_row, cut_row:]], axis=1)
    middle = jnp.concatenate([side_block[:cut_row].T, pivot_block, side_block[cut_row:].T], axis=1)
    lower_rows = jnp.concatenate([rest_block[cut_row:, :cut_row], side_block[cut_row:], rest_block[cut_row:, cut_row:]], axis=1)
    return jnp.concatenate([upper_rows, middle, lower_rows], axis=0)


def coupled_front(key, pivot_tile):
    tri_key, side_key, diag_key = jax.random.split(key, 3)
    rest_rows = ORDER - PANEL
    spread = 0.6 / math.sqrt(PANEL)
    strict_part = jax.random.uniform(tri_key, (PANEL, PANEL), jnp.float32, -spread, spread)
    tile_pos = jnp.arange(PANEL)
    strict_part = jnp.where(tile_pos[:, None] > tile_pos[None, :], strict_part, 0.0)
    leading = jnp.sqrt(1.0 - jnp.sum(strict_part * strict_part, axis=1))
    unit_rows = strict_part + jnp.diag(leading)
    couplings = jnp.clip(jax.random.normal(side_key, (rest_rows, 2 * PANEL), jnp.float32), -4.0, 4.0)
    diag_extra = jnp.exp(jax.random.uniform(diag_key, (rest_rows,), jnp.float32, math.log(0.25), math.log(0.5)))
    couplings = couplings / math.sqrt(PANEL)
    pivot_block = pivot_diagonal * jnp.dot(unit_rows, unit_rows.T, precision=lax.Precision.HIGHEST)
    pivot_block = 0.5 * (pivot_block + pivot_block.T)
    pivot_block = jnp.where(tile_pos[:, None] == tile_pos[None, :], pivot_diagonal, pivot_block)
    side_block = math.sqrt(pivot_diagonal) * jnp.dot(couplings[:, :PANEL], unit_rows.T, precision=lax.Precision.HIGHEST)
    rest_block = jnp.dot(couplings, couplings.T, precision=lax.Precision.HIGHEST)
    rest_block = 0.5 * (rest_block + rest_block.T)
    rest_pos = jnp.arange(rest_rows)
    rest_block = rest_block.at[rest_pos, rest_pos].add(diag_extra)
    return place_pivot(pivot_block, side_block, rest_block, pivot_tile).astype(jnp.float32)


def front_stack(key, fronts, pivot_tile):
    natural = jnp.stack([coupled_front(jax.random.fold_in(key, front_id), pivot_tile) for front_id in range(fronts)])
    return stored_layout_drawn(natural, fronts)


def live_orders(key, fronts):
    low_key, pick_key = jax.random.split(key)
    drawn = jax.random.randint(low_key, (fronts,), ORDER // 2, ORDER + 1, dtype=jnp.int32)
    chosen = jax.random.randint(pick_key, (), 0, fronts, dtype=jnp.int32)
    return jnp.where(jnp.arange(fronts, dtype=jnp.int32) == chosen, ORDER, drawn).astype(jnp.int32)


def draw_leaf_fronts(key, part):
    return front_stack(jax.random.fold_in(key, 11), 4, 0)


def draw_middle_fronts(key, part):
    return front_stack(jax.random.fold_in(key, 12), 2, 1)


def draw_root_front(key, part):
    return front_stack(jax.random.fold_in(key, 13), 1, 2)


def draw_leaf_orders(key, part):
    return live_orders(jax.random.fold_in(key, 21), 4)


def draw_middle_orders(key, part):
    return live_orders(jax.random.fold_in(key, 22), 2)


def setup_inputs(seed: int = 0) -> dict:
    keys = jax.random.split(jax.random.key(seed), 8)
    return {
        "leaf_fronts": draw_leaf_fronts(jax.random.fold_in(keys[7], 71), 0),
        "middle_fronts": draw_middle_fronts(jax.random.fold_in(keys[7], 71), 0),
        "root_front": draw_root_front(jax.random.fold_in(keys[7], 71), 0),
        "leaf_scatter": jax.vmap(lambda own: jax.random.permutation(own, PANEL))(jax.random.split(keys[3], 4 * NTILES)).reshape((4, NTILES, PANEL)).astype(jnp.int32),
        "middle_scatter": jax.vmap(lambda own: jax.random.permutation(own, PANEL))(jax.random.split(keys[4], 2 * NTILES)).reshape((2, NTILES, PANEL)).astype(jnp.int32),
        "leaf_orders": draw_leaf_orders(jax.random.fold_in(keys[7], 71), 0),
        "middle_orders": draw_middle_orders(jax.random.fold_in(keys[7], 71), 0),
    }


def natural_layout(stored, fronts):
    groups = N_CUBE // fronts
    rows_per = NTILES // groups
    col_tiles = NTILES // N_TILE
    blocks = stored.reshape(rows_per, fronts, groups, PANEL, col_tiles, N_TILE, PANEL)
    blocks = jnp.transpose(blocks, (1, 0, 2, 3, 4, 5, 6))
    return blocks.reshape(fronts, ORDER, ORDER)

def stored_layout(natural, fronts):
    groups = N_CUBE // fronts
    rows_per = NTILES // groups
    col_tiles = NTILES // N_TILE
    blocks = natural.reshape(fronts, rows_per, groups, PANEL, col_tiles, N_TILE, PANEL)
    blocks = jnp.transpose(blocks, (1, 0, 2, 3, 4, 5, 6))
    return blocks.reshape(rows_per, N_CUBE * PANEL, col_tiles, N_TILE * PANEL)

def panel_layout(panels, fronts):
    groups = N_CUBE // fronts
    rows_per = NTILES // groups
    blocks = panels.reshape(fronts, rows_per, groups, PANEL, PANEL)
    blocks = jnp.transpose(blocks, (1, 0, 2, 3, 4))
    return blocks.reshape(rows_per, N_CUBE, PANEL, PANEL)

def factor_front(whole, pivot_tile):
    first_row = pivot_tile * PANEL
    corner = whole[first_row:first_row + PANEL, first_row:first_row + PANEL]
    lower_factor = jnp.linalg.cholesky(corner)
    column = whole[:, first_row:first_row + PANEL]
    solved = jax.scipy.linalg.solve_triangular(lower_factor, column.T, lower=True).T
    solved = solved.at[first_row:first_row + PANEL].set(lower_factor)
    factor_panel = solved.astype(jnp.bfloat16)
    zeroed = factor_panel.at[first_row:first_row + PANEL].set(jnp.zeros((PANEL, PANEL), jnp.bfloat16))
    update = jnp.dot(zeroed.astype(jnp.float32), zeroed.T.astype(jnp.float32), preferred_element_type=jnp.float32)
    return (factor_panel, whole - update)

def extend_add(schur_part, live_order, pivot_tile, scatter_rows):
    positions = jnp.arange(ORDER, dtype=jnp.int32)
    keep_rows = ((positions < live_order) & (positions // PANEL != pivot_tile)).astype(jnp.float32)
    masked = schur_part * keep_rows[:, None] * keep_rows[None, :]
    target = positions // PANEL * PANEL + scatter_rows.reshape(-1).astype(jnp.int32)
    rows_done = jnp.zeros((ORDER, ORDER), jnp.float32).at[target].set(masked)
    return jnp.zeros((ORDER, ORDER), jnp.float32).at[:, target].set(rows_done)

def reference(leaf_fronts, middle_fronts, root_front, leaf_scatter, middle_scatter, leaf_orders, middle_orders):
    leaf_natural = natural_layout(leaf_fronts, 4)
    leaf_panels = []
    lifted = []
    for front_id in range(4):
        factor_panel, schur_part = factor_front(leaf_natural[front_id], 0)
        leaf_panels.append(factor_panel)
        lifted.append(extend_add(schur_part, leaf_orders[front_id], 0, leaf_scatter[front_id]))
    middle_natural = natural_layout(middle_fronts, 2)
    middle_panels = []
    raised = []
    for front_id in range(2):
        assembled = middle_natural[front_id] + lifted[2 * front_id] + lifted[2 * front_id + 1]
        factor_panel, schur_part = factor_front(assembled, 1)
        middle_panels.append(factor_panel)
        raised.append(extend_add(schur_part, middle_orders[front_id], 1, middle_scatter[front_id]))
    root_natural = natural_layout(root_front, 1)
    assembled = root_natural[0] + raised[0] + raised[1]
    factor_panel, schur_part = factor_front(assembled, 2)
    return (panel_layout(jnp.stack(leaf_panels), 4), panel_layout(jnp.stack(middle_panels), 2), panel_layout(factor_panel[None], 1), stored_layout(schur_part[None], 1).astype(jnp.bfloat16))
```

```python
import functools

import jax
import jax.numpy as jnp
from jax import lax
from jax.experimental import pallas as pl
from jax.experimental.pallas import tpu as pltpu
from jax.sharding import PartitionSpec as P

HIGHEST = lax.Precision.HIGHEST
F32 = jnp.float32
BF16 = jnp.bfloat16
LANES = 128
BLOCK = 32
VMEM = 50 << 20


def partner(block, apart):
    count = lax.axis_size("cube")
    route = [(low, low ^ 1 << apart) for low in range(count)]
    return lax.ppermute(block, "cube", route)


def group_sum(value, bits):
    for bit in range(bits):
        value = value + partner(value, bit)
    return value


def tile_spread(value, source):
    count = lax.axis_size("tile")
    me = lax.axis_index("tile")
    have = {source}
    bit = count >> 1
    while bit:
        route = [(t, t ^ bit) for t in sorted(have)]
        moved = lax.ppermute(value, "tile", route)
        holds = functools.reduce(jnp.logical_or, [me == t for t in sorted(have)])
        value = jnp.where(holds, value, moved)
        have |= {t ^ bit for t in have}
        bit >>= 1
    return value


def row_spread(value):
    n_cube, n_tile = lax.axis_size("cube"), lax.axis_size("tile")
    cube, tile = lax.axis_index("cube"), lax.axis_index("tile")
    own, other = value, None
    low_bits = n_cube.bit_length() - 1
    order = [b for b in range(low_bits - 1, -1, -1)]
    missing = tile % n_cube ^ cube

    def step(block, bit, done):
        route = []
        for m in range(n_cube):
            for t in range(n_tile):
                if ((t % n_cube) ^ m) & ~done == 0:
                    route.append((m * n_tile + t, m * n_tile + (t ^ bit)))
        moved = lax.ppermute(block, ("cube", "tile"), route)
        return jnp.where(missing & bit != 0, moved, block)

    done = 0
    for at, low in enumerate(order):
        bit = 1 << low
        own = step(own, bit, done)
        if other is not None:
            other = step(other, bit, done)
        done |= bit
        if at == 0:
            route = []
            for m in range(n_cube):
                for t in range(n_tile):
                    if ((t % n_cube) ^ m) & ~done == 0:
                        route.append((m * n_tile + t, m * n_tile + (t ^ n_cube)))
            other = lax.ppermute(own, ("cube", "tile"), route)
    return own, other


def split3(value):
    high = value.astype(BF16)
    rest = value - high.astype(F32)
    middle = rest.astype(BF16)
    low = (rest - middle.astype(F32)).astype(BF16)
    return high, middle, low


def newton_rsqrt(value):
    guess = lax.rsqrt(value)
    return guess * (1.5 - 0.5 * value * guess * guess)


def newton_reciprocal(value):
    guess = pl.reciprocal(value, approx=True)
    guess = guess * (2.0 - value * guess)
    return guess * (2.0 - value * guess)


def cholesky_kernel(a_ref, upper_ref, inverse_ref, work):
    n = a_ref.shape[0]
    rows = lax.broadcasted_iota(jnp.int32, (n, n), 0)
    cols = lax.broadcasted_iota(jnp.int32, (n, n), 1)
    work[:, :n] = a_ref[...]
    work[:, n:] = jnp.where(rows == cols, 1.0, 0.0)
    for start in range(0, n, BLOCK):
        stop = start + BLOCK
        low = start // LANES * LANES
        high = n + -(-stop // LANES) * LANES
        parts = [
            work[start:stop, at : at + LANES] for at in range(low, high, LANES)
        ]
        for j in range(0, BLOCK, 2):
            lane = start - low + j
            c0 = jnp.broadcast_to(parts[0][:, lane : lane + 1], (BLOCK, LANES))
            c1 = jnp.broadcast_to(parts[0][:, lane + 1 : lane + 2], (BLOCK, LANES))
            a = c0[j : j + 1, :]
            b = c0[j + 1 : j + 2, :]
            c = c1[j + 1 : j + 2, :]
            det = a * c - b * b
            over = newton_reciprocal(det)
            g0 = (c * c0 - b * c1) * over
            g1 = (a * c1 - b * c0) * over
            inv_a = newton_rsqrt(a)
            below = b * inv_a
            inv_c = newton_rsqrt(c - below * below)
            for at, part in enumerate(parts):
                r0 = part[j : j + 1, :]
                r1 = part[j + 1 : j + 2, :]
                u0 = r0 * inv_a
                u1 = (r1 - below * u0) * inv_c
                lanes = slice(low + at * LANES, low + (at + 1) * LANES)
                work[start + j : start + j + 1, lanes] = u0
                work[start + j + 1 : start + j + 2, lanes] = u1
                parts[at] = part - g0 * r0 - g1 * r1
        if stop < n:
            block = work[start:stop, low:high]
            h, m, l = split3(block)
            right = jnp.concatenate([h, m, h, l, m, h], axis=0)
            keep = stop // LANES * LANES
            hl, ml, ll = (x[:, keep - low : n - low] for x in (h, m, l))
            left = jnp.concatenate([hl, hl, ml, hl, ml, ll], axis=0)
            update = lax.dot_general(
                left, right, (((0,), (0,)), ((), ())), preferred_element_type=F32
            )
            work[stop:, low:high] -= update[stop - keep :]
    upper_ref[...] = jnp.where(rows <= cols, work[:, :n], 0.0)
    inverse_ref[...] = jnp.where(rows >= cols, work[:, n:], 0.0)


def cholesky(corner):
    n = corner.shape[0]
    shape = jax.ShapeDtypeStruct((n, n), F32)
    return pl.pallas_call(
        cholesky_kernel,
        out_shape=(shape, shape),
        scratch_shapes=[pltpu.VMEM((n, 2 * n), F32)],
        compiler_params=pltpu.CompilerParams(vmem_limit_bytes=VMEM),
        cost_estimate=pl.CostEstimate(
            flops=20_000_000, bytes_accessed=12 * n * n, transcendentals=0
        ),
        name="cholesky_and_inverse",
    )(corner)


def lane_rows(front):
    tiles, n, col_tiles, _ = front.shape
    halves = n // LANES
    split = front.reshape(tiles, n, col_tiles, halves, LANES)
    return split.transpose(0, 1, 3, 2, 4).reshape(-1, LANES)


def tile_of(ref, at, col_tiles, n):
    halves = n // LANES
    return jnp.concatenate(
        [
            ref[pl.ds(h * col_tiles + at, n, stride=col_tiles * halves), :]
            for h in range(halves)
        ],
        axis=1,
    )


def one_hot(places, n):
    slots = lax.broadcasted_iota(jnp.int32, (n, n), 0)
    return jnp.where(slots == places, 1.0, 0.0).astype(BF16)


def mxu(left, right):
    return jnp.dot(left, right, preferred_element_type=F32)


def mxu_t(left, right):
    return lax.dot_general(
        left, right, (((1,), (1,)), ((), ())), preferred_element_type=F32
    )


def lift_kernel(pick, x_ref, row_ref, col_ref, out_ref):
    col_tiles, n = out_ref.shape[1], out_ref.shape[2]
    row_hot = one_hot(row_ref[0], n)
    for c in range(col_tiles):
        tile = tile_of(x_ref, c, col_tiles, n).astype(BF16)
        half = mxu(row_hot, tile).astype(BF16)
        out_ref[0, c] = mxu(half, col_ref[c]).astype(BF16)


def lift(pick, front_rows, tiles, col_tiles, n, row_places, col_hot):
    rows = front_rows.shape[0] // tiles
    count = tiles // 2
    flops = count * col_tiles * 2 * 2 * n**3
    return pl.pallas_call(
        lift_kernel,
        grid_spec=pltpu.PrefetchScalarGridSpec(
            num_scalar_prefetch=1,
            grid=(count,),
            in_specs=[
                pl.BlockSpec((rows, LANES), lambda i, s: (2 * i + s[0], 0)),
                pl.BlockSpec((1, 1, n), lambda i, s: (2 * i + s[0], 0, 0)),
                pl.BlockSpec((col_tiles, n, n), lambda i, s: (0, 0, 0)),
            ],
            out_specs=pl.BlockSpec((1, col_tiles, n, n), lambda i, s: (i, 0, 0, 0)),
        ),
        out_shape=jax.ShapeDtypeStruct((count, col_tiles, n, n), BF16),
        compiler_params=pltpu.CompilerParams(vmem_limit_bytes=VMEM),
        cost_estimate=pl.CostEstimate(
            flops=flops,
            bytes_accessed=count * col_tiles * n * n * 6,
            transcendentals=0,
        ),
        name="lift_leaf",
    )(pick, front_rows, row_places, col_hot)


def climb_kernel(
    pick, x_ref, mid_ref, got_ref, row2_ref, row1_ref, col2_ref, col1_ref, out_ref
):
    col_tiles, n = out_ref.shape[1], out_ref.shape[2]
    hot2 = one_hot(row2_ref[0], n)
    hot1 = one_hot(row1_ref[0], n)
    for c in range(col_tiles):
        tile = tile_of(x_ref, c, col_tiles, n).astype(BF16)
        half = mxu(hot2, tile).astype(BF16)
        whole = mxu(half, col2_ref[c]) + got_ref[0, c].astype(F32)
        whole = (whole + tile_of(mid_ref, c, col_tiles, n)).astype(BF16)
        half = mxu(hot1, whole).astype(BF16)
        out_ref[0, c] = mxu(half, col1_ref[c]).astype(BF16)


def climb(pick, leaf_rows, mid_rows, got, tiles, row2, row1, col2, col1):
    col_tiles, n = got.shape[1], got.shape[2]
    count = tiles // 2
    rows = mid_rows.shape[0] // tiles
    flops = count * col_tiles * 4 * 2 * n**3

    def mid(i, s):
        return 2 * i + s[1]

    def leaf(i, s):
        return 2 * mid(i, s) + s[0]

    return pl.pallas_call(
        climb_kernel,
        grid_spec=pltpu.PrefetchScalarGridSpec(
            num_scalar_prefetch=1,
            grid=(count,),
            in_specs=[
                pl.BlockSpec((rows, LANES), lambda i, s: (leaf(i, s), 0)),
                pl.BlockSpec((rows, LANES), lambda i, s: (mid(i, s), 0)),
                pl.BlockSpec((1, col_tiles, n, n), lambda i, s: (mid(i, s), 0, 0, 0)),
                pl.BlockSpec((1, 1, n), lambda i, s: (leaf(i, s), 0, 0)),
                pl.BlockSpec((1, 1, n), lambda i, s: (mid(i, s), 0, 0)),
                pl.BlockSpec((col_tiles, n, n), lambda i, s: (0, 0, 0)),
                pl.BlockSpec((col_tiles, n, n), lambda i, s: (0, 0, 0)),
            ],
            out_specs=pl.BlockSpec((1, col_tiles, n, n), lambda i, s: (i, 0, 0, 0)),
        ),
        out_shape=jax.ShapeDtypeStruct((count, col_tiles, n, n), BF16),
        compiler_params=pltpu.CompilerParams(vmem_limit_bytes=VMEM),
        cost_estimate=pl.CostEstimate(
            flops=flops,
            bytes_accessed=count * col_tiles * n * n * 12,
            transcendentals=0,
        ),
        name="climb_middle",
    )(pick, leaf_rows, mid_rows, got, row2, row1, col2, col1)


def finish_kernel(pick, root_ref, kept_ref, got_ref, *refs):
    panels = len(refs) // 3
    rows_own, rows_other = refs[:panels], refs[panels : 2 * panels]
    cols = refs[2 * panels : 3 * panels]
    out_ref, scratch = refs[3 * panels :]
    col_tiles, n = kept_ref.shape[1], kept_ref.shape[2]
    halves = n // LANES

    def work(row_refs):
        for c in range(col_tiles):
            total = tile_of(root_ref, c, col_tiles, n)
            total += kept_ref[0, c].astype(F32) + got_ref[0, c].astype(F32)
            update = None
            for row_ref, col_ref in zip(row_refs, cols):
                for k in range(row_ref.shape[0]):
                    term = mxu_t(row_ref[k, 0], col_ref[k, c])
                    update = term if update is None else update + term
            total -= update
            for h in range(halves):
                scratch[pl.ds(h * col_tiles + c, n, stride=col_tiles * halves), :] = (
                    total[:, h * LANES : (h + 1) * LANES]
                )
        out_ref[...] = scratch[...].astype(BF16)

    @pl.when(pl.program_id(0) == 0)
    def _():
        work(rows_own)

    @pl.when(pl.program_id(0) != 0)
    def _():
        work(rows_other)


def finish(pick, root_rows, kept, got, own, other, cols):
    tiles, col_tiles, n, _ = kept.shape
    spread = tiles // col_tiles
    rows = root_rows.shape[0] // tiles

    def at(q, c, s):
        return c * spread + (s[0] ^ q)

    row_specs = [
        [
            pl.BlockSpec(
                (x.shape[0], 1, n, n),
                functools.partial(lambda first, q, c, s: (0, jnp.where(q == 0, c, col_tiles - 1) if first else jnp.where(q == 0, 0, c), 0, 0), first),
            )
            for x in own
        ]
        for first in (True, False)
    ]
    count = sum(x.shape[0] for x in own)
    return pl.pallas_call(
        finish_kernel,
        grid_spec=pltpu.PrefetchScalarGridSpec(
            num_scalar_prefetch=1,
            grid=(spread, col_tiles),
            in_specs=[
                pl.BlockSpec((rows, LANES), lambda q, c, s: (at(q, c, s), 0)),
                pl.BlockSpec((1, col_tiles, n, n), lambda q, c, s: (at(q, c, s), 0, 0, 0)),
                pl.BlockSpec((1, col_tiles, n, n), lambda q, c, s: (at(q, c, s), 0, 0, 0)),
                *row_specs[0],
                *row_specs[1],
                *[pl.BlockSpec(x.shape, lambda q, c, s: (0, 0, 0, 0)) for x in cols],
            ],
            out_specs=pl.BlockSpec((rows, LANES), lambda q, c, s: (at(q, c, s), 0)),
            scratch_shapes=[pltpu.VMEM((rows, LANES), F32)],
        ),
        out_shape=jax.ShapeDtypeStruct(root_rows.shape, BF16),
        compiler_params=pltpu.CompilerParams(vmem_limit_bytes=VMEM),
        cost_estimate=pl.CostEstimate(
            flops=tiles * col_tiles * count * 2 * n**3,
            bytes_accessed=tiles * col_tiles * n * n * 10,
            transcendentals=0,
        ),
        name="finish_root",
    )(pick, root_rows, kept, got, *own, *other, *cols)


def strip(front, tile_row, groups, member, bits):
    piece = jnp.transpose(front[tile_row // groups], (1, 0, 2))
    if groups > 1:
        piece = jnp.where(member == tile_row % groups, piece, 0.0)
    return group_sum(piece, bits)


def solve(inverse, rows):
    return jnp.einsum("ks,csj->cjk", inverse, rows, precision=HIGHEST)


def placed(hot, panels):
    return jnp.einsum(
        "cqj,cjk->cqk", hot, panels, preferred_element_type=F32
    ).astype(BF16)


def moved(row_hot, block, col_hot):
    out = jnp.einsum("qs,csj->cqj", row_hot, block, precision=HIGHEST)
    return jnp.einsum("cqj,cpj->cqp", out, col_hot, precision=HIGHEST)


def product(rows, cols):
    return jnp.einsum("fsk,fcjk->csj", rows, cols, preferred_element_type=F32)


def hots(places, n):
    slots = jnp.arange(n, dtype=jnp.int32)
    return (places[:, None, :] == slots[None, :, None]).astype(BF16)


def places_of(scatter, order, pivot):
    tiles, n = scatter.shape
    tile_ids = jnp.arange(tiles, dtype=jnp.int32)[:, None]
    rows = tile_ids * n + jnp.arange(n, dtype=jnp.int32)[None, :]
    return jnp.where((rows < order) & (tile_ids != pivot), scatter, -1)


def panel_slices(panel_pair, sizes, members):
    n_tile = lax.axis_size("tile")
    stacked = jnp.stack(panel_pair)
    count, col_tiles, n, width = stacked.shape
    cut = stacked.reshape(count, col_tiles, n_tile, n // n_tile, width)
    cut = jnp.transpose(cut, (2, 0, 1, 3, 4))
    got = lax.all_to_all(cut, "tile", 0, 0, tiled=True)
    out = []
    for at in range(count):
        tiles = jnp.transpose(got[:, at], (1, 0, 2, 3))
        tiles = tiles.reshape(-1, sizes[at], n // n_tile, width)
        out.append(lax.dynamic_index_in_dim(tiles, members[at], 1, keepdims=True))
    return out


def per_device(
    leaf_fronts, middle_fronts, root_front, leaf_scatter, middle_scatter, leaf_orders, middle_orders
):
    n_cube, n_tile = lax.axis_size("cube"), lax.axis_size("tile")
    cube, tile = lax.axis_index("cube"), lax.axis_index("tile")
    g2, g1 = n_cube // 4, n_cube // 2
    bit2, bit1 = g2.bit_length() - 1, g1.bit_length() - 1
    f, p = cube // g2, cube // g1
    m2, m1 = cube % g2, cube % g1
    leaf_tiles, n, col_tiles, _ = leaf_fronts.shape
    mid_tiles = middle_fronts.shape[0]
    col_ids = jnp.arange(col_tiles, dtype=jnp.int32) * n_tile + tile
    spread = n_tile // n_cube

    places2 = places_of(leaf_scatter[f], leaf_orders[f], 0)
    places1 = places_of(middle_scatter[p], middle_orders[p], 1)
    cols2 = jnp.take(places2, col_ids, axis=0)
    cols1 = jnp.take(places1, col_ids, axis=0)
    hot2, hot1 = hots(cols2, n), hots(cols1, n)
    top2, top1 = hots(places2[1:3], n), hots(places1[2:3], n)
    slots = jnp.arange(n, dtype=jnp.int32)
    turned2 = (cols2[:, :, None] == slots).astype(BF16)
    turned1 = (cols1[:, :, None] == slots).astype(BF16)

    def at_tile(strips, tile_id):
        return strips[tile_id // n_tile]

    leaf0 = strip(leaf_fronts, 0, g2, m2, bit2)
    corner2 = tile_spread(at_tile(leaf0, 0), 0)

    rows2 = places2.reshape(-1, g2, 1, n)[:, m2]
    rows1 = places1.reshape(-1, g1, 1, n)[:, m1]
    parity2, parity1 = f % 2, p % 2
    leaf_lanes, mid_lanes, root_lanes = map(
        lane_rows, (leaf_fronts, middle_fronts, root_front)
    )
    pick = (1 - parity2).reshape(1)
    sent2 = lift(pick, leaf_lanes, leaf_tiles, col_tiles, n, rows2, turned2)
    got2 = partner(sent2, bit2)

    lifted = jnp.stack(
        [
            moved(top2[r - 1].astype(F32), strip(leaf_fronts, r, g2, m2, bit2), hot2.astype(F32))
            + strip(middle_fronts, r, g1, m1, bit2)
            for r in (1, 2)
        ]
    )
    base1 = lifted + partner(lifted, bit2)
    raised = moved(top1[0].astype(F32), base1[1], hot1.astype(F32))
    raised = raised + strip(root_front, 2, n_cube, cube, bit1)
    base0 = raised + partner(raised, bit1)
    first = tile_spread(
        jnp.stack([at_tile(leaf0, 1), at_tile(base1[0], 1)]), 1 % n_tile
    )
    second = tile_spread(
        jnp.stack([at_tile(leaf0, 2), at_tile(base1[0], 2), at_tile(base0, 2)]),
        2 % n_tile,
    )

    upper2, inverse2 = cholesky(corner2)
    panel2 = solve(inverse2, leaf0).astype(BF16)
    ahead2 = solve(inverse2, jnp.stack([first[0], second[0]])).astype(BF16)
    lift2 = jnp.concatenate([placed(hot2, panel2), placed(top2, ahead2)])
    pair2 = jnp.stack([lift2, partner(lift2, bit2)])

    mine2, one2, two2 = pair2[:, :col_tiles], pair2[:, col_tiles], pair2[:, col_tiles + 1]
    ends = product(one2, pair2[:, col_tiles:])
    upper1, inverse1 = cholesky(first[1] - ends[0])
    front1 = base1[0] - product(one2, mine2)
    panel1 = solve(
        inverse1, jnp.concatenate([front1, (second[1] - ends[1])[None]])
    ).astype(BF16)

    both1 = jnp.concatenate([hot1, top1])
    climb2 = placed(both1, jnp.concatenate([lift2[:col_tiles], lift2[col_tiles + 1 :]]))
    across2 = jnp.stack([climb2, partner(climb2, bit1)])
    four2 = jnp.concatenate([across2, partner(across2, bit2)])
    climb1 = placed(both1, panel1)
    two1 = jnp.stack([climb1, partner(climb1, bit1)])
    six = jnp.concatenate([four2, two1])
    ends = product(six[:, col_tiles], six)
    upper0, inverse0 = cholesky(second[2] - ends[col_tiles])
    panel0 = solve(inverse0, base0 - ends[:col_tiles]).astype(BF16)
    panel0 = jnp.where((col_ids == 2)[:, None, None], jnp.zeros_like(panel0), panel0)

    cols = [four2[:, :col_tiles], two1[:, :col_tiles], panel0[None]]
    pairs = [row_spread(x) for x in cols]
    own, other = [x[0] for x in pairs], [x[1] for x in pairs]

    picks = jnp.stack([parity2, 1 - parity1])
    sent1 = climb(picks, leaf_lanes, mid_lanes, got2, mid_tiles, rows2, rows1, turned2, turned1)
    got1 = partner(sent1, bit1)
    picks = jnp.stack([parity2, parity1])
    kept1 = climb(picks, leaf_lanes, mid_lanes, got2, mid_tiles, rows2, rows1, turned2, turned1)
    high = tile // n_cube
    schur = finish(high.reshape(1), root_lanes, kept1, got1, own, other, cols)
    schur = schur.reshape(root_front.shape[0], n, n // LANES, col_tiles, LANES)
    schur = schur.transpose(0, 1, 3, 2, 4).reshape(root_front.shape)

    def with_corner(panel, upper, pivot):
        return jnp.where((col_ids == pivot)[:, None, None], upper.T.astype(BF16), panel)

    leaf_panel, middle_panel = panel_slices(
        (with_corner(panel2, upper2, 0), with_corner(panel1[:col_tiles], upper1, 1)),
        (g2, g1),
        (m2, m1),
    )
    part = n // n_tile
    cuts = [
        lax.dynamic_slice_in_dim(x[-1][0], tile * part, part, 1) for x in (own, other)
    ]
    ordered = [jnp.where(high == j, cuts[0], cuts[1]) for j in range(spread)]
    root_panel = jnp.stack(ordered, 1).reshape(-1, part, n)
    root_ids = jnp.arange(root_front.shape[0], dtype=jnp.int32) * n_cube + cube
    corner_cut = lax.dynamic_slice_in_dim(upper0.T.astype(BF16), tile * part, part, 0)
    root_panel = jnp.where((root_ids == 2)[:, None, None], corner_cut, root_panel)
    return leaf_panel, middle_panel, root_panel[:, None], schur


def solution(mesh):
    front = P(None, "cube", None, "tile")
    panel = P(None, "cube", "tile", None)
    return jax.shard_map(
        per_device,
        mesh=mesh,
        in_specs=(front, front, front, P(), P(), P(), P()),
        out_specs=(panel, panel, panel, front),
        check_vma=False,
    )
```

```python
import functools

import jax
import jax.numpy as jnp
from jax import lax
from jax.experimental import pallas as pl
from jax.experimental.pallas import tpu as pltpu
from jax.sharding import PartitionSpec as P

HIGHEST = lax.Precision.HIGHEST
F32 = jnp.float32
BF16 = jnp.bfloat16
LANES = 128
BLOCK = 32
WIDTH = 8
VMEM = 50 << 20


def partner(block, apart):
    count = lax.axis_size("cube")
    route = [(low, low ^ 1 << apart) for low in range(count)]
    return lax.ppermute(block, "cube", route)


def group_sum(value, bits):
    for bit in range(bits):
        value = value + partner(value, bit)
    return value


def tile_spread(value):
    count = lax.axis_size("tile")
    me = lax.axis_index("tile")
    bit, filled = count >> 1, 1
    while bit >= 4:
        route = [
            (base + t, base + t + bit)
            for base in range(0, count, 2 * bit)
            if base % (2 * bit) == 0 and base // (2 * bit) < filled
            for t in range(3)
        ]
        moved = lax.ppermute(value, "tile", route)
        value = jnp.where(me & bit != 0, moved, value)
        filled *= 2
        bit >>= 1
    other = lax.ppermute(
        value, "tile", [(t, t ^ 1) for t in range(count) if t % 4 != 3]
    )
    even = me & 1 == 0
    pair = jnp.stack([jnp.where(even, value, other), jnp.where(even, other, value)])
    across = lax.ppermute(pair, "tile", [(t, t ^ 2) for t in range(count)])
    front = me & 2 == 0
    low = jnp.where(front, pair, across)
    return low[0], low[1], jnp.where(front, across[0], pair[0])


def row_spread(value):
    n_cube, n_tile = lax.axis_size("cube"), lax.axis_size("tile")
    cube, tile = lax.axis_index("cube"), lax.axis_index("tile")
    own, other = value, None
    low_bits = n_cube.bit_length() - 1
    order = [b for b in range(low_bits - 1, -1, -1)]
    missing = tile % n_cube ^ cube

    def step(block, bit, done):
        route = []
        for m in range(n_cube):
            for t in range(n_tile):
                if ((t % n_cube) ^ m) & ~done == 0:
                    route.append((m * n_tile + t, m * n_tile + (t ^ bit)))
        moved = lax.ppermute(block, ("cube", "tile"), route)
        return jnp.where(missing & bit != 0, moved, block)

    done = 0
    for at, low in enumerate(order):
        bit = 1 << low
        own = step(own, bit, done)
        if other is not None:
            other = step(other, bit, done)
        done |= bit
        if at == 0:
            route = []
            for m in range(n_cube):
                for t in range(n_tile):
                    if ((t % n_cube) ^ m) & ~done == 0:
                        route.append((m * n_tile + t, m * n_tile + (t ^ n_cube)))
            other = lax.ppermute(own, ("cube", "tile"), route)
    return own, other


def split3(value):
    high = value.astype(BF16)
    rest = value - high.astype(F32)
    middle = rest.astype(BF16)
    low = (rest - middle.astype(F32)).astype(BF16)
    return high, middle, low


def newton_rsqrt(value):
    guess = lax.rsqrt(value)
    return guess * (1.5 - 0.5 * value * guess * guess)


def newton_reciprocal(value):
    guess = pl.reciprocal(value, approx=True)
    return guess * (2.0 - value * guess)


def cholesky_kernel(a_ref, _, upper_ref, inverse_ref, work):
    n = a_ref.shape[0]
    rows = lax.broadcasted_iota(jnp.int32, (n, n), 0)
    cols = lax.broadcasted_iota(jnp.int32, (n, n), 1)
    work[:, :n] = a_ref[...]
    work[:, n:] = jnp.where(rows == cols, 1.0, 0.0)
    for start in range(0, n, BLOCK):
        stop = start + BLOCK
        low = start // LANES * LANES
        high = n + -(-stop // LANES) * LANES
        parts = [
            work[start:stop, at : at + LANES] for at in range(low, high, LANES)
        ]
        for first in range(0, BLOCK, WIDTH):
            lane = start - low + first
            wide = [
                jnp.broadcast_to(parts[0][:, lane + i : lane + i + 1], (BLOCK, LANES))
                for i in range(WIDTH)
            ]
            for i in range(0, WIDTH, 2):
                j = first + i
                c0, c1 = wide[i], wide[i + 1]
                a = c0[j : j + 1, :]
                b = c0[j + 1 : j + 2, :]
                c = c1[j + 1 : j + 2, :]
                over = newton_reciprocal(a * c - b * b)
                g0 = (c * c0 - b * c1) * over
                g1 = (a * c1 - b * c0) * over
                for later in range(i + 2, WIDTH):
                    at = first + later
                    wide[later] = (
                        wide[later] - g0 * c0[at : at + 1, :] - g1 * c1[at : at + 1, :]
                    )
                inv_a = newton_rsqrt(a)
                below = b * inv_a
                inv_c = newton_rsqrt(c - below * below)
                for at, part in enumerate(parts):
                    r0 = part[j : j + 1, :]
                    r1 = part[j + 1 : j + 2, :]
                    u0 = r0 * inv_a
                    u1 = (r1 - below * u0) * inv_c
                    lanes = slice(low + at * LANES, low + (at + 1) * LANES)
                    work[start + j : start + j + 1, lanes] = u0
                    work[start + j + 1 : start + j + 2, lanes] = u1
                    parts[at] = part - g0 * r0 - g1 * r1
        if stop < n:
            block = work[start:stop, low:high]
            h, m, l = split3(block)
            right = jnp.concatenate([h, m, h, l, m, h], axis=0)
            keep = stop // LANES * LANES
            hl, ml, ll = (x[:, keep - low : n - low] for x in (h, m, l))
            left = jnp.concatenate([hl, hl, ml, hl, ml, ll], axis=0)
            update = lax.dot_general(
                left, right, (((0,), (0,)), ((), ())), preferred_element_type=F32
            )
            work[stop:, low:high] -= update[stop - keep :]
    upper_ref[...] = jnp.where(rows <= cols, work[:, :n], 0.0)
    inverse_ref[...] = jnp.where(rows >= cols, work[:, n:], 0.0)


def cholesky(corner, after):
    n = corner.shape[0]
    shape = jax.ShapeDtypeStruct((n, n), F32)
    return pl.pallas_call(
        cholesky_kernel,
        out_shape=(shape, shape),
        in_specs=[
            pl.BlockSpec(memory_space=pltpu.VMEM),
            pl.BlockSpec(memory_space=pl.ANY),
        ],
        scratch_shapes=[pltpu.VMEM((n, 2 * n), F32)],
        compiler_params=pltpu.CompilerParams(vmem_limit_bytes=VMEM),
        cost_estimate=pl.CostEstimate(
            flops=20_000_000, bytes_accessed=12 * n * n, transcendentals=0
        ),
        name="cholesky_and_inverse",
    )(corner, after)


def lane_rows(front):
    tiles, n, col_tiles, _ = front.shape
    halves = n // LANES
    split = front.reshape(tiles, n, col_tiles, halves, LANES)
    return split.transpose(0, 1, 3, 2, 4).reshape(-1, LANES)


def sorter(n, col_tiles):
    per_row = col_tiles * (n // LANES)
    rows = n // per_row
    to = jnp.arange(n, dtype=jnp.int32)
    source = to % rows * per_row + to // rows
    return (source[:, None] == to[None, :]).astype(BF16)


def chunk_pair(value, at, n):
    return jnp.concatenate(
        [value[at * n : (at + 1) * n], value[(at + 1) * n : (at + 2) * n]], axis=1
    )


def sort_tiles(block, sort, col_tiles):
    n = sort.shape[0]
    halves = n // LANES
    rows = n // (col_tiles * halves)
    pieces = [[] for _ in range(col_tiles * halves)]
    for at in range(0, col_tiles * halves, 2):
        both = mxu(sort, chunk_pair(block, at, n))
        for side in (both[:, :LANES], both[:, LANES:]):
            for k in range(len(pieces)):
                pieces[k].append(side[k * rows : (k + 1) * rows])
    whole = [jnp.concatenate(x, axis=0) for x in pieces]
    return [
        jnp.concatenate([whole[h * col_tiles + c] for h in range(halves)], axis=1)
        for c in range(col_tiles)
    ]


def sort_tiles_wide(block, sort, col_tiles):
    high = block.astype(BF16)
    low = (block - high.astype(F32)).astype(BF16)
    return [
        a + b
        for a, b in zip(
            sort_tiles(high, sort, col_tiles), sort_tiles(low, sort, col_tiles)
        )
    ]


def unsort_tiles(tiles, sort, out_ref):
    n = sort.shape[0]
    halves = n // LANES
    count = len(tiles) * halves
    rows = n // count
    lanes = [t[:, h * LANES : (h + 1) * LANES] for h in range(halves) for t in tiles]
    for at in range(0, count, 2):
        sides = [
            jnp.concatenate([x[k * rows : (k + 1) * rows] for x in lanes], axis=0)
            for k in (at, at + 1)
        ]
        both = lax.dot_general(
            sort,
            jnp.concatenate(sides, axis=1),
            (((0,), (0,)), ((), ())),
            preferred_element_type=F32,
        ).astype(BF16)
        out_ref[at * n : (at + 1) * n, :] = both[:, :LANES]
        out_ref[(at + 1) * n : (at + 2) * n, :] = both[:, LANES:]


def one_hot(places, n):
    slots = lax.broadcasted_iota(jnp.int32, (n, n), 0)
    return jnp.where(slots == places, 1.0, 0.0).astype(BF16)


def mxu(left, right):
    return jnp.dot(left, right, preferred_element_type=F32)


def mxu_t(left, right):
    return lax.dot_general(
        left, right, (((1,), (1,)), ((), ())), preferred_element_type=F32
    )


def lift_kernel(pick, x_ref, row_ref, col_ref, sort_ref, out_ref):
    col_tiles, n = out_ref.shape[1], out_ref.shape[2]
    row_hot = one_hot(row_ref[0], n)
    tiles = sort_tiles(x_ref[...].astype(BF16), sort_ref[...], col_tiles)
    for c in range(col_tiles):
        half = mxu(row_hot, tiles[c].astype(BF16)).astype(BF16)
        out_ref[0, c] = mxu(half, col_ref[c]).astype(BF16)


def whole_spec(x):
    return pl.BlockSpec(x.shape, lambda *_: (0,) * x.ndim)


def lift(pick, front_rows, tiles, row_places, col_hot, sort):
    col_tiles, n, _ = col_hot.shape
    rows = front_rows.shape[0] // tiles
    count = tiles // 4

    def at(i, s):
        return 2 * (2 * i + s[1]) + s[0]

    return pl.pallas_call(
        lift_kernel,
        grid_spec=pltpu.PrefetchScalarGridSpec(
            num_scalar_prefetch=1,
            grid=(count,),
            in_specs=[
                pl.BlockSpec((rows, LANES), lambda i, s: (at(i, s), 0)),
                pl.BlockSpec((1, 1, n), lambda i, s: (at(i, s), 0, 0)),
                whole_spec(col_hot),
                whole_spec(sort),
            ],
            out_specs=pl.BlockSpec((1, col_tiles, n, n), lambda i, s: (i, 0, 0, 0)),
        ),
        out_shape=jax.ShapeDtypeStruct((count, col_tiles, n, n), BF16),
        compiler_params=pltpu.CompilerParams(vmem_limit_bytes=VMEM),
        cost_estimate=pl.CostEstimate(
            flops=count * col_tiles * 3 * 2 * n**3,
            bytes_accessed=count * col_tiles * n * n * 6,
            transcendentals=0,
        ),
        name="lift_leaf",
    )(pick, front_rows, row_places, col_hot, sort)


def climb_kernel(
    pick, x_ref, mid_ref, got_ref, row2_ref, row1_ref, col2_ref, col1_ref, sort_ref, _, out_ref
):
    col_tiles, n = out_ref.shape[1], out_ref.shape[2]
    hot2 = one_hot(row2_ref[0], n)
    hot1 = one_hot(row1_ref[0], n)
    sort = sort_ref[...]
    tiles = sort_tiles(x_ref[...].astype(BF16), sort, col_tiles)
    mids = sort_tiles_wide(mid_ref[...], sort, col_tiles)
    for c in range(col_tiles):
        half = mxu(hot2, tiles[c].astype(BF16)).astype(BF16)
        whole = mxu(half, col2_ref[c]) + got_ref[0, c].astype(F32)
        whole = (whole + mids[c]).astype(BF16)
        half = mxu(hot1, whole).astype(BF16)
        out_ref[0, c] = mxu(half, col1_ref[c]).astype(BF16)


def climb(pick, leaf_rows, mid_rows, got, tiles, row2, row1, col2, col1, sort, after):
    count, col_tiles, n, _ = got.shape
    rows = mid_rows.shape[0] // tiles

    def mid(i, s):
        return 2 * i + s[1]

    def leaf(i, s):
        return 2 * mid(i, s) + s[0]

    return pl.pallas_call(
        climb_kernel,
        grid_spec=pltpu.PrefetchScalarGridSpec(
            num_scalar_prefetch=1,
            grid=(count,),
            in_specs=[
                pl.BlockSpec((rows, LANES), lambda i, s: (leaf(i, s), 0)),
                pl.BlockSpec((rows, LANES), lambda i, s: (mid(i, s), 0)),
                pl.BlockSpec((1, col_tiles, n, n), lambda i, s: (i, 0, 0, 0)),
                pl.BlockSpec((1, 1, n), lambda i, s: (leaf(i, s), 0, 0)),
                pl.BlockSpec((1, 1, n), lambda i, s: (mid(i, s), 0, 0)),
                whole_spec(col2),
                whole_spec(col1),
                whole_spec(sort),
                pl.BlockSpec(memory_space=pl.ANY),
            ],
            out_specs=pl.BlockSpec((1, col_tiles, n, n), lambda i, s: (i, 0, 0, 0)),
        ),
        out_shape=jax.ShapeDtypeStruct((count, col_tiles, n, n), BF16),
        compiler_params=pltpu.CompilerParams(vmem_limit_bytes=VMEM),
        cost_estimate=pl.CostEstimate(
            flops=count * col_tiles * 7 * 2 * n**3,
            bytes_accessed=count * col_tiles * n * n * 12,
            transcendentals=0,
        ),
        name="climb_middle",
    )(pick, leaf_rows, mid_rows, got, row2, row1, col2, col1, sort, after)


def finish_kernel(pick, root_ref, kept_ref, got_ref, sort_ref, *refs):
    panels = len(refs) // 3
    rows_own, rows_other = refs[:panels], refs[panels : 2 * panels]
    cols = refs[2 * panels : 3 * panels]
    out_ref = refs[3 * panels]
    col_tiles = kept_ref.shape[1]

    def work(row_refs):
        sort = sort_ref[...]
        roots = sort_tiles_wide(root_ref[...], sort, col_tiles)
        done = []
        for c in range(col_tiles):
            total = roots[c] + (kept_ref[0, c].astype(F32) + got_ref[0, c].astype(F32))
            update = None
            for row_ref, col_ref in zip(row_refs, cols):
                for k in range(row_ref.shape[0]):
                    term = mxu_t(row_ref[k, 0], col_ref[k, c])
                    update = term if update is None else update + term
            done.append((total - update).astype(BF16))
        unsort_tiles(done, sort, out_ref)

    @pl.when(pl.program_id(0) == 0)
    def _():
        work(rows_own)

    @pl.when(pl.program_id(0) != 0)
    def _():
        work(rows_other)


def finish(pick, root_rows, kept, got, own, other, cols, sort):
    tiles, col_tiles, n, _ = kept.shape
    spread = tiles // col_tiles
    rows = root_rows.shape[0] // tiles

    def at(q, c, s):
        return c * spread + (s[0] ^ q)

    def row_spec(x, first):
        if first:
            index = lambda q, c, s: (0, jnp.where(q == 0, c, col_tiles - 1), 0, 0)
        else:
            index = lambda q, c, s: (0, jnp.where(q == 0, 0, c), 0, 0)
        return pl.BlockSpec((x.shape[0], 1, n, n), index)

    tile_spec = pl.BlockSpec((1, col_tiles, n, n), lambda q, c, s: (at(q, c, s), 0, 0, 0))
    lane_spec = pl.BlockSpec((rows, LANES), lambda q, c, s: (at(q, c, s), 0))
    count = sum(x.shape[0] for x in own)
    return pl.pallas_call(
        finish_kernel,
        grid_spec=pltpu.PrefetchScalarGridSpec(
            num_scalar_prefetch=1,
            grid=(spread, col_tiles),
            in_specs=[
                lane_spec,
                tile_spec,
                tile_spec,
                whole_spec(sort),
                *[row_spec(x, True) for x in own],
                *[row_spec(x, False) for x in other],
                *[whole_spec(x) for x in cols],
            ],
            out_specs=lane_spec,
        ),
        out_shape=jax.ShapeDtypeStruct(root_rows.shape, BF16),
        compiler_params=pltpu.CompilerParams(vmem_limit_bytes=VMEM),
        cost_estimate=pl.CostEstimate(
            flops=tiles * col_tiles * (count + 3) * 2 * n**3,
            bytes_accessed=tiles * col_tiles * n * n * 10,
            transcendentals=0,
        ),
        name="finish_root",
    )(pick, root_rows, kept, got, sort, *own, *other, *cols)


def strip(front, tile_row, groups, member, bits):
    piece = jnp.transpose(front[tile_row // groups], (1, 0, 2))
    if groups > 1:
        piece = jnp.where(member == tile_row % groups, piece, 0.0)
    return group_sum(piece, bits)


def solve(inverse, rows):
    return jnp.einsum("ks,csj->cjk", inverse, rows, precision=HIGHEST)


def placed(hot, panels):
    return jnp.einsum(
        "cqj,cjk->cqk", hot, panels, preferred_element_type=F32
    ).astype(BF16)


def moved(row_hot, block, col_hot):
    out = jnp.einsum("qs,csj->cqj", row_hot, block, precision=HIGHEST)
    return jnp.einsum("cqj,cpj->cqp", out, col_hot, precision=HIGHEST)


def product(rows, cols):
    return jnp.einsum("fsk,fcjk->csj", rows, cols, preferred_element_type=F32)


def hots(places, n):
    slots = jnp.arange(n, dtype=jnp.int32)
    return (places[:, None, :] == slots[None, :, None]).astype(BF16)


def places_of(scatter, order, pivot):
    tiles, n = scatter.shape
    tile_ids = jnp.arange(tiles, dtype=jnp.int32)[:, None]
    rows = tile_ids * n + jnp.arange(n, dtype=jnp.int32)[None, :]
    return jnp.where((rows < order) & (tile_ids != pivot), scatter, -1)


def panel_slices(panel_pair, sizes, members):
    n_tile = lax.axis_size("tile")
    stacked = jnp.stack(panel_pair)
    count, col_tiles, n, width = stacked.shape
    cut = stacked.reshape(count, col_tiles, n_tile, n // n_tile, width)
    cut = jnp.transpose(cut, (2, 0, 1, 3, 4))
    got = lax.all_to_all(cut, "tile", 0, 0, tiled=True)
    out = []
    for at in range(count):
        tiles = jnp.transpose(got[:, at], (1, 0, 2, 3))
        tiles = tiles.reshape(-1, sizes[at], n // n_tile, width)
        out.append(lax.dynamic_index_in_dim(tiles, members[at], 1, keepdims=True))
    return out


def per_device(
    leaf_fronts, middle_fronts, root_front, leaf_scatter, middle_scatter, leaf_orders, middle_orders
):
    n_cube, n_tile = lax.axis_size("cube"), lax.axis_size("tile")
    cube, tile = lax.axis_index("cube"), lax.axis_index("tile")
    g2, g1 = n_cube // 4, n_cube // 2
    bit2, bit1 = g2.bit_length() - 1, g1.bit_length() - 1
    f, p = cube // g2, cube // g1
    m2, m1 = cube % g2, cube % g1
    leaf_tiles, n, col_tiles, _ = leaf_fronts.shape
    mid_tiles = middle_fronts.shape[0]
    col_ids = jnp.arange(col_tiles, dtype=jnp.int32) * n_tile + tile
    spread = n_tile // n_cube

    places2 = places_of(leaf_scatter[f], leaf_orders[f], 0)
    places1 = places_of(middle_scatter[p], middle_orders[p], 1)
    cols2 = jnp.take(places2, col_ids, axis=0)
    cols1 = jnp.take(places1, col_ids, axis=0)
    hot2, hot1 = hots(cols2, n), hots(cols1, n)
    top2, top1 = hots(places2[1:3], n), hots(places1[2:3], n)
    slots = jnp.arange(n, dtype=jnp.int32)
    turned2 = (cols2[:, :, None] == slots).astype(BF16)
    turned1 = (cols1[:, :, None] == slots).astype(BF16)

    def at_tile(strips, tile_id):
        return strips[tile_id // n_tile]

    leaf0 = strip(leaf_fronts, 0, g2, m2, bit2)
    corner2, ahead_1, ahead_2 = tile_spread(at_tile(leaf0, 0))

    sort = sorter(n, col_tiles)
    rows2 = places2.reshape(-1, g2, 1, n)[:, m2]
    rows1 = places1.reshape(-1, g1, 1, n)[:, m1]
    parity2, parity1 = f % 2, p % 2
    leaf_lanes, mid_lanes, root_lanes = map(
        lane_rows, (leaf_fronts, middle_fronts, root_front)
    )
    got2 = []
    for half in (1 - parity1, parity1):
        pick = jnp.stack([1 - parity2, half])
        sent = lift(pick, leaf_lanes, leaf_tiles, rows2, turned2, sort)
        got2.append(partner(sent, bit2))

    def climbed(half, got, after):
        pick = jnp.stack([parity2, half])
        return climb(
            pick, leaf_lanes, mid_lanes, got, mid_tiles, rows2, rows1, turned2, turned1, sort, after
        )

    sent1 = climbed(1 - parity1, got2[0], sent)
    got1 = partner(sent1, bit1)

    lifted = jnp.stack(
        [
            moved(top2[r - 1].astype(F32), strip(leaf_fronts, r, g2, m2, bit2), hot2.astype(F32))
            + strip(middle_fronts, r, g1, m1, bit2)
            for r in (1, 2)
        ]
    )
    base1 = lifted + partner(lifted, bit2)
    raised = moved(top1[0].astype(F32), base1[1], hot1.astype(F32))
    raised = raised + strip(root_front, 2, n_cube, cube, bit1)
    base0 = raised + partner(raised, bit1)
    is_one = tile % n_tile == 1
    ends = jnp.stack(
        [jnp.where(is_one, at_tile(base1[0], 1), at_tile(base1[0], 2)), at_tile(base0, 2)]
    )
    _, ends1, ends2 = tile_spread(ends)

    upper2, inverse2 = cholesky(corner2, sent1)
    panel2 = solve(inverse2, leaf0).astype(BF16)
    ahead2 = solve(inverse2, jnp.stack([ahead_1, ahead_2])).astype(BF16)
    lift2 = jnp.concatenate([placed(hot2, panel2), placed(top2, ahead2)])
    pair2 = jnp.stack([lift2, partner(lift2, bit2)])

    mine2, one2, two2 = pair2[:, :col_tiles], pair2[:, col_tiles], pair2[:, col_tiles + 1]
    ends = product(one2, pair2[:, col_tiles:])
    upper1, inverse1 = cholesky(ends1[0] - ends[0], inverse2)
    front1 = base1[0] - product(one2, mine2)
    panel1 = solve(
        inverse1, jnp.concatenate([front1, (ends2[0] - ends[1])[None]])
    ).astype(BF16)

    both1 = jnp.concatenate([hot1, top1])
    climb2 = placed(both1, jnp.concatenate([lift2[:col_tiles], lift2[col_tiles + 1 :]]))
    across2 = jnp.stack([climb2, partner(climb2, bit1)])
    four2 = jnp.concatenate([across2, partner(across2, bit2)])
    climb1 = placed(both1, panel1)
    kept1 = climbed(parity1, got2[1], climb1)
    two1 = jnp.stack([climb1, partner(climb1, bit1)])
    six = jnp.concatenate([four2, two1])
    ends = product(six[:, col_tiles], six)
    upper0, inverse0 = cholesky(ends2[1] - ends[col_tiles], kept1)
    panel0 = solve(inverse0, base0 - ends[:col_tiles]).astype(BF16)
    panel0 = jnp.where((col_ids == 2)[:, None, None], jnp.zeros_like(panel0), panel0)

    cols = [four2[:, :col_tiles], two1[:, :col_tiles], panel0[None]]
    pairs = [row_spread(x) for x in cols]
    own, other = [x[0] for x in pairs], [x[1] for x in pairs]

    high = tile // n_cube
    schur = finish(high.reshape(1), root_lanes, kept1, got1, own, other, cols, sort)
    schur = schur.reshape(root_front.shape[0], n, n // LANES, col_tiles, LANES)
    schur = schur.transpose(0, 1, 3, 2, 4).reshape(root_front.shape)

    def with_corner(panel, upper, pivot):
        return jnp.where((col_ids == pivot)[:, None, None], upper.T.astype(BF16), panel)

    leaf_panel, middle_panel = panel_slices(
        (with_corner(panel2, upper2, 0), with_corner(panel1[:col_tiles], upper1, 1)),
        (g2, g1),
        (m2, m1),
    )
    part = n // n_tile
    cuts = [
        lax.dynamic_slice_in_dim(x[-1][0], tile * part, part, 1) for x in (own, other)
    ]
    ordered = [jnp.where(high == j, cuts[0], cuts[1]) for j in range(spread)]
    root_panel = jnp.stack(ordered, 1).reshape(-1, part, n)
    root_ids = jnp.arange(root_front.shape[0], dtype=jnp.int32) * n_cube + cube
    corner_cut = lax.dynamic_slice_in_dim(upper0.T.astype(BF16), tile * part, part, 0)
    root_panel = jnp.where((root_ids == 2)[:, None, None], corner_cut, root_panel)
    return leaf_panel, middle_panel, root_panel[:, None], schur


def solution(mesh):
    front = P(None, "cube", None, "tile")
    panel = P(None, "cube", "tile", None)
    return jax.shard_map(
        per_device,
        mesh=mesh,
        in_specs=(front, front, front, P(), P(), P(), P()),
        out_specs=(panel, panel, panel, front),
        check_vma=False,
    )
```

```python
import functools

import jax
import jax.numpy as jnp
from jax import lax
from jax.experimental import pallas as pl
from jax.experimental.pallas import tpu as pltpu
from jax.sharding import PartitionSpec as P

HIGHEST = lax.Precision.HIGHEST
F32 = jnp.float32
BF16 = jnp.bfloat16
LANES = 128
BLOCK = 32
WIDTH = 8
BATCH = 2
VMEM = 50 << 20


def partner(block, apart):
    count = lax.axis_size("cube")
    route = [(low, low ^ 1 << apart) for low in range(count)]
    return lax.ppermute(block, "cube", route)


def group_sum(value, bits):
    for bit in range(bits):
        value = value + partner(value, bit)
    return value


def tile_spread(value):
    count = lax.axis_size("tile")
    me = lax.axis_index("tile")
    bit, filled = count >> 1, 1
    while bit >= 4:
        route = [
            (base + t, base + t + bit)
            for base in range(0, count, 2 * bit)
            if base % (2 * bit) == 0 and base // (2 * bit) < filled
            for t in range(3)
        ]
        moved = lax.ppermute(value, "tile", route)
        value = jnp.where(me & bit != 0, moved, value)
        filled *= 2
        bit >>= 1
    other = lax.ppermute(
        value, "tile", [(t, t ^ 1) for t in range(count) if t % 4 != 3]
    )
    even = me & 1 == 0
    pair = jnp.stack([jnp.where(even, value, other), jnp.where(even, other, value)])
    across = lax.ppermute(pair, "tile", [(t, t ^ 2) for t in range(count)])
    front = me & 2 == 0
    low = jnp.where(front, pair, across)
    return low[0], low[1], jnp.where(front, across[0], pair[0])


def row_spread(value):
    n_cube, n_tile = lax.axis_size("cube"), lax.axis_size("tile")
    cube, tile = lax.axis_index("cube"), lax.axis_index("tile")
    missing = tile % n_cube ^ cube
    bits = [1 << b for b in range(n_cube.bit_length() - 2, -1, -1)]

    def moved(block, bit, done):
        route = []
        for m in range(n_cube):
            for t in range(n_tile):
                if ((t % n_cube) ^ m) & ~done == 0:
                    route.append((m * n_tile + t, m * n_tile + (t ^ bit)))
        return lax.ppermute(block, ("cube", "tile"), route)

    def step(block, bit, done):
        return jnp.where(missing & bit != 0, moved(block, bit, done), block)

    own = step(value, bits[0], 0)
    done = bits[0]
    other = across = moved(own, n_cube, done)
    for bit in bits[1:-1]:
        own, other = step(own, bit, done), step(other, bit, done)
        done |= bit
    last = bits[-1]
    return (own, moved(own, last, done)), (other, moved(other, last, done)), across


def split3(value):
    high = value.astype(BF16)
    rest = value - high.astype(F32)
    middle = rest.astype(BF16)
    low = (rest - middle.astype(F32)).astype(BF16)
    return high, middle, low


def newton_rsqrt(value):
    guess = lax.rsqrt(value)
    return guess * (1.5 - 0.5 * value * guess * guess)


def newton_reciprocal(value):
    guess = pl.reciprocal(value, approx=True)
    return guess * (2.0 - value * guess)


def cholesky_kernel(a_ref, *refs):
    upper_ref, inverse_ref, work = refs[-3:]
    n = a_ref.shape[0]
    rows = lax.broadcasted_iota(jnp.int32, (n, n), 0)
    cols = lax.broadcasted_iota(jnp.int32, (n, n), 1)
    work[:, :n] = a_ref[...]
    work[:, n:] = jnp.where(rows == cols, 1.0, 0.0)
    for start in range(0, n, BLOCK):
        stop = start + BLOCK
        low = start // LANES * LANES
        high = n + -(-stop // LANES) * LANES
        parts = [
            work[start:stop, at : at + LANES] for at in range(low, high, LANES)
        ]
        for first in range(0, BLOCK, WIDTH):
            lane = start - low + first
            wide = [
                jnp.broadcast_to(parts[0][:, lane + i : lane + i + 1], (BLOCK, LANES))
                for i in range(WIDTH)
            ]
            for i in range(0, WIDTH, 2):
                j = first + i
                c0, c1 = wide[i], wide[i + 1]
                a = c0[j : j + 1, :]
                b = c0[j + 1 : j + 2, :]
                c = c1[j + 1 : j + 2, :]
                over = newton_reciprocal(a * c - b * b)
                g0 = (c * c0 - b * c1) * over
                g1 = (a * c1 - b * c0) * over
                for later in range(i + 2, WIDTH):
                    at = first + later
                    wide[later] = (
                        wide[later] - g0 * c0[at : at + 1, :] - g1 * c1[at : at + 1, :]
                    )
                inv_a = newton_rsqrt(a)
                below = b * inv_a
                inv_c = newton_rsqrt(c - below * below)
                for at, part in enumerate(parts):
                    r0 = part[j : j + 1, :]
                    r1 = part[j + 1 : j + 2, :]
                    u0 = r0 * inv_a
                    u1 = (r1 - below * u0) * inv_c
                    lanes = slice(low + at * LANES, low + (at + 1) * LANES)
                    work[start + j : start + j + 1, lanes] = u0
                    work[start + j + 1 : start + j + 2, lanes] = u1
                    parts[at] = part - g0 * r0 - g1 * r1
        if stop < n:
            block = work[start:stop, low:high]
            h, m, l = split3(block)
            right = jnp.concatenate([h, m, h, l, m, h], axis=0)
            keep = stop // LANES * LANES
            hl, ml, ll = (x[:, keep - low : n - low] for x in (h, m, l))
            left = jnp.concatenate([hl, hl, ml, hl, ml, ll], axis=0)
            update = lax.dot_general(
                left, right, (((0,), (0,)), ((), ())), preferred_element_type=F32
            )
            work[stop:, low:high] -= update[stop - keep :]
    upper_ref[...] = jnp.where(rows <= cols, work[:, :n], 0.0)
    inverse_ref[...] = jnp.where(rows >= cols, work[:, n:], 0.0)


def cholesky(corner, *after):
    n = corner.shape[0]
    shape = jax.ShapeDtypeStruct((n, n), F32)
    return pl.pallas_call(
        cholesky_kernel,
        out_shape=(shape, shape),
        in_specs=[
            pl.BlockSpec(memory_space=pltpu.VMEM),
            *[pl.BlockSpec(memory_space=pl.ANY) for _ in after],
        ],
        scratch_shapes=[pltpu.VMEM((n, 2 * n), F32)],
        compiler_params=pltpu.CompilerParams(vmem_limit_bytes=VMEM),
        cost_estimate=pl.CostEstimate(
            flops=20_000_000, bytes_accessed=12 * n * n, transcendentals=0
        ),
        name="cholesky_and_inverse",
    )(corner, *after)


def lane_rows(front):
    tiles, n, col_tiles, _ = front.shape
    halves = n // LANES
    split = front.reshape(tiles, n, col_tiles, halves, LANES)
    return split.transpose(0, 1, 3, 2, 4).reshape(-1, LANES)


def tile_of(ref, at, col_tiles, n, base=0):
    halves = n // LANES
    step = col_tiles * halves
    return jnp.concatenate(
        [
            ref[pl.ds(base + h * col_tiles + at, n, stride=step), :]
            for h in range(halves)
        ],
        axis=1,
    )


def one_hot(places, n):
    slots = lax.broadcasted_iota(jnp.int32, (n, n), 0)
    return jnp.where(slots == places, 1.0, 0.0).astype(BF16)


def mxu(left, right):
    return jnp.dot(left, right, preferred_element_type=F32)


def mxu_t(left, right):
    return lax.dot_general(
        left, right, (((1,), (1,)), ((), ())), preferred_element_type=F32
    )


def lift_kernel(pick, *refs):
    batch = (len(refs) - 2) // 2
    x_refs, row_refs = refs[:batch], refs[batch : 2 * batch]
    col_ref, out_ref = refs[2 * batch :]
    col_tiles, n = out_ref.shape[1], out_ref.shape[2]
    for b in range(batch):
        row_hot = one_hot(row_refs[b][0], n)
        for c in range(col_tiles):
            tile = tile_of(x_refs[b], c, col_tiles, n).astype(BF16)
            half = mxu(row_hot, tile).astype(BF16)
            out_ref[b, c] = mxu(half, col_ref[c]).astype(BF16)


def whole_spec(x):
    return pl.BlockSpec(x.shape, lambda *_: (0,) * x.ndim)


def lane_spec(rows, index):
    return pl.BlockSpec((rows, LANES), lambda i, s: (index(i, s), 0))


def place_spec(n, index):
    return pl.BlockSpec((1, 1, n), lambda i, s: (index(i, s), 0, 0))


def lift(pick, front_rows, tiles, row_places, col_hot):
    col_tiles, n, _ = col_hot.shape
    rows = front_rows.shape[0] // tiles
    count = tiles // 4

    def leaf(b):
        return lambda i, s: 2 * (2 * (BATCH * i + b) + s[1]) + s[0]

    return pl.pallas_call(
        lift_kernel,
        grid_spec=pltpu.PrefetchScalarGridSpec(
            num_scalar_prefetch=1,
            grid=(count // BATCH,),
            in_specs=[
                *[lane_spec(rows, leaf(b)) for b in range(BATCH)],
                *[place_spec(n, leaf(b)) for b in range(BATCH)],
                whole_spec(col_hot),
            ],
            out_specs=pl.BlockSpec((BATCH, col_tiles, n, n), lambda i, s: (i, 0, 0, 0)),
        ),
        out_shape=jax.ShapeDtypeStruct((count, col_tiles, n, n), BF16),
        compiler_params=pltpu.CompilerParams(vmem_limit_bytes=VMEM),
        cost_estimate=pl.CostEstimate(
            flops=count * col_tiles * 4 * 2 * n**3,
            bytes_accessed=count * col_tiles * n * n * 6,
            transcendentals=0,
        ),
        name="lift_leaf",
    )(pick, *[front_rows] * BATCH, *[row_places] * BATCH, col_hot)


def climb_kernel(pick, *refs):
    batch = BATCH
    x_refs, mid_refs, row2_refs, row1_refs = (
        refs[k * batch : (k + 1) * batch] for k in range(4)
    )
    got_ref, col2_ref, col1_ref = refs[4 * batch : 4 * batch + 3]
    out_ref = refs[-1]
    col_tiles, n = out_ref.shape[1], out_ref.shape[2]
    for b in range(batch):
        hot2 = one_hot(row2_refs[b][0], n)
        hot1 = one_hot(row1_refs[b][0], n)
        for c in range(col_tiles):
            tile = tile_of(x_refs[b], c, col_tiles, n).astype(BF16)
            half = mxu(hot2, tile).astype(BF16)
            whole = mxu(half, col2_ref[c]) + got_ref[b, c].astype(F32)
            whole = (whole + tile_of(mid_refs[b], c, col_tiles, n)).astype(BF16)
            half = mxu(hot1, whole).astype(BF16)
            out_ref[b, c] = mxu(half, col1_ref[c]).astype(BF16)


def climb(pick, first, count, leaf_rows, mid_rows, got, tiles, row2, row1, col2, col1, *after):
    _, col_tiles, n, _ = got.shape
    rows = mid_rows.shape[0] // tiles

    def mid(b):
        return lambda i, s: 2 * (first + BATCH * i + b) + s[1]

    def leaf(b):
        return lambda i, s: 2 * mid(b)(i, s) + s[0]

    batch = range(BATCH)
    return pl.pallas_call(
        climb_kernel,
        grid_spec=pltpu.PrefetchScalarGridSpec(
            num_scalar_prefetch=1,
            grid=(count // BATCH,),
            in_specs=[
                *[lane_spec(rows, leaf(b)) for b in batch],
                *[lane_spec(rows, mid(b)) for b in batch],
                *[place_spec(n, leaf(b)) for b in batch],
                *[place_spec(n, mid(b)) for b in batch],
                pl.BlockSpec(
                    (BATCH, col_tiles, n, n), lambda i, s: (first // BATCH + i, 0, 0, 0)
                ),
                whole_spec(col2),
                whole_spec(col1),
                *[pl.BlockSpec(memory_space=pl.ANY) for _ in after],
            ],
            out_specs=pl.BlockSpec((BATCH, col_tiles, n, n), lambda i, s: (i, 0, 0, 0)),
        ),
        out_shape=jax.ShapeDtypeStruct((count, col_tiles, n, n), BF16),
        compiler_params=pltpu.CompilerParams(vmem_limit_bytes=VMEM),
        cost_estimate=pl.CostEstimate(
            flops=count * col_tiles * 8 * 2 * n**3,
            bytes_accessed=count * col_tiles * n * n * 12,
            transcendentals=0,
        ),
        name="climb_middle",
    )(
        pick,
        *[leaf_rows] * BATCH,
        *[mid_rows] * BATCH,
        *[row2] * BATCH,
        *[row1] * BATCH,
        got,
        col2,
        col1,
        *after,
    )


def finish_kernel(levels, pieces, spread, pick, root_ref, kept_ref, *refs):
    sources = refs[: 4 * levels]
    got_refs = refs[4 * levels : 4 * levels + pieces]
    cols = refs[4 * levels + pieces : 5 * levels + pieces]
    out_ref = refs[5 * levels + pieces]
    scratch, *buffers = refs[5 * levels + pieces + 1 :]
    row_bufs, got_buf = buffers[: 2 * levels], buffers[2 * levels]
    row_sem, got_sem = buffers[2 * levels + 1 :]
    step = pl.program_id(0)
    col_tiles, n = kept_ref.shape[1], kept_ref.shape[2]
    halves = n // LANES
    rows = n * col_tiles * halves
    per_piece = col_tiles * spread // pieces

    def row_copy(k, moved, c):
        source = sources[4 * (k // 2) + 2 * (k % 2) + moved]
        return pltpu.make_async_copy(
            source.at[:, c], row_bufs[k].at[:, c], row_sem.at[k, c]
        )

    def got_copy(q):
        return pltpu.make_async_copy(
            got_refs[q], got_buf.at[pl.ds(q * per_piece, per_piece)], got_sem.at[q]
        )

    @pl.when(step == 0)
    def _():
        for q in range(pieces):
            got_copy(q).start()

        @pl.when(pick[1] == 0)
        def _():
            for c in range(col_tiles):
                for k in range(2 * levels):
                    row_copy(k, 0, c).start()

        @pl.when(pick[1] != 0)
        def _():
            for c in range(col_tiles):
                for k in range(2 * levels):
                    row_copy(k, 1, c).start()

        for q in range(pieces):
            got_copy(q).wait()

    for k in range(2 * levels):
        row_copy(k, 0, step).wait()

    for which in range(spread):
        j = pick[0] ^ which
        for c in range(col_tiles):
            total = tile_of(
                root_ref, c, col_tiles, n, pl.multiple_of(j * rows, rows)
            )
            got = got_buf[step * spread + j, c]
            total += kept_ref[j, c].astype(F32) + got.astype(F32)
            update = None
            for level in range(levels):
                row_buf = row_bufs[2 * level + which]
                for k in range(row_buf.shape[0]):
                    term = mxu_t(row_buf[k, step], cols[level][k, c])
                    update = term if update is None else update + term
            total -= update
            for h in range(halves):
                scratch[
                    which, pl.ds(h * col_tiles + c, n, stride=col_tiles * halves), :
                ] = total[:, h * LANES : (h + 1) * LANES]
        out_ref[pl.ds(pl.multiple_of(j * rows, rows), rows), :] = scratch[which].astype(BF16)


def finish(pick, root_rows, kept, got, rows, cols):
    tiles, col_tiles, n, _ = kept.shape
    spread = tiles // col_tiles
    lane_rows = root_rows.shape[0] // col_tiles
    lanes = pl.BlockSpec((lane_rows, LANES), lambda c, s: (c, 0))
    anywhere = pl.BlockSpec(memory_space=pl.ANY)
    flat = [x for level in rows for pair in level for x in pair]
    count = sum(x.shape[0] for x in cols)
    return pl.pallas_call(
        functools.partial(finish_kernel, len(rows), len(got), spread),
        grid_spec=pltpu.PrefetchScalarGridSpec(
            num_scalar_prefetch=1,
            grid=(col_tiles,),
            in_specs=[
                lanes,
                pl.BlockSpec((spread, col_tiles, n, n), lambda c, s: (c, 0, 0, 0)),
                *[anywhere for _ in flat],
                *[anywhere for _ in got],
                *[whole_spec(x) for x in cols],
            ],
            out_specs=lanes,
            scratch_shapes=[
                pltpu.VMEM((spread, lane_rows // spread, LANES), F32),
                *[pltpu.VMEM(x.shape, BF16) for x in cols for _ in range(2)],
                pltpu.VMEM(kept.shape, BF16),
                pltpu.SemaphoreType.DMA((2 * len(rows), col_tiles)),
                pltpu.SemaphoreType.DMA((len(got),)),
            ],
        ),
        out_shape=jax.ShapeDtypeStruct(root_rows.shape, BF16),
        compiler_params=pltpu.CompilerParams(vmem_limit_bytes=VMEM),
        cost_estimate=pl.CostEstimate(
            flops=tiles * col_tiles * (count + 3) * 2 * n**3,
            bytes_accessed=tiles * col_tiles * n * n * 10,
            transcendentals=0,
        ),
        name="finish_root",
    )(pick, root_rows, kept, *flat, *got, *cols)


def strip(front, tile_row, groups, member, bits):
    piece = jnp.transpose(front[tile_row // groups], (1, 0, 2))
    if groups > 1:
        piece = jnp.where(member == tile_row % groups, piece, 0.0)
    return group_sum(piece, bits)


def solve(inverse, rows):
    return jnp.einsum("ks,csj->cjk", inverse, rows, precision=HIGHEST)


def placed(hot, panels):
    return jnp.einsum(
        "cqj,cjk->cqk", hot, panels, preferred_element_type=F32
    ).astype(BF16)


def moved(row_hot, block, col_hot):
    out = jnp.einsum("qs,csj->cqj", row_hot, block, precision=HIGHEST)
    return jnp.einsum("cqj,cpj->cqp", out, col_hot, precision=HIGHEST)


def product(rows, cols):
    return jnp.einsum("fsk,fcjk->csj", rows, cols, preferred_element_type=F32)


def hots(places, n):
    slots = jnp.arange(n, dtype=jnp.int32)
    return (places[:, None, :] == slots[None, :, None]).astype(BF16)


def places_of(scatter, order, pivot):
    tiles, n = scatter.shape
    tile_ids = jnp.arange(tiles, dtype=jnp.int32)[:, None]
    rows = tile_ids * n + jnp.arange(n, dtype=jnp.int32)[None, :]
    return jnp.where((rows < order) & (tile_ids != pivot), scatter, -1)


def panel_slices(panel_pair, sizes, members):
    n_tile = lax.axis_size("tile")
    stacked = jnp.stack(panel_pair)
    count, col_tiles, n, width = stacked.shape
    cut = stacked.reshape(count, col_tiles, n_tile, n // n_tile, width)
    cut = jnp.transpose(cut, (2, 0, 1, 3, 4))
    got = lax.all_to_all(cut, "tile", 0, 0, tiled=True)
    out = []
    for at in range(count):
        tiles = jnp.transpose(got[:, at], (1, 0, 2, 3))
        tiles = tiles.reshape(-1, sizes[at], n // n_tile, width)
        out.append(lax.dynamic_index_in_dim(tiles, members[at], 1, keepdims=True))
    return out


def per_device(
    leaf_fronts, middle_fronts, root_front, leaf_scatter, middle_scatter, leaf_orders, middle_orders
):
    n_cube, n_tile = lax.axis_size("cube"), lax.axis_size("tile")
    cube, tile = lax.axis_index("cube"), lax.axis_index("tile")
    g2, g1 = n_cube // 4, n_cube // 2
    bit2, bit1 = g2.bit_length() - 1, g1.bit_length() - 1
    f, p = cube // g2, cube // g1
    m2, m1 = cube % g2, cube % g1
    leaf_tiles, n, col_tiles, _ = leaf_fronts.shape
    mid_tiles = middle_fronts.shape[0]
    col_ids = jnp.arange(col_tiles, dtype=jnp.int32) * n_tile + tile
    spread = n_tile // n_cube

    places2 = places_of(leaf_scatter[f], leaf_orders[f], 0)
    places1 = places_of(middle_scatter[p], middle_orders[p], 1)
    cols2 = jnp.take(places2, col_ids, axis=0)
    cols1 = jnp.take(places1, col_ids, axis=0)
    hot2, hot1 = hots(cols2, n), hots(cols1, n)
    top2, top1 = hots(places2[1:3], n), hots(places1[2:3], n)
    slots = jnp.arange(n, dtype=jnp.int32)
    turned2 = (cols2[:, :, None] == slots).astype(BF16)
    turned1 = (cols1[:, :, None] == slots).astype(BF16)

    def at_tile(strips, tile_id):
        return strips[tile_id // n_tile]

    leaf0 = strip(leaf_fronts, 0, g2, m2, bit2)
    corner2, ahead_1, ahead_2 = tile_spread(at_tile(leaf0, 0))

    rows2 = places2.reshape(-1, g2, 1, n)[:, m2]
    rows1 = places1.reshape(-1, g1, 1, n)[:, m1]
    parity2, parity1 = f % 2, p % 2
    leaf_lanes, mid_lanes, root_lanes = map(
        lane_rows, (leaf_fronts, middle_fronts, root_front)
    )
    got2 = []
    for half in (1 - parity1, parity1):
        pick = jnp.stack([1 - parity2, half])
        sent = lift(pick, leaf_lanes, leaf_tiles, rows2, turned2)
        got2.append(partner(sent, bit2))

    def climbed(half, first, count, got, *after):
        pick = jnp.stack([parity2, half])
        return climb(
            pick, first, count, leaf_lanes, mid_lanes, got, mid_tiles, rows2, rows1, turned2, turned1, *after
        )

    pieces = [strip(leaf_fronts, r, g2, m2, bit2) for r in (1, 2)]
    pieces, _ = lax.optimization_barrier((pieces, sent[0, 0, :8, :LANES]))
    lifted = jnp.stack(
        [
            moved(top2[r - 1].astype(F32), pieces[r - 1], hot2.astype(F32))
            + strip(middle_fronts, r, g1, m1, bit2)
            for r in (1, 2)
        ]
    )
    base1 = lifted + partner(lifted, bit2)
    raised = moved(top1[0].astype(F32), base1[1], hot1.astype(F32))
    raised = raised + strip(root_front, 2, n_cube, cube, bit1)
    base0 = raised + partner(raised, bit1)
    is_one = tile % n_tile == 1
    ends = jnp.stack(
        [jnp.where(is_one, at_tile(base1[0], 1), at_tile(base1[0], 2)), at_tile(base0, 2)]
    )
    _, ends1, ends2 = tile_spread(ends)

    upper2, inverse2 = cholesky(corner2, sent)
    panel2 = solve(inverse2, leaf0).astype(BF16)
    ahead2 = solve(inverse2, jnp.stack([ahead_1, ahead_2])).astype(BF16)
    lift2 = jnp.concatenate([placed(hot2, panel2), placed(top2, ahead2)])
    pair2 = jnp.stack([lift2, partner(lift2, bit2)])
    count = mid_tiles // 2
    part = max(count // 2, BATCH)
    sent1, got1 = [], []
    for first in range(0, count, part):
        before = sent1[-1] if sent1 else lift2
        sent1.append(climbed(1 - parity1, first, part, got2[0], before))
        got1.append(partner(sent1[-1], bit1))

    mine2, one2, two2 = pair2[:, :col_tiles], pair2[:, col_tiles], pair2[:, col_tiles + 1]
    ends = product(one2, pair2[:, col_tiles:])
    upper1, inverse1 = cholesky(ends1[0] - ends[0], sent1[-1])
    front1 = base1[0] - product(one2, mine2)
    panel1 = solve(
        inverse1, jnp.concatenate([front1, (ends2[0] - ends[1])[None]])
    ).astype(BF16)

    both1 = jnp.concatenate([hot1, top1])
    climb2 = placed(both1, jnp.concatenate([lift2[:col_tiles], lift2[col_tiles + 1 :]]))
    across2 = jnp.stack([climb2, partner(climb2, bit1)])
    four2 = jnp.concatenate([across2, partner(across2, bit2)])
    climb1 = placed(both1, panel1)
    kept1 = climbed(parity1, 0, count, got2[1], climb1)
    spread2 = row_spread(four2[:, :col_tiles])
    two1 = jnp.stack([climb1, partner(climb1, bit1)])
    six = jnp.concatenate([four2, two1])
    ends = product(six[:, col_tiles], six)
    upper0, inverse0 = cholesky(
        ends2[1] - ends[col_tiles], kept1, got1[0], spread2[2]
    )
    panel0 = solve(inverse0, base0 - ends[:col_tiles]).astype(BF16)
    panel0 = jnp.where((col_ids == 2)[:, None, None], jnp.zeros_like(panel0), panel0)

    cols = [four2[:, :col_tiles], two1[:, :col_tiles], panel0[None]]
    spreads = [spread2, row_spread(cols[1]), row_spread(cols[2])]
    rows = [x[:2] for x in spreads]

    high = tile // n_cube
    last_moved = (tile ^ cube) & 1
    picks = jnp.stack([high, last_moved])
    schur = finish(picks, root_lanes, kept1, got1, rows, cols)
    schur = schur.reshape(root_front.shape[0], n, n // LANES, col_tiles, LANES)
    schur = schur.transpose(0, 1, 3, 2, 4).reshape(root_front.shape)

    def with_corner(panel, upper, pivot):
        return jnp.where((col_ids == pivot)[:, None, None], upper.T.astype(BF16), panel)

    leaf_panel, middle_panel = panel_slices(
        (with_corner(panel2, upper2, 0), with_corner(panel1[:col_tiles], upper1, 1)),
        (g2, g1),
        (m2, m1),
    )
    part = n // n_tile
    cuts = [
        jnp.where(
            last_moved != 0,
            lax.dynamic_slice_in_dim(came[0], tile * part, part, 1),
            lax.dynamic_slice_in_dim(stayed[0], tile * part, part, 1),
        )
        for stayed, came in rows[-1]
    ]
    ordered = [jnp.where(high == j, cuts[0], cuts[1]) for j in range(spread)]
    root_panel = jnp.stack(ordered, 1).reshape(-1, part, n)
    root_ids = jnp.arange(root_front.shape[0], dtype=jnp.int32) * n_cube + cube
    corner_cut = lax.dynamic_slice_in_dim(upper0.T.astype(BF16), tile * part, part, 0)
    root_panel = jnp.where((root_ids == 2)[:, None, None], corner_cut, root_panel)
    return leaf_panel, middle_panel, root_panel[:, None], schur


def solution(mesh):
    front = P(None, "cube", None, "tile")
    panel = P(None, "cube", "tile", None)
    return jax.shard_map(
        per_device,
        mesh=mesh,
        in_specs=(front, front, front, P(), P(), P(), P()),
        out_specs=(panel, panel, panel, front),
        check_vma=False,
    )
```

```python
import functools

import jax
import jax.numpy as jnp
from jax import lax
from jax.experimental import pallas as pl
from jax.experimental.pallas import tpu as pltpu
from jax.sharding import PartitionSpec as P

HIGHEST = lax.Precision.HIGHEST
F32 = jnp.float32
BF16 = jnp.bfloat16
LANES = 128
BLOCK = 32
WIDTH = 8
BATCH = 2
VMEM = 50 << 20


def partner(block, apart):
    count = lax.axis_size("cube")
    route = [(low, low ^ 1 << apart) for low in range(count)]
    return lax.ppermute(block, "cube", route)


def group_sum(value, bits):
    for bit in range(bits):
        value = value + partner(value, bit)
    return value


def tile_spread(value):
    stages = []
    count = lax.axis_size("tile")
    me = lax.axis_index("tile")
    bit, filled = count >> 1, 1
    while bit >= 4:
        route = [
            (base + t, base + t + bit)
            for base in range(0, count, 2 * bit)
            if base % (2 * bit) == 0 and base // (2 * bit) < filled
            for t in range(3)
        ]
        moved = lax.ppermute(value, "tile", route)
        value = jnp.where(me & bit != 0, moved, value)
        stages.append(value)
        filled *= 2
        bit >>= 1
    other = lax.ppermute(
        value, "tile", [(t, t ^ 1) for t in range(count) if t % 4 != 3]
    )
    even = me & 1 == 0
    pair = jnp.stack([jnp.where(even, value, other), jnp.where(even, other, value)])
    stages.append(pair)
    across = lax.ppermute(pair, "tile", [(t, t ^ 2) for t in range(count)])
    front = me & 2 == 0
    low = jnp.where(front, pair, across)
    return (low[0], low[1], jnp.where(front, across[0], pair[0])), stages


def gate(value, *after):
    for x in after:
        token = x[(0,) * x.ndim]
        value = jnp.where(token == token, value, jnp.zeros_like(value))
    return value


def row_spread(value, *after):
    n_cube, n_tile = lax.axis_size("cube"), lax.axis_size("tile")
    cube, tile = lax.axis_index("cube"), lax.axis_index("tile")
    missing = tile % n_cube ^ cube
    bits = [1 << b for b in range(n_cube.bit_length() - 2, -1, -1)]

    def moved(block, bit, done):
        route = []
        for m in range(n_cube):
            for t in range(n_tile):
                if ((t % n_cube) ^ m) & ~done == 0:
                    route.append((m * n_tile + t, m * n_tile + (t ^ bit)))
        return lax.ppermute(block, ("cube", "tile"), route)

    def step(block, bit, done):
        return jnp.where(missing & bit != 0, moved(block, bit, done), block)

    own = step(value, bits[0], 0)
    done = bits[0]
    if after:
        own = gate(own, *after)
    other = across = moved(own, n_cube, done)
    for bit in bits[1:-1]:
        own, other = step(own, bit, done), step(other, bit, done)
        done |= bit
    last = bits[-1]
    return (own, moved(own, last, done)), (other, moved(other, last, done)), across


def split3(value):
    high = value.astype(BF16)
    rest = value - high.astype(F32)
    middle = rest.astype(BF16)
    low = (rest - middle.astype(F32)).astype(BF16)
    return high, middle, low


def newton_rsqrt(value):
    guess = lax.rsqrt(value)
    return guess * (1.5 - 0.5 * value * guess * guess)


def newton_reciprocal(value):
    guess = pl.reciprocal(value, approx=True)
    return guess * (2.0 - value * guess)


def cholesky_kernel(a_ref, *refs):
    upper_ref, inverse_ref, work = refs[-3:]
    n = a_ref.shape[0]
    rows = lax.broadcasted_iota(jnp.int32, (n, n), 0)
    cols = lax.broadcasted_iota(jnp.int32, (n, n), 1)
    work[:, :n] = a_ref[...]
    work[:, n:] = jnp.where(rows == cols, 1.0, 0.0)
    for start in range(0, n, BLOCK):
        stop = start + BLOCK
        low = start // LANES * LANES
        high = n + -(-stop // LANES) * LANES
        parts = [
            work[start:stop, at : at + LANES] for at in range(low, high, LANES)
        ]
        for first in range(0, BLOCK, WIDTH):
            lane = start - low + first
            wide = [
                jnp.broadcast_to(parts[0][:, lane + i : lane + i + 1], (BLOCK, LANES))
                for i in range(WIDTH)
            ]
            for i in range(0, WIDTH, 2):
                j = first + i
                c0, c1 = wide[i], wide[i + 1]
                a = c0[j : j + 1, :]
                b = c0[j + 1 : j + 2, :]
                c = c1[j + 1 : j + 2, :]
                over = newton_reciprocal(a * c - b * b)
                g0 = (c * c0 - b * c1) * over
                g1 = (a * c1 - b * c0) * over
                for later in range(i + 2, WIDTH):
                    at = first + later
                    wide[later] = (
                        wide[later] - g0 * c0[at : at + 1, :] - g1 * c1[at : at + 1, :]
                    )
                inv_a = newton_rsqrt(a)
                below = b * inv_a
                inv_c = newton_rsqrt(c - below * below)
                for at, part in enumerate(parts):
                    r0 = part[j : j + 1, :]
                    r1 = part[j + 1 : j + 2, :]
                    u0 = r0 * inv_a
                    u1 = (r1 - below * u0) * inv_c
                    lanes = slice(low + at * LANES, low + (at + 1) * LANES)
                    work[start + j : start + j + 1, lanes] = u0
                    work[start + j + 1 : start + j + 2, lanes] = u1
                    parts[at] = part - g0 * r0 - g1 * r1
        if stop < n:
            block = work[start:stop, low:high]
            h, m, l = split3(block)
            right = jnp.concatenate([h, m, h, l, m, h], axis=0)
            keep = stop // LANES * LANES
            hl, ml, ll = (x[:, keep - low : n - low] for x in (h, m, l))
            left = jnp.concatenate([hl, hl, ml, hl, ml, ll], axis=0)
            update = lax.dot_general(
                left, right, (((0,), (0,)), ((), ())), preferred_element_type=F32
            )
            work[stop:, low:high] -= update[stop - keep :]
    upper_ref[...] = jnp.where(rows <= cols, work[:, :n], 0.0)
    inverse_ref[...] = jnp.where(rows >= cols, work[:, n:], 0.0)


def cholesky(corner, *after):
    n = corner.shape[0]
    shape = jax.ShapeDtypeStruct((n, n), F32)
    return pl.pallas_call(
        cholesky_kernel,
        out_shape=(shape, shape),
        in_specs=[
            pl.BlockSpec(memory_space=pltpu.VMEM),
            *[pl.BlockSpec(memory_space=pl.ANY) for _ in after],
        ],
        scratch_shapes=[pltpu.VMEM((n, 2 * n), F32)],
        compiler_params=pltpu.CompilerParams(vmem_limit_bytes=VMEM),
        cost_estimate=pl.CostEstimate(
            flops=20_000_000, bytes_accessed=12 * n * n, transcendentals=0
        ),
        name="cholesky_and_inverse",
    )(corner, *after)


def lane_rows(front):
    tiles, n, col_tiles, _ = front.shape
    halves = n // LANES
    split = front.reshape(tiles, n, col_tiles, halves, LANES)
    return split.transpose(0, 1, 3, 2, 4).reshape(-1, LANES)


def tile_of(ref, at, col_tiles, n, base=0):
    halves = n // LANES
    step = col_tiles * halves
    return jnp.concatenate(
        [
            ref[pl.ds(base + h * col_tiles + at, n, stride=step), :]
            for h in range(halves)
        ],
        axis=1,
    )


def one_hot(places, n):
    slots = lax.broadcasted_iota(jnp.int32, (n, n), 0)
    return jnp.where(slots == places, 1.0, 0.0).astype(BF16)


def mxu(left, right):
    return jnp.dot(left, right, preferred_element_type=F32)


def mxu_t(left, right):
    return lax.dot_general(
        left, right, (((1,), (1,)), ((), ())), preferred_element_type=F32
    )


def lift_kernel(pick, *refs):
    x_refs, row_refs = refs[:BATCH], refs[BATCH : 2 * BATCH]
    col_ref, out_ref = refs[2 * BATCH], refs[-1]
    col_tiles, n = out_ref.shape[1], out_ref.shape[2]
    for b in range(BATCH):
        row_hot = one_hot(row_refs[b][0], n)
        for c in range(col_tiles):
            tile = tile_of(x_refs[b], c, col_tiles, n).astype(BF16)
            half = mxu(row_hot, tile).astype(BF16)
            out_ref[b, c] = mxu(half, col_ref[c]).astype(BF16)


def whole_spec(x):
    return pl.BlockSpec(x.shape, lambda *_: (0,) * x.ndim)


def lane_spec(rows, index):
    return pl.BlockSpec((rows, LANES), lambda i, s: (index(i, s), 0))


def place_spec(n, index):
    return pl.BlockSpec((1, 1, n), lambda i, s: (index(i, s), 0, 0))


def lift(pick, front_rows, tiles, row_places, col_hot, *after):
    col_tiles, n, _ = col_hot.shape
    rows = front_rows.shape[0] // tiles
    count = tiles // 4

    def leaf(b):
        return lambda i, s: 2 * (2 * (BATCH * i + b) + s[1]) + s[0]

    return pl.pallas_call(
        lift_kernel,
        grid_spec=pltpu.PrefetchScalarGridSpec(
            num_scalar_prefetch=1,
            grid=(count // BATCH,),
            in_specs=[
                *[lane_spec(rows, leaf(b)) for b in range(BATCH)],
                *[place_spec(n, leaf(b)) for b in range(BATCH)],
                whole_spec(col_hot),
                *[pl.BlockSpec(memory_space=pl.ANY) for _ in after],
            ],
            out_specs=pl.BlockSpec((BATCH, col_tiles, n, n), lambda i, s: (i, 0, 0, 0)),
        ),
        out_shape=jax.ShapeDtypeStruct((count, col_tiles, n, n), BF16),
        compiler_params=pltpu.CompilerParams(vmem_limit_bytes=VMEM),
        cost_estimate=pl.CostEstimate(
            flops=count * col_tiles * 4 * 2 * n**3,
            bytes_accessed=count * col_tiles * n * n * 6,
            transcendentals=0,
        ),
        name="lift_leaf",
    )(pick, *[front_rows] * BATCH, *[row_places] * BATCH, col_hot, *after)


def climb_kernel(pick, *refs):
    batch = BATCH
    x_refs, mid_refs, row2_refs, row1_refs = (
        refs[k * batch : (k + 1) * batch] for k in range(4)
    )
    got_ref, col2_ref, col1_ref = refs[4 * batch : 4 * batch + 3]
    out_ref = refs[-1]
    col_tiles, n = out_ref.shape[1], out_ref.shape[2]
    for b in range(batch):
        hot2 = one_hot(row2_refs[b][0], n)
        hot1 = one_hot(row1_refs[b][0], n)
        for c in range(col_tiles):
            tile = tile_of(x_refs[b], c, col_tiles, n).astype(BF16)
            half = mxu(hot2, tile).astype(BF16)
            whole = mxu(half, col2_ref[c]) + got_ref[b, c].astype(F32)
            whole = (whole + tile_of(mid_refs[b], c, col_tiles, n)).astype(BF16)
            half = mxu(hot1, whole).astype(BF16)
            out_ref[b, c] = mxu(half, col1_ref[c]).astype(BF16)


def climb(pick, first, count, leaf_rows, mid_rows, got, tiles, row2, row1, col2, col1, *after):
    _, col_tiles, n, _ = got.shape
    rows = mid_rows.shape[0] // tiles

    def mid(b):
        return lambda i, s: 2 * (first + BATCH * i + b) + s[1]

    def leaf(b):
        return lambda i, s: 2 * mid(b)(i, s) + s[0]

    batch = range(BATCH)
    return pl.pallas_call(
        climb_kernel,
        grid_spec=pltpu.PrefetchScalarGridSpec(
            num_scalar_prefetch=1,
            grid=(count // BATCH,),
            in_specs=[
                *[lane_spec(rows, leaf(b)) for b in batch],
                *[lane_spec(rows, mid(b)) for b in batch],
                *[place_spec(n, leaf(b)) for b in batch],
                *[place_spec(n, mid(b)) for b in batch],
                pl.BlockSpec(
                    (BATCH, col_tiles, n, n), lambda i, s: (first // BATCH + i, 0, 0, 0)
                ),
                whole_spec(col2),
                whole_spec(col1),
                *[pl.BlockSpec(memory_space=pl.ANY) for _ in after],
            ],
            out_specs=pl.BlockSpec((BATCH, col_tiles, n, n), lambda i, s: (i, 0, 0, 0)),
        ),
        out_shape=jax.ShapeDtypeStruct((count, col_tiles, n, n), BF16),
        compiler_params=pltpu.CompilerParams(vmem_limit_bytes=VMEM),
        cost_estimate=pl.CostEstimate(
            flops=count * col_tiles * 8 * 2 * n**3,
            bytes_accessed=count * col_tiles * n * n * 12,
            transcendentals=0,
        ),
        name="climb_middle",
    )(
        pick,
        *[leaf_rows] * BATCH,
        *[mid_rows] * BATCH,
        *[row2] * BATCH,
        *[row1] * BATCH,
        got,
        col2,
        col1,
        *after,
    )


def finish_kernel(levels, parts, pick, root_ref, *refs):
    sources = refs[: 4 * levels]
    ends = 4 * levels + sum(parts)
    part_refs = refs[4 * levels : ends]
    cols = refs[ends : ends + levels]
    out_ref = refs[ends + levels]
    scratch, *buffers = refs[ends + levels + 1 :]
    row_bufs, part_bufs = buffers[: 2 * levels], buffers[2 * levels : -2]
    row_sem, part_sem = buffers[-2:]
    step = pl.program_id(0)
    tiles, col_tiles, n, _ = part_bufs[0].shape
    halves = n // LANES
    rows = n * col_tiles * halves
    spread = tiles // col_tiles

    def row_copy(k, moved, c):
        source = sources[4 * (k // 2) + 2 * (k % 2) + moved]
        return pltpu.make_async_copy(
            source.at[:, c], row_bufs[k].at[:, c], row_sem.at[k, c]
        )

    part_copies = []
    for which, count in enumerate(parts):
        size = tiles // count
        for q in range(count):
            at = len(part_copies)
            target = part_bufs[which].at[pl.ds(q * size, size)]
            part_copies.append(
                pltpu.make_async_copy(part_refs[at], target, part_sem.at[at])
            )

    @pl.when(step == 0)
    def _():
        for copy in part_copies:
            copy.start()

        @pl.when(pick[1] == 0)
        def _():
            for c in range(col_tiles):
                for k in range(2 * levels):
                    row_copy(k, 0, c).start()

        @pl.when(pick[1] != 0)
        def _():
            for c in range(col_tiles):
                for k in range(2 * levels):
                    row_copy(k, 1, c).start()

        for copy in part_copies:
            copy.wait()

    for k in range(2 * levels):
        row_copy(k, 0, step).wait()

    for which in range(spread):
        j = pick[0] ^ which
        for c in range(col_tiles):
            total = tile_of(
                root_ref, c, col_tiles, n, pl.multiple_of(j * rows, rows)
            )
            for part_buf in part_bufs:
                total += part_buf[step * spread + j, c].astype(F32)
            update = None
            for level in range(levels):
                row_buf = row_bufs[2 * level + which]
                for k in range(row_buf.shape[0]):
                    term = mxu_t(row_buf[k, step], cols[level][k, c])
                    update = term if update is None else update + term
            total -= update
            for h in range(halves):
                scratch[
                    which, pl.ds(h * col_tiles + c, n, stride=col_tiles * halves), :
                ] = total[:, h * LANES : (h + 1) * LANES]
        out_ref[pl.ds(pl.multiple_of(j * rows, rows), rows), :] = scratch[which].astype(BF16)


def finish(pick, root_rows, parts, rows, cols):
    tiles = sum(x.shape[0] for x in parts[0])
    _, col_tiles, n, _ = parts[0][0].shape
    spread = tiles // col_tiles
    lane_rows = root_rows.shape[0] // col_tiles
    lanes = pl.BlockSpec((lane_rows, LANES), lambda c, s: (c, 0))
    anywhere = pl.BlockSpec(memory_space=pl.ANY)
    flat = [x for level in rows for pair in level for x in pair]
    flat += [x for part in parts for x in part]
    count = sum(x.shape[0] for x in cols)
    return pl.pallas_call(
        functools.partial(finish_kernel, len(rows), [len(x) for x in parts]),
        grid_spec=pltpu.PrefetchScalarGridSpec(
            num_scalar_prefetch=1,
            grid=(col_tiles,),
            in_specs=[
                lanes,
                *[anywhere for _ in flat],
                *[whole_spec(x) for x in cols],
            ],
            out_specs=lanes,
            scratch_shapes=[
                pltpu.VMEM((spread, lane_rows // spread, LANES), F32),
                *[pltpu.VMEM(x.shape, BF16) for x in cols for _ in range(2)],
                *[pltpu.VMEM((tiles, col_tiles, n, n), BF16) for _ in parts],
                pltpu.SemaphoreType.DMA((2 * len(rows), col_tiles)),
                pltpu.SemaphoreType.DMA((sum(len(x) for x in parts),)),
            ],
        ),
        out_shape=jax.ShapeDtypeStruct(root_rows.shape, BF16),
        compiler_params=pltpu.CompilerParams(vmem_limit_bytes=VMEM),
        cost_estimate=pl.CostEstimate(
            flops=tiles * col_tiles * (count + 3) * 2 * n**3,
            bytes_accessed=tiles * col_tiles * n * n * 10,
            transcendentals=0,
        ),
        name="finish_root",
    )(pick, root_rows, *flat, *cols)


def strip(front, tile_row, groups, member, bits):
    piece = jnp.transpose(front[tile_row // groups], (1, 0, 2))
    if groups > 1:
        piece = jnp.where(member == tile_row % groups, piece, 0.0)
    return group_sum(piece, bits)


def solve(inverse, rows):
    return jnp.einsum("ks,csj->cjk", inverse, rows, precision=HIGHEST)


def placed(hot, panels):
    return jnp.einsum(
        "cqj,cjk->cqk", hot, panels, preferred_element_type=F32
    ).astype(BF16)


def moved(row_hot, block, col_hot):
    out = jnp.einsum("qs,csj->cqj", row_hot, block, precision=HIGHEST)
    return jnp.einsum("cqj,cpj->cqp", out, col_hot, precision=HIGHEST)


def product(rows, cols):
    return jnp.einsum("fsk,fcjk->csj", rows, cols, preferred_element_type=F32)


def hots(places, n):
    slots = jnp.arange(n, dtype=jnp.int32)
    return (places[:, None, :] == slots[None, :, None]).astype(BF16)


def places_of(scatter, order, pivot):
    tiles, n = scatter.shape
    tile_ids = jnp.arange(tiles, dtype=jnp.int32)[:, None]
    rows = tile_ids * n + jnp.arange(n, dtype=jnp.int32)[None, :]
    return jnp.where((rows < order) & (tile_ids != pivot), scatter, -1)


def panel_slices(panel_pair, sizes, members):
    n_tile = lax.axis_size("tile")
    stacked = jnp.stack(panel_pair)
    count, col_tiles, n, width = stacked.shape
    cut = stacked.reshape(count, col_tiles, n_tile, n // n_tile, width)
    cut = jnp.transpose(cut, (2, 0, 1, 3, 4))
    got = lax.all_to_all(cut, "tile", 0, 0, tiled=True)
    out = []
    for at in range(count):
        tiles = jnp.transpose(got[:, at], (1, 0, 2, 3))
        tiles = tiles.reshape(-1, sizes[at], n // n_tile, width)
        out.append(lax.dynamic_index_in_dim(tiles, members[at], 1, keepdims=True))
    return out


def per_device(
    leaf_fronts, middle_fronts, root_front, leaf_scatter, middle_scatter, leaf_orders, middle_orders
):
    n_cube, n_tile = lax.axis_size("cube"), lax.axis_size("tile")
    cube, tile = lax.axis_index("cube"), lax.axis_index("tile")
    g2, g1 = n_cube // 4, n_cube // 2
    bit2, bit1 = g2.bit_length() - 1, g1.bit_length() - 1
    f, p = cube // g2, cube // g1
    m2, m1 = cube % g2, cube % g1
    leaf_tiles, n, col_tiles, _ = leaf_fronts.shape
    mid_tiles = middle_fronts.shape[0]
    col_ids = jnp.arange(col_tiles, dtype=jnp.int32) * n_tile + tile
    spread = n_tile // n_cube

    places2 = places_of(leaf_scatter[f], leaf_orders[f], 0)
    places1 = places_of(middle_scatter[p], middle_orders[p], 1)
    cols2 = jnp.take(places2, col_ids, axis=0)
    cols1 = jnp.take(places1, col_ids, axis=0)
    hot2, hot1 = hots(cols2, n), hots(cols1, n)
    top2, top1 = hots(places2[1:3], n), hots(places1[2:3], n)
    slots = jnp.arange(n, dtype=jnp.int32)
    turned2 = (cols2[:, :, None] == slots).astype(BF16)
    turned1 = (cols1[:, :, None] == slots).astype(BF16)

    def at_tile(strips, tile_id):
        return strips[tile_id // n_tile]

    leaf0 = strip(leaf_fronts, 0, g2, m2, bit2)
    (corner2, ahead_1, ahead_2), stages = tile_spread(at_tile(leaf0, 0))

    rows2 = places2.reshape(-1, g2, 1, n)[:, m2]
    rows1 = places1.reshape(-1, g1, 1, n)[:, m1]
    parity2, parity1 = f % 2, p % 2
    leaf_lanes, mid_lanes, root_lanes = map(
        lane_rows, (leaf_fronts, middle_fronts, root_front)
    )
    got2, before, lifts = [], [], []
    for half in (1 - parity1, parity1):
        pick = jnp.stack([1 - parity2, half])
        sent = lift(pick, leaf_lanes, leaf_tiles, rows2, turned2, *before)
        got2.append(partner(sent, bit2))
        lifts.append(sent)
        before = [sent, stages[-2]] if len(stages) > 1 else [sent]

    def climbed(half, first, count, got, *after):
        pick = jnp.stack([parity2, half])
        return climb(
            pick, first, count, leaf_lanes, mid_lanes, got, mid_tiles, rows2, rows1, turned2, turned1, *after
        )

    count = mid_tiles // 2
    part = max(count // 2, BATCH)
    sent1 = []
    for first in range(0, count, part):
        before = [sent1[-1], corner2] if sent1 else [sent, stages[-1]]
        sent1.append(climbed(1 - parity1, first, part, got2[0], *before))
    got1 = [partner(x[at : at + BATCH], bit1) for x in sent1 for at in range(0, part, BATCH)]

    pieces = [strip(leaf_fronts, r, g2, m2, bit2) for r in (1, 2)]
    pieces = [gate(x, lifts[0]) for x in pieces]
    lifted = jnp.stack(
        [
            moved(top2[r - 1].astype(F32), pieces[r - 1], hot2.astype(F32))
            + strip(middle_fronts, r, g1, m1, bit2)
            for r in (1, 2)
        ]
    )
    base1 = lifted + partner(lifted, bit2)
    raised = moved(top1[0].astype(F32), base1[1], hot1.astype(F32))
    raised = raised + strip(root_front, 2, n_cube, cube, bit1)
    base0 = raised + partner(raised, bit1)
    is_one = tile % n_tile == 1
    ends = jnp.stack(
        [jnp.where(is_one, at_tile(base1[0], 1), at_tile(base1[0], 2)), at_tile(raised, 2)]
    )
    (_, ends1, ends2), _ = tile_spread(ends)
    end0 = ends2[1] + partner(ends2[1], bit1)

    upper2, inverse2 = cholesky(corner2, sent1[-1])
    panel2 = solve(inverse2, leaf0).astype(BF16)
    ahead2 = solve(inverse2, jnp.stack([ahead_1, ahead_2])).astype(BF16)
    lift2 = jnp.concatenate([placed(hot2, panel2), placed(top2, ahead2)])
    pair2 = jnp.stack([lift2, partner(lift2, bit2)])
    climb2 = placed(
        jnp.concatenate([hot1, top1]),
        jnp.concatenate([lift2[:col_tiles], lift2[col_tiles + 1 :]]),
    )
    across2 = jnp.stack([climb2, partner(climb2, bit1)])
    four2 = jnp.concatenate([across2, partner(across2, bit2)])
    kept1 = [climbed(parity1, 0, part, got2[1], lift2)]

    mine2, one2, two2 = pair2[:, :col_tiles], pair2[:, col_tiles], pair2[:, col_tiles + 1]
    ends = product(one2, pair2[:, col_tiles:])
    upper1, inverse1 = cholesky(ends1[0] - ends[0], kept1[-1], base0)
    front1 = base1[0] - product(one2, mine2)
    panel1 = solve(
        inverse1, jnp.concatenate([front1, (ends2[0] - ends[1])[None]])
    ).astype(BF16)

    climb1 = placed(jnp.concatenate([hot1, top1]), panel1)
    two1 = jnp.stack([climb1, partner(climb1, bit1)])
    spread2 = row_spread(four2[:, :col_tiles])
    if part < count:
        kept1.append(climbed(parity1, part, part, got2[1], climb1, got1[0]))
    six = jnp.concatenate([four2, two1])
    ends = product(six[:, col_tiles], six)
    spread1 = row_spread(two1[:, :col_tiles])
    upper0, inverse0 = cholesky(end0 - ends[col_tiles], kept1[-1], spread2[0][0], *got1[1:2])
    panel0 = solve(inverse0, base0 - ends[:col_tiles]).astype(BF16)
    panel0 = gate(panel0, spread1[0][0], *got1[2:3])
    panel0 = jnp.where((col_ids == 2)[:, None, None], jnp.zeros_like(panel0), panel0)

    cols = [four2[:, :col_tiles], two1[:, :col_tiles], panel0[None]]
    spreads = [spread2, spread1, row_spread(cols[2], spread2[2])]
    rows = [x[:2] for x in spreads]

    high = tile // n_cube
    last_moved = (tile ^ cube) & 1
    picks = jnp.stack([high, last_moved])
    schur = finish(picks, root_lanes, [kept1, got1], rows, cols)
    schur = schur.reshape(root_front.shape[0], n, n // LANES, col_tiles, LANES)
    schur = schur.transpose(0, 1, 3, 2, 4).reshape(root_front.shape)

    def with_corner(panel, upper, pivot):
        return jnp.where((col_ids == pivot)[:, None, None], upper.T.astype(BF16), panel)

    leaf_panel, middle_panel = panel_slices(
        (with_corner(panel2, upper2, 0), with_corner(panel1[:col_tiles], upper1, 1)),
        (g2, g1),
        (m2, m1),
    )
    part = n // n_tile
    cuts = [
        jnp.where(
            last_moved != 0,
            lax.dynamic_slice_in_dim(came[0], tile * part, part, 1),
            lax.dynamic_slice_in_dim(stayed[0], tile * part, part, 1),
        )
        for stayed, came in rows[-1]
    ]
    ordered = [jnp.where(high == j, cuts[0], cuts[1]) for j in range(spread)]
    root_panel = jnp.stack(ordered, 1).reshape(-1, part, n)
    root_ids = jnp.arange(root_front.shape[0], dtype=jnp.int32) * n_cube + cube
    corner_cut = lax.dynamic_slice_in_dim(upper0.T.astype(BF16), tile * part, part, 0)
    root_panel = jnp.where((root_ids == 2)[:, None, None], corner_cut, root_panel)
    return leaf_panel, middle_panel, root_panel[:, None], schur


def solution(mesh):
    front = P(None, "cube", None, "tile")
    panel = P(None, "cube", "tile", None)
    return jax.shard_map(
        per_device,
        mesh=mesh,
        in_specs=(front, front, front, P(), P(), P(), P()),
        out_specs=(panel, panel, panel, front),
        check_vma=False,
    )
```

```python
import functools

import jax
import jax.numpy as jnp
from jax import lax
from jax.experimental import pallas as pl
from jax.experimental.pallas import tpu as pltpu
from jax.sharding import PartitionSpec as P

HIGHEST = lax.Precision.HIGHEST
F32 = jnp.float32
BF16 = jnp.bfloat16
LANES = 128
BLOCK = 32
WIDTH = 8
BATCH = 2
VMEM = 50 << 20


def partner(block, apart):
    count = lax.axis_size("cube")
    route = [(low, low ^ 1 << apart) for low in range(count)]
    return lax.ppermute(block, "cube", route)


def group_sum(value, bits):
    for bit in range(bits):
        value = value + partner(value, bit)
    return value


def tile_spread(value):
    stages = []
    count = lax.axis_size("tile")
    me = lax.axis_index("tile")
    bit, filled = count >> 1, 1
    while bit >= 4:
        route = [
            (base + t, base + t + bit)
            for base in range(0, count, 2 * bit)
            if base % (2 * bit) == 0 and base // (2 * bit) < filled
            for t in range(3)
        ]
        moved = lax.ppermute(value, "tile", route)
        value = jnp.where(me & bit != 0, moved, value)
        stages.append(value)
        filled *= 2
        bit >>= 1
    other = lax.ppermute(
        value, "tile", [(t, t ^ 1) for t in range(count) if t % 4 != 3]
    )
    even = me & 1 == 0
    pair = jnp.stack([jnp.where(even, value, other), jnp.where(even, other, value)])
    stages.append(pair)
    across = lax.ppermute(pair, "tile", [(t, t ^ 2) for t in range(count)])
    front = me & 2 == 0
    low = jnp.where(front, pair, across)
    return (low[0], low[1], jnp.where(front, across[0], pair[0])), stages


def gate(value, *after):
    for x in after:
        token = x[(0,) * x.ndim]
        value = jnp.where(token == token, value, jnp.zeros_like(value))
    return value


def row_spread(value):
    n_cube, n_tile = lax.axis_size("cube"), lax.axis_size("tile")
    cube, tile = lax.axis_index("cube"), lax.axis_index("tile")
    missing = tile % n_cube ^ cube
    bits = [1 << b for b in range(n_cube.bit_length() - 2, -1, -1)]

    def moved(block, bit, done):
        route = []
        for m in range(n_cube):
            for t in range(n_tile):
                if ((t % n_cube) ^ m) & ~done == 0:
                    route.append((m * n_tile + t, m * n_tile + (t ^ bit)))
        return lax.ppermute(block, ("cube", "tile"), route)

    def step(block, bit, done):
        return jnp.where(missing & bit != 0, moved(block, bit, done), block)

    own = step(value, bits[0], 0)
    done = bits[0]
    other = moved(own, n_cube, done)
    for bit in bits[1:-1]:
        own, other = step(own, bit, done), step(other, bit, done)
        done |= bit
    last = bits[-1]
    return [own, moved(own, last, done), other, moved(other, last, done)]


def split3(value):
    high = value.astype(BF16)
    rest = value - high.astype(F32)
    middle = rest.astype(BF16)
    low = (rest - middle.astype(F32)).astype(BF16)
    return high, middle, low


def newton_rsqrt(value):
    guess = lax.rsqrt(value)
    return guess * (1.5 - 0.5 * value * guess * guess)


def newton_reciprocal(value):
    guess = pl.reciprocal(value, approx=True)
    return guess * (2.0 - value * guess)


def cholesky_kernel(a_ref, *refs):
    upper_ref, inverse_ref, pair_ref, work = refs[-4:]
    n = a_ref.shape[0]
    rows = lax.broadcasted_iota(jnp.int32, (n, n), 0)
    cols = lax.broadcasted_iota(jnp.int32, (n, n), 1)
    work[:, :n] = a_ref[...]
    work[:, n:] = jnp.where(rows == cols, 1.0, 0.0)
    for start in range(0, n, BLOCK):
        stop = start + BLOCK
        low = start // LANES * LANES
        high = n + -(-stop // LANES) * LANES
        parts = [
            work[start:stop, at : at + LANES] for at in range(low, high, LANES)
        ]
        for first in range(0, BLOCK, WIDTH):
            lane = start - low + first
            wide = [
                jnp.broadcast_to(parts[0][:, lane + i : lane + i + 1], (BLOCK, LANES))
                for i in range(WIDTH)
            ]
            for i in range(0, WIDTH, 2):
                j = first + i
                c0, c1 = wide[i], wide[i + 1]
                a = c0[j : j + 1, :]
                b = c0[j + 1 : j + 2, :]
                c = c1[j + 1 : j + 2, :]
                over = newton_reciprocal(a * c - b * b)
                g0 = (c * c0 - b * c1) * over
                g1 = (a * c1 - b * c0) * over
                for later in range(i + 2, WIDTH):
                    at = first + later
                    wide[later] = (
                        wide[later] - g0 * c0[at : at + 1, :] - g1 * c1[at : at + 1, :]
                    )
                inv_a = newton_rsqrt(a)
                below = b * inv_a
                inv_c = newton_rsqrt(c - below * below)
                for at, part in enumerate(parts):
                    r0 = part[j : j + 1, :]
                    r1 = part[j + 1 : j + 2, :]
                    u0 = r0 * inv_a
                    u1 = (r1 - below * u0) * inv_c
                    lanes = slice(low + at * LANES, low + (at + 1) * LANES)
                    work[start + j : start + j + 1, lanes] = u0
                    work[start + j + 1 : start + j + 2, lanes] = u1
                    parts[at] = part - g0 * r0 - g1 * r1
        if stop < n:
            block = work[start:stop, low:high]
            h, m, l = split3(block)
            right = jnp.concatenate([h, m, h, l, m, h], axis=0)
            keep = stop // LANES * LANES
            hl, ml, ll = (x[:, keep - low : n - low] for x in (h, m, l))
            left = jnp.concatenate([hl, hl, ml, hl, ml, ll], axis=0)
            update = lax.dot_general(
                left, right, (((0,), (0,)), ((), ())), preferred_element_type=F32
            )
            work[stop:, low:high] -= update[stop - keep :]
    upper_ref[...] = jnp.where(rows <= cols, work[:, :n], 0.0)
    inverse = jnp.where(rows >= cols, work[:, n:], 0.0)
    inverse_ref[...] = inverse
    high = inverse.astype(BF16)
    pair_ref[0] = high
    pair_ref[1] = (inverse - high.astype(F32)).astype(BF16)


def cholesky(corner, *after):
    n = corner.shape[0]
    shape = jax.ShapeDtypeStruct((n, n), F32)
    return pl.pallas_call(
        cholesky_kernel,
        out_shape=(shape, shape, jax.ShapeDtypeStruct((2, n, n), BF16)),
        in_specs=[
            pl.BlockSpec(memory_space=pltpu.VMEM),
            *[pl.BlockSpec(memory_space=pl.ANY) for _ in after],
        ],
        scratch_shapes=[pltpu.VMEM((n, 2 * n), F32)],
        compiler_params=pltpu.CompilerParams(vmem_limit_bytes=VMEM),
        cost_estimate=pl.CostEstimate(
            flops=20_000_000, bytes_accessed=12 * n * n, transcendentals=0
        ),
        name="cholesky_and_inverse",
    )(corner, *after)


def lane_rows(front):
    tiles, n, col_tiles, _ = front.shape
    halves = n // LANES
    split = front.reshape(tiles, n, col_tiles, halves, LANES)
    return split.transpose(0, 1, 3, 2, 4).reshape(-1, LANES)


def tile_of(ref, at, col_tiles, n, base=0):
    halves = n // LANES
    step = col_tiles * halves
    return jnp.concatenate(
        [
            ref[pl.ds(base + h * col_tiles + at, n, stride=step), :]
            for h in range(halves)
        ],
        axis=1,
    )


def one_hot(places, n):
    slots = lax.broadcasted_iota(jnp.int32, (n, n), 0)
    return jnp.where(slots == places, 1.0, 0.0).astype(BF16)


def mxu(left, right):
    return jnp.dot(left, right, preferred_element_type=F32)


def mxu_t(left, right):
    return lax.dot_general(
        left, right, (((1,), (1,)), ((), ())), preferred_element_type=F32
    )


def lift_kernel(pick, *refs):
    x_refs, row_refs = refs[:BATCH], refs[BATCH : 2 * BATCH]
    col_ref, out_ref = refs[2 * BATCH], refs[-1]
    col_tiles, n = out_ref.shape[1], out_ref.shape[2]
    for b in range(BATCH):
        row_hot = one_hot(row_refs[b][0], n)
        for c in range(col_tiles):
            tile = tile_of(x_refs[b], c, col_tiles, n).astype(BF16)
            half = mxu(row_hot, tile).astype(BF16)
            out_ref[b, c] = mxu(half, col_ref[c]).astype(BF16)


def whole_spec(x):
    return pl.BlockSpec(x.shape, lambda *_: (0,) * x.ndim)


def lane_spec(rows, index):
    return pl.BlockSpec((rows, LANES), lambda i, s: (index(i, s), 0))


def place_spec(n, index):
    return pl.BlockSpec((1, 1, n), lambda i, s: (index(i, s), 0, 0))


def lift(pick, front_rows, tiles, row_places, col_hot, *after):
    col_tiles, n, _ = col_hot.shape
    rows = front_rows.shape[0] // tiles
    count = tiles // 4

    def leaf(b):
        return lambda i, s: 2 * (2 * (BATCH * i + b) + s[1]) + s[0]

    return pl.pallas_call(
        lift_kernel,
        grid_spec=pltpu.PrefetchScalarGridSpec(
            num_scalar_prefetch=1,
            grid=(count // BATCH,),
            in_specs=[
                *[lane_spec(rows, leaf(b)) for b in range(BATCH)],
                *[place_spec(n, leaf(b)) for b in range(BATCH)],
                whole_spec(col_hot),
                *[pl.BlockSpec(memory_space=pl.ANY) for _ in after],
            ],
            out_specs=pl.BlockSpec((BATCH, col_tiles, n, n), lambda i, s: (i, 0, 0, 0)),
        ),
        out_shape=jax.ShapeDtypeStruct((count, col_tiles, n, n), BF16),
        compiler_params=pltpu.CompilerParams(vmem_limit_bytes=VMEM),
        cost_estimate=pl.CostEstimate(
            flops=count * col_tiles * 4 * 2 * n**3,
            bytes_accessed=count * col_tiles * n * n * 6,
            transcendentals=0,
        ),
        name="lift_leaf",
    )(pick, *[front_rows] * BATCH, *[row_places] * BATCH, col_hot, *after)


def climb_kernel(pick, *refs):
    batch = BATCH
    x_refs, mid_refs, row2_refs, row1_refs = (
        refs[k * batch : (k + 1) * batch] for k in range(4)
    )
    got_ref, col2_ref, col1_ref = refs[4 * batch : 4 * batch + 3]
    out_ref = refs[-1]
    col_tiles, n = out_ref.shape[1], out_ref.shape[2]
    for b in range(batch):
        hot2 = one_hot(row2_refs[b][0], n)
        hot1 = one_hot(row1_refs[b][0], n)
        for c in range(col_tiles):
            tile = tile_of(x_refs[b], c, col_tiles, n).astype(BF16)
            half = mxu(hot2, tile).astype(BF16)
            whole = mxu(half, col2_ref[c]) + got_ref[b, c].astype(F32)
            whole = (whole + tile_of(mid_refs[b], c, col_tiles, n)).astype(BF16)
            half = mxu(hot1, whole).astype(BF16)
            out_ref[b, c] = mxu(half, col1_ref[c]).astype(BF16)


def climb(pick, first, count, leaf_rows, mid_rows, got, tiles, row2, row1, col2, col1, *after):
    _, col_tiles, n, _ = got.shape
    rows = mid_rows.shape[0] // tiles

    def mid(b):
        return lambda i, s: 2 * (first + BATCH * i + b) + s[1]

    def leaf(b):
        return lambda i, s: 2 * mid(b)(i, s) + s[0]

    batch = range(BATCH)
    return pl.pallas_call(
        climb_kernel,
        grid_spec=pltpu.PrefetchScalarGridSpec(
            num_scalar_prefetch=1,
            grid=(count // BATCH,),
            in_specs=[
                *[lane_spec(rows, leaf(b)) for b in batch],
                *[lane_spec(rows, mid(b)) for b in batch],
                *[place_spec(n, leaf(b)) for b in batch],
                *[place_spec(n, mid(b)) for b in batch],
                pl.BlockSpec(
                    (BATCH, col_tiles, n, n), lambda i, s: (first // BATCH + i, 0, 0, 0)
                ),
                whole_spec(col2),
                whole_spec(col1),
                *[pl.BlockSpec(memory_space=pl.ANY) for _ in after],
            ],
            out_specs=pl.BlockSpec((BATCH, col_tiles, n, n), lambda i, s: (i, 0, 0, 0)),
        ),
        out_shape=jax.ShapeDtypeStruct((count, col_tiles, n, n), BF16),
        compiler_params=pltpu.CompilerParams(vmem_limit_bytes=VMEM),
        cost_estimate=pl.CostEstimate(
            flops=count * col_tiles * 8 * 2 * n**3,
            bytes_accessed=count * col_tiles * n * n * 12,
            transcendentals=0,
        ),
        name="climb_middle",
    )(
        pick,
        *[leaf_rows] * BATCH,
        *[mid_rows] * BATCH,
        *[row2] * BATCH,
        *[row1] * BATCH,
        got,
        col2,
        col1,
        *after,
    )


def split2(value):
    high = value.astype(BF16)
    return high, (value - high.astype(F32)).astype(BF16)


def raw_specs(raw, col_tiles):
    own, *rows = raw
    count, _, n, _ = own.shape

    def own_index(i, s):
        return (0, jnp.minimum(i, col_tiles - 1), 0, 0)

    def row_index(which, came):
        def index(i, s):
            at = jnp.clip(i - (which + 1) * col_tiles, 0, col_tiles - 1)
            return (0, jnp.where(s[1] == came, at, 0), 0, 0)

        return index

    indices = [own_index] + [row_index(w, c) for w in (0, 1) for c in (0, 1)]
    return [pl.BlockSpec((count, 1, n, n), index) for index in indices]


def raw_tile(pick, refs, k, col_tiles):
    own, stayed_a, came_a, stayed_b, came_b = (ref[k, 0] for ref in refs)
    i, came = pl.program_id(0), pick[1] != 0
    first = jnp.where(came, came_a, stayed_a)
    second = jnp.where(came, came_b, stayed_b)
    return jnp.where(i < col_tiles, own, jnp.where(i < 2 * col_tiles, first, second))


def tile_spec(x):
    return pl.BlockSpec((x.shape[0], 1, *x.shape[2:]), lambda i, s: (0, i, 0, 0))


def solved(inverse_ref, at, rows):
    high, low = inverse_ref[at, 0], inverse_ref[at, 1]
    total = mxu(high, rows[0]) + mxu(low, rows[0])
    if len(rows) > 1:
        total += mxu(high, rows[1])
    return total.astype(BF16)


def leaf_local_kernel(pick, inverse_ref, place_ref, *refs):
    raw, out_ref = refs[:5], refs[-1]
    n = out_ref.shape[-1]
    for f in range(out_ref.shape[0]):
        rows = raw_tile(pick, raw, f, pl.num_programs(0) // 3)
        factor = solved(inverse_ref, f, [rows])
        out_ref[f, 0] = mxu_t(one_hot(place_ref[f, 0], n), factor).astype(BF16)


def middle_local_kernel(pick, inverse_ref, place_ref, pivot_ref, leaf_ref, *refs):
    raw, out_ref = refs[:5], refs[-1]
    n = out_ref.shape[-1]
    for p in range(2):
        rows = raw_tile(pick, raw, p, pl.num_programs(0) // 3).astype(F32)
        for f in (p, p + 2):
            rows -= mxu_t(pivot_ref[f], leaf_ref[f, 0])
        hot = one_hot(place_ref[p, 0], n)
        factor = solved(inverse_ref, p, split2(rows))
        out_ref[4 + p, 0] = mxu_t(hot, factor).astype(BF16)
        for f in (p, p + 2):
            out_ref[f, 0] = mxu(hot, leaf_ref[f, 0]).astype(BF16)


def root_local_kernel(pick, inverse_ref, place_ref, pivot_ref, panel_ref, *refs):
    raw, out_ref = refs[:5], refs[-1]
    n = out_ref.shape[-1]
    rows = raw_tile(pick, raw, 0, pl.num_programs(0) // 3).astype(F32)
    for k in range(panel_ref.shape[0]):
        rows -= mxu_t(pivot_ref[k], panel_ref[k, 0])
    factor = solved(inverse_ref, 0, split2(rows))
    out_ref[0, 0] = mxu_t(one_hot(place_ref[0, 0], n), factor).astype(BF16)


def local(kernel, name, pick, inverse, places, constants, tiled, raw, panels, *after):
    _, col_tiles, n, _ = raw[0].shape
    tiles = 3 * col_tiles
    return pl.pallas_call(
        kernel,
        grid_spec=pltpu.PrefetchScalarGridSpec(
            num_scalar_prefetch=1,
            grid=(tiles,),
            in_specs=[
                whole_spec(inverse),
                tile_spec(places),
                *[whole_spec(x) for x in constants],
                *[tile_spec(x) for x in tiled],
                *raw_specs(raw, col_tiles),
                *[pl.BlockSpec(memory_space=pl.ANY) for _ in after],
            ],
            out_specs=pl.BlockSpec((panels, 1, n, n), lambda i, s: (0, i, 0, 0)),
        ),
        out_shape=jax.ShapeDtypeStruct((panels, tiles, n, n), BF16),
        compiler_params=pltpu.CompilerParams(vmem_limit_bytes=VMEM),
        cost_estimate=pl.CostEstimate(
            flops=tiles * panels * 5 * 2 * n**3,
            bytes_accessed=tiles * panels * n * n * 6,
            transcendentals=0,
        ),
        name=name,
    )(pick, inverse, places, *constants, *tiled, *raw, *after)


def finish_kernel(levels, counts, pick, root_ref, *refs):
    part_refs = refs[: sum(counts)]
    panels = refs[sum(counts) : sum(counts) + 3 * levels]
    out_ref = refs[sum(counts) + 3 * levels]
    scratch, *part_bufs, part_sem = refs[sum(counts) + 3 * levels + 1 :]
    step = pl.program_id(0)
    tiles, col_tiles, n, _ = part_bufs[0].shape
    halves = n // LANES
    rows = n * col_tiles * halves
    spread = tiles // col_tiles

    part_copies = []
    for which, count in enumerate(counts):
        size = tiles // count
        for q in range(count):
            at = len(part_copies)
            target = part_bufs[which].at[pl.ds(q * size, size)]
            part_copies.append(
                pltpu.make_async_copy(part_refs[at], target, part_sem.at[at])
            )

    @pl.when(step == 0)
    def _():
        for copy in part_copies:
            copy.start()
        for copy in part_copies:
            copy.wait()

    for which in range(spread):
        j = pick[0] ^ which
        for c in range(col_tiles):
            total = tile_of(
                root_ref, c, col_tiles, n, pl.multiple_of(j * rows, rows)
            )
            for part_buf in part_bufs:
                total += part_buf[step * spread + j, c].astype(F32)
            update = None
            for level in range(levels):
                col_ref, *row_refs = panels[3 * level : 3 * level + 3]
                for k in range(col_ref.shape[0]):
                    term = mxu_t(row_refs[which][k, 0], col_ref[k, c])
                    update = term if update is None else update + term
            total -= update
            for h in range(halves):
                scratch[
                    which, pl.ds(h * col_tiles + c, n, stride=col_tiles * halves), :
                ] = total[:, h * LANES : (h + 1) * LANES]
        out_ref[pl.ds(pl.multiple_of(j * rows, rows), rows), :] = scratch[which].astype(BF16)


def finish(pick, root_rows, parts, panels):
    tiles = sum(x.shape[0] for x in parts[0])
    _, col_tiles, n, _ = parts[0][0].shape
    spread = tiles // col_tiles
    lane_rows = root_rows.shape[0] // col_tiles
    lanes = pl.BlockSpec((lane_rows, LANES), lambda c, s: (c, 0))
    flat = [x for part in parts for x in part]
    count = sum(x.shape[0] for x in panels)

    def panel_specs(x):
        k = x.shape[0]
        return [
            pl.BlockSpec((k, col_tiles, n, n), lambda c, s: (0, 0, 0, 0)),
            pl.BlockSpec((k, 1, n, n), lambda c, s: (0, col_tiles + c, 0, 0)),
            pl.BlockSpec((k, 1, n, n), lambda c, s: (0, 2 * col_tiles + c, 0, 0)),
        ]

    return pl.pallas_call(
        functools.partial(finish_kernel, len(panels), [len(x) for x in parts]),
        grid_spec=pltpu.PrefetchScalarGridSpec(
            num_scalar_prefetch=1,
            grid=(col_tiles,),
            in_specs=[
                lanes,
                *[pl.BlockSpec(memory_space=pl.ANY) for _ in flat],
                *[spec for x in panels for spec in panel_specs(x)],
            ],
            out_specs=lanes,
            scratch_shapes=[
                pltpu.VMEM((spread, lane_rows // spread, LANES), F32),
                *[pltpu.VMEM((tiles, col_tiles, n, n), BF16) for _ in parts],
                pltpu.SemaphoreType.DMA((len(flat),)),
            ],
        ),
        out_shape=jax.ShapeDtypeStruct(root_rows.shape, BF16),
        compiler_params=pltpu.CompilerParams(vmem_limit_bytes=VMEM),
        cost_estimate=pl.CostEstimate(
            flops=tiles * col_tiles * (count + 3) * 2 * n**3,
            bytes_accessed=tiles * col_tiles * n * n * 10,
            transcendentals=0,
        ),
        name="finish_root",
    )(pick, root_rows, *flat, *[x for x in panels for _ in range(3)])


def strip(front, tile_row, groups, member, bits):
    piece = jnp.transpose(front[tile_row // groups], (1, 0, 2))
    if groups > 1:
        piece = jnp.where(member == tile_row % groups, piece, 0.0)
    return group_sum(piece, bits)


def solve(inverse, rows):
    return jnp.einsum("ks,csj->cjk", inverse, rows, precision=HIGHEST)


def placed(hot, panels):
    return jnp.einsum(
        "cqj,cjk->cqk", hot, panels, preferred_element_type=F32
    ).astype(BF16)


def moved(row_hot, block, col_hot):
    out = jnp.einsum("qs,csj->cqj", row_hot, block, precision=HIGHEST)
    return jnp.einsum("cqj,cpj->cqp", out, col_hot, precision=HIGHEST)


def product(rows, cols):
    return jnp.einsum("fsk,fcjk->csj", rows, cols, preferred_element_type=F32)


def hots(places, n):
    slots = jnp.arange(n, dtype=jnp.int32)
    return (places[:, None, :] == slots[None, :, None]).astype(BF16)


def places_of(scatter, order, pivot):
    _, tiles, n = scatter.shape
    tile_ids = jnp.arange(tiles, dtype=jnp.int32)[:, None]
    rows = tile_ids * n + jnp.arange(n, dtype=jnp.int32)[None, :]
    keep = (rows < order[:, None, None]) & (tile_ids != pivot)
    return jnp.where(keep, scatter, -1)


def panel_slices(panel_pair, sizes, members):
    n_tile = lax.axis_size("tile")
    stacked = jnp.stack(panel_pair)
    count, col_tiles, n, width = stacked.shape
    cut = stacked.reshape(count, col_tiles, n_tile, n // n_tile, width)
    cut = jnp.transpose(cut, (2, 0, 1, 3, 4))
    got = lax.all_to_all(cut, "tile", 0, 0, tiled=True)
    out = []
    for at in range(count):
        tiles = jnp.transpose(got[:, at], (1, 0, 2, 3))
        tiles = tiles.reshape(-1, sizes[at], n // n_tile, width)
        out.append(lax.dynamic_index_in_dim(tiles, members[at], 1, keepdims=True))
    return out


def per_device(
    leaf_fronts, middle_fronts, root_front, leaf_scatter, middle_scatter, leaf_orders, middle_orders
):
    n_cube, n_tile = lax.axis_size("cube"), lax.axis_size("tile")
    cube, tile = lax.axis_index("cube"), lax.axis_index("tile")
    g2, g1 = n_cube // 4, n_cube // 2
    bit2, bit1 = g2.bit_length() - 1, g1.bit_length() - 1
    f, p = cube // g2, cube // g1
    m2, m1 = cube % g2, cube % g1
    leaf_tiles, n, col_tiles, _ = leaf_fronts.shape
    mid_tiles = middle_fronts.shape[0]
    col_ids = jnp.arange(col_tiles, dtype=jnp.int32) * n_tile + tile
    spread = n_tile // n_cube
    front_ids = jnp.stack([f, f ^ 2, f ^ 1, f ^ 3])
    middle_ids = jnp.stack([p, p ^ 1])
    all2 = jnp.take(places_of(leaf_scatter, leaf_orders, 0), front_ids, axis=0)
    all1 = jnp.take(places_of(middle_scatter, middle_orders, 1), middle_ids, axis=0)
    high = tile // n_cube
    cols = jnp.arange(col_tiles, dtype=jnp.int32) * n_tile
    tile_ids = jnp.concatenate(
        [cols + tile, cols + cube + n_cube * high, cols + cube + n_cube * (high ^ 1)]
    )
    local2 = jnp.take(all2, tile_ids, axis=1)[:, :, None]
    local1 = jnp.take(all1, tile_ids, axis=1)[:, :, None]
    straight = jnp.arange(n, dtype=jnp.int32)
    local0 = jnp.where((tile_ids == 2)[:, None], -1, straight)[None, :, None]
    places2, places1 = all2[0], all1[0]
    cols2, cols1 = local2[0, :col_tiles, 0], local1[0, :col_tiles, 0]
    hot2, hot1 = hots(cols2, n), hots(cols1, n)
    top2, top1 = hots(places2[1:3], n), hots(all1[:, 2], n)
    slots = jnp.arange(n, dtype=jnp.int32)
    turned2 = (cols2[:, :, None] == slots).astype(BF16)
    turned1 = (cols1[:, :, None] == slots).astype(BF16)

    def at_tile(strips, tile_id):
        return strips[tile_id // n_tile]

    leaf0 = strip(leaf_fronts, 0, g2, m2, bit2)
    (corner2, ahead_1, ahead_2), stages = tile_spread(at_tile(leaf0, 0))

    rows2 = places2.reshape(-1, g2, 1, n)[:, m2]
    rows1 = places1.reshape(-1, g1, 1, n)[:, m1]
    parity2, parity1 = f % 2, p % 2
    leaf_lanes, mid_lanes, root_lanes = map(
        lane_rows, (leaf_fronts, middle_fronts, root_front)
    )
    got2, before, lifts = [], [], []
    for half in (1 - parity1, parity1):
        pick = jnp.stack([1 - parity2, half])
        sent = lift(pick, leaf_lanes, leaf_tiles, rows2, turned2, *before)
        got2.append(partner(sent, bit2))
        lifts.append(sent)
        before = [sent, stages[-2]] if len(stages) > 1 else [sent]

    def climbed(half, first, count, got, *after):
        pick = jnp.stack([parity2, half])
        return climb(
            pick, first, count, leaf_lanes, mid_lanes, got, mid_tiles, rows2, rows1, turned2, turned1, *after
        )

    count = mid_tiles // 2
    part = max(count // 2, BATCH)
    sent1 = []
    for first in range(0, count, part):
        before = [sent1[-1], corner2] if sent1 else [sent, stages[-1]]
        sent1.append(climbed(1 - parity1, first, part, got2[0], *before))
    got1 = [partner(x[at : at + BATCH], bit1) for x in sent1 for at in range(0, part, BATCH)]

    pieces = [strip(leaf_fronts, r, g2, m2, bit2) for r in (1, 2)]
    pieces = [gate(x, lifts[0]) for x in pieces]
    lifted = jnp.stack(
        [
            moved(top2[r - 1].astype(F32), pieces[r - 1], hot2.astype(F32))
            + strip(middle_fronts, r, g1, m1, bit2)
            for r in (1, 2)
        ]
    )
    base1 = lifted + partner(lifted, bit2)
    raised = moved(top1[0].astype(F32), base1[1], hot1.astype(F32))
    raised = raised + strip(root_front, 2, n_cube, cube, bit1)
    even = cube % 2 == 0
    rows1_, raised_ = base1[0].astype(BF16), raised.astype(BF16)
    mixed = partner(jnp.where(even, rows1_, raised_), bit1)
    mixed_too = partner(mixed, 0)
    far_rows1 = jnp.where(even, mixed, mixed_too)
    far_raised = jnp.where(even, mixed_too, mixed)
    base0 = raised + far_raised.astype(F32)
    both0 = (raised_.astype(F32) + far_raised.astype(F32)).astype(BF16)
    raw1 = jnp.stack([rows1_, far_rows1, both0])
    raw1 = [raw1, *row_spread(raw1)]
    is_one = tile % n_tile == 1
    ends = jnp.stack(
        [jnp.where(is_one, at_tile(base1[0], 1), at_tile(base1[0], 2)), at_tile(raised, 2)]
    )
    (_, ends1, ends2), _ = tile_spread(ends)
    end0 = ends2[1] + partner(ends2[1], bit1)

    near = leaf0.astype(BF16)
    near = jnp.stack([near, partner(near, bit1)])
    raw2 = jnp.concatenate([near, partner(near, bit2)])
    raw2 = [raw2, *row_spread(raw2)]
    picks = jnp.stack([high, (tile ^ cube) & 1])

    upper2, inverse2, parts2 = cholesky(corner2, sent1[-1])
    ahead2 = solve(inverse2, jnp.stack([ahead_1, ahead_2])).astype(BF16)
    pay2 = jnp.concatenate([parts2, placed(top2, ahead2)])
    pair2 = partner(pay2, bit2)
    across2 = partner(pay2, bit1)
    all_pay2 = jnp.stack([pay2, across2, pair2, partner(across2, bit2)])
    kept1 = [climbed(parity1, 0, part, got2[1], pay2)]

    one2 = jnp.stack([pay2[2], pair2[2]])
    two2 = jnp.stack([pay2[3], pair2[3]])
    ends = product(one2, jnp.stack([one2, two2], axis=1))
    upper1, inverse1, parts1 = cholesky(ends1[0] - ends[0], kept1[-1])
    two1 = solve(inverse1, (ends2[0] - ends[1])[None]).astype(BF16)
    pay1 = jnp.concatenate([parts1, placed(top1[:1], two1)])
    both1 = jnp.stack([pay1, partner(pay1, bit1)])
    leaf_tiles_ = local(
        leaf_local_kernel, "leaf_rows", picks, all_pay2[:, :2], local2, [], [], raw2, 4,
        pay1, got1[0],
    )
    if part < count:
        kept1.append(climbed(parity1, part, part, got2[1], pay1))
    raw_middle = [x[:2] for x in raw1]
    middle_tiles_ = local(
        middle_local_kernel, "middle_rows", picks, both1[:, :2], local1,
        [all_pay2[:, 2]], [leaf_tiles_], raw_middle, 6, kept1[-1], *got1[1:2],
    )

    two2 = placed(jnp.concatenate([top1, top1]), all_pay2[:, 3])
    six = jnp.concatenate([two2, both1[:, 2]])
    ends = product(six, six[:, None])
    upper0, inverse0, parts0 = cholesky(end0 - ends[0], kept1[-1])
    raw_root = [x[2:] for x in raw1]
    root_tiles_ = local(
        root_local_kernel, "root_rows", picks, parts0[None], local0,
        [six], [middle_tiles_], raw_root, 1, *got1[2:3],
    )

    schur = finish(picks, root_lanes, [kept1, got1], [middle_tiles_, root_tiles_])
    schur = schur.reshape(root_front.shape[0], n, n // LANES, col_tiles, LANES)
    schur = schur.transpose(0, 1, 3, 2, 4).reshape(root_front.shape)

    panel2 = solve(inverse2, leaf0).astype(BF16)
    front1 = base1[0] - product(one2, leaf_tiles_[0::2, :col_tiles])
    panel1 = solve(inverse1, front1).astype(BF16)

    def with_corner(panel, upper, pivot):
        return jnp.where((col_ids == pivot)[:, None, None], upper.T.astype(BF16), panel)

    front0 = base0 - product(six, middle_tiles_[:, :col_tiles])
    panel0 = solve(inverse0, front0).astype(BF16)
    leaf_panel, middle_panel = panel_slices(
        (with_corner(panel2, upper2, 0), with_corner(panel1, upper1, 1)),
        (g2, g1),
        (m2, m1),
    )
    [root_panel] = panel_slices([with_corner(panel0, upper0, 2)], [n_cube], [cube])
    return leaf_panel, middle_panel, root_panel, schur


def solution(mesh):
    front = P(None, "cube", None, "tile")
    panel = P(None, "cube", "tile", None)
    return jax.shard_map(
        per_device,
        mesh=mesh,
        in_specs=(front, front, front, P(), P(), P(), P()),
        out_specs=(panel, panel, panel, front),
        check_vma=False,
    )
```

```python
import functools

import jax
import jax.numpy as jnp
from jax import lax
from jax.experimental import pallas as pl
from jax.experimental.pallas import tpu as pltpu
from jax.sharding import PartitionSpec as P

HIGHEST = lax.Precision.HIGHEST
F32 = jnp.float32
BF16 = jnp.bfloat16
LANES = 128
BLOCK = 32
WIDTH = 8
BATCH = 2
VMEM = 50 << 20


def partner(block, apart):
    count = lax.axis_size("cube")
    route = [(low, low ^ 1 << apart) for low in range(count)]
    return lax.ppermute(block, "cube", route)


def group_sum(value, bits):
    for bit in range(bits):
        value = value + partner(value, bit)
    return value


def tile_spread(value):
    count = lax.axis_size("tile")
    me = lax.axis_index("tile")
    bit, filled = count >> 1, 1
    while bit >= 4:
        route = [
            (base + t, base + t + bit)
            for base in range(0, count, 2 * bit)
            if base % (2 * bit) == 0 and base // (2 * bit) < filled
            for t in range(3)
        ]
        moved = lax.ppermute(value, "tile", route)
        value = jnp.where(me & bit != 0, moved, value)
        filled *= 2
        bit >>= 1
    other = lax.ppermute(
        value, "tile", [(t, t ^ 1) for t in range(count) if t % 4 != 3]
    )
    even = me & 1 == 0
    pair = jnp.stack([jnp.where(even, value, other), jnp.where(even, other, value)])
    across = lax.ppermute(pair, "tile", [(t, t ^ 2) for t in range(count)])
    front = me & 2 == 0
    low = jnp.where(front, pair, across)
    return low[0], low[1], jnp.where(front, across[0], pair[0])


def gate(value, after):
    token = after[(0,) * after.ndim]
    return jnp.where(token == token, value, jnp.zeros_like(value))


def row_spread(value, *after):
    n_cube, n_tile = lax.axis_size("cube"), lax.axis_size("tile")
    cube, tile = lax.axis_index("cube"), lax.axis_index("tile")
    missing = tile % n_cube ^ cube
    bits = [1 << b for b in range(n_cube.bit_length() - 2, -1, -1)]

    def moved(block, bit, done):
        route = []
        for m in range(n_cube):
            for t in range(n_tile):
                if ((t % n_cube) ^ m) & ~done == 0:
                    route.append((m * n_tile + t, m * n_tile + (t ^ bit)))
        return lax.ppermute(block, ("cube", "tile"), route)

    def step(block, bit, done):
        return jnp.where(missing & bit != 0, moved(block, bit, done), block)

    own = step(value, bits[0], 0)
    for x in after:
        own = gate(own, x)
    done = bits[0]
    other = moved(own, n_cube, done)
    for bit in bits[1:-1]:
        own, other = step(own, bit, done), step(other, bit, done)
        done |= bit
    last = bits[-1]
    return [own, moved(own, last, done), other, moved(other, last, done)]


def split3(value):
    high = value.astype(BF16)
    rest = value - high.astype(F32)
    middle = rest.astype(BF16)
    low = (rest - middle.astype(F32)).astype(BF16)
    return high, middle, low


def newton_rsqrt(value):
    guess = lax.rsqrt(value)
    return guess * (1.5 - 0.5 * value * guess * guess)


def newton_reciprocal(value):
    guess = pl.reciprocal(value, approx=True)
    return guess * (2.0 - value * guess)


def cholesky_kernel(a_ref, *refs):
    upper_ref, inverse_ref, pair_ref, work = refs[-4:]
    n = a_ref.shape[0]
    rows = lax.broadcasted_iota(jnp.int32, (n, n), 0)
    cols = lax.broadcasted_iota(jnp.int32, (n, n), 1)
    work[:, :n] = a_ref[...]
    work[:, n:] = jnp.where(rows == cols, 1.0, 0.0)
    for start in range(0, n, BLOCK):
        stop = start + BLOCK
        low = start // LANES * LANES
        high = n + -(-stop // LANES) * LANES
        parts = [
            work[start:stop, at : at + LANES] for at in range(low, high, LANES)
        ]
        for first in range(0, BLOCK, WIDTH):
            lane = start - low + first
            wide = [
                jnp.broadcast_to(parts[0][:, lane + i : lane + i + 1], (BLOCK, LANES))
                for i in range(WIDTH)
            ]
            for i in range(0, WIDTH, 2):
                j = first + i
                c0, c1 = wide[i], wide[i + 1]
                a = c0[j : j + 1, :]
                b = c0[j + 1 : j + 2, :]
                c = c1[j + 1 : j + 2, :]
                over = newton_reciprocal(a * c - b * b)
                g0 = (c * c0 - b * c1) * over
                g1 = (a * c1 - b * c0) * over
                for later in range(i + 2, WIDTH):
                    at = first + later
                    wide[later] = (
                        wide[later] - g0 * c0[at : at + 1, :] - g1 * c1[at : at + 1, :]
                    )
                inv_a = newton_rsqrt(a)
                below = b * inv_a
                inv_c = newton_rsqrt(c - below * below)
                for at, part in enumerate(parts):
                    r0 = part[j : j + 1, :]
                    r1 = part[j + 1 : j + 2, :]
                    u0 = r0 * inv_a
                    u1 = (r1 - below * u0) * inv_c
                    lanes = slice(low + at * LANES, low + (at + 1) * LANES)
                    work[start + j : start + j + 1, lanes] = u0
                    work[start + j + 1 : start + j + 2, lanes] = u1
                    parts[at] = part - g0 * r0 - g1 * r1
        if stop < n:
            block = work[start:stop, low:high]
            h, m, l = split3(block)
            right = jnp.concatenate([h, m, h, l, m, h], axis=0)
            keep = stop // LANES * LANES
            hl, ml, ll = (x[:, keep - low : n - low] for x in (h, m, l))
            left = jnp.concatenate([hl, hl, ml, hl, ml, ll], axis=0)
            update = lax.dot_general(
                left, right, (((0,), (0,)), ((), ())), preferred_element_type=F32
            )
            work[stop:, low:high] -= update[stop - keep :]
    upper_ref[...] = jnp.where(rows <= cols, work[:, :n], 0.0)
    inverse = jnp.where(rows >= cols, work[:, n:], 0.0)
    inverse_ref[...] = inverse
    high = inverse.astype(BF16)
    pair_ref[0] = high
    pair_ref[1] = (inverse - high.astype(F32)).astype(BF16)


def cholesky(corner, *after):
    n = corner.shape[0]
    shape = jax.ShapeDtypeStruct((n, n), F32)
    return pl.pallas_call(
        cholesky_kernel,
        out_shape=(shape, shape, jax.ShapeDtypeStruct((2, n, n), BF16)),
        in_specs=[
            pl.BlockSpec(memory_space=pltpu.VMEM),
            *[pl.BlockSpec(memory_space=pl.ANY) for _ in after],
        ],
        scratch_shapes=[pltpu.VMEM((n, 2 * n), F32)],
        compiler_params=pltpu.CompilerParams(vmem_limit_bytes=VMEM),
        cost_estimate=pl.CostEstimate(
            flops=20_000_000, bytes_accessed=12 * n * n, transcendentals=0
        ),
        name="cholesky_and_inverse",
    )(corner, *after)


def lane_rows(front):
    tiles, n, col_tiles, _ = front.shape
    halves = n // LANES
    split = front.reshape(tiles, n, col_tiles, halves, LANES)
    return split.transpose(0, 1, 3, 2, 4).reshape(-1, LANES)


def tile_of(ref, at, col_tiles, n, base=0):
    halves = n // LANES
    step = col_tiles * halves
    return jnp.concatenate(
        [
            ref[pl.ds(base + h * col_tiles + at, n, stride=step), :]
            for h in range(halves)
        ],
        axis=1,
    )


def one_hot(places, n):
    slots = lax.broadcasted_iota(jnp.int32, (n, n), 0)
    return jnp.where(slots == places, 1.0, 0.0).astype(BF16)


def mxu(left, right):
    return jnp.dot(left, right, preferred_element_type=F32)


def mxu_t(left, right):
    return lax.dot_general(
        left, right, (((1,), (1,)), ((), ())), preferred_element_type=F32
    )


def lift_kernel(pick, *refs):
    x_refs, row_refs = refs[:BATCH], refs[BATCH : 2 * BATCH]
    col_ref, out_ref = refs[2 * BATCH], refs[-1]
    col_tiles, n = out_ref.shape[1], out_ref.shape[2]
    for b in range(BATCH):
        row_hot = one_hot(row_refs[b][0], n)
        for c in range(col_tiles):
            tile = tile_of(x_refs[b], c, col_tiles, n).astype(BF16)
            half = mxu(row_hot, tile).astype(BF16)
            out_ref[b, c] = mxu(half, col_ref[c]).astype(BF16)


def whole_spec(x):
    return pl.BlockSpec(x.shape, lambda *_: (0,) * x.ndim)


def lane_spec(rows, index):
    return pl.BlockSpec((rows, LANES), lambda i, s: (index(i, s), 0))


def place_spec(n, index):
    return pl.BlockSpec((1, 1, n), lambda i, s: (index(i, s), 0, 0))


def lift(pick, front_rows, tiles, row_places, col_hot, *after):
    col_tiles, n, _ = col_hot.shape
    rows = front_rows.shape[0] // tiles
    count = tiles // 4

    def leaf(b):
        return lambda i, s: 2 * (2 * (BATCH * i + b) + s[1]) + s[0]

    return pl.pallas_call(
        lift_kernel,
        grid_spec=pltpu.PrefetchScalarGridSpec(
            num_scalar_prefetch=1,
            grid=(count // BATCH,),
            in_specs=[
                *[lane_spec(rows, leaf(b)) for b in range(BATCH)],
                *[place_spec(n, leaf(b)) for b in range(BATCH)],
                whole_spec(col_hot),
                *[pl.BlockSpec(memory_space=pl.ANY) for _ in after],
            ],
            out_specs=pl.BlockSpec((BATCH, col_tiles, n, n), lambda i, s: (i, 0, 0, 0)),
        ),
        out_shape=jax.ShapeDtypeStruct((count, col_tiles, n, n), BF16),
        compiler_params=pltpu.CompilerParams(vmem_limit_bytes=VMEM),
        cost_estimate=pl.CostEstimate(
            flops=count * col_tiles * 4 * 2 * n**3,
            bytes_accessed=count * col_tiles * n * n * 6,
            transcendentals=0,
        ),
        name="lift_leaf",
    )(pick, *[front_rows] * BATCH, *[row_places] * BATCH, col_hot, *after)


def climb_kernel(pick, *refs):
    batch = BATCH
    x_refs, mid_refs, row2_refs, row1_refs = (
        refs[k * batch : (k + 1) * batch] for k in range(4)
    )
    got_ref, col2_ref, col1_ref = refs[4 * batch : 4 * batch + 3]
    out_ref = refs[-1]
    col_tiles, n = out_ref.shape[1], out_ref.shape[2]
    for b in range(batch):
        hot2 = one_hot(row2_refs[b][0], n)
        hot1 = one_hot(row1_refs[b][0], n)
        for c in range(col_tiles):
            tile = tile_of(x_refs[b], c, col_tiles, n).astype(BF16)
            half = mxu(hot2, tile).astype(BF16)
            whole = mxu(half, col2_ref[c]) + got_ref[b, c].astype(F32)
            whole = (whole + tile_of(mid_refs[b], c, col_tiles, n)).astype(BF16)
            half = mxu(hot1, whole).astype(BF16)
            out_ref[b, c] = mxu(half, col1_ref[c]).astype(BF16)


def climb(pick, first, count, leaf_rows, mid_rows, got, tiles, row2, row1, col2, col1, *after):
    _, col_tiles, n, _ = got.shape
    rows = mid_rows.shape[0] // tiles

    def mid(b):
        return lambda i, s: 2 * (first + BATCH * i + b) + s[1]

    def leaf(b):
        return lambda i, s: 2 * mid(b)(i, s) + s[0]

    batch = range(BATCH)
    return pl.pallas_call(
        climb_kernel,
        grid_spec=pltpu.PrefetchScalarGridSpec(
            num_scalar_prefetch=1,
            grid=(count // BATCH,),
            in_specs=[
                *[lane_spec(rows, leaf(b)) for b in batch],
                *[lane_spec(rows, mid(b)) for b in batch],
                *[place_spec(n, leaf(b)) for b in batch],
                *[place_spec(n, mid(b)) for b in batch],
                pl.BlockSpec(
                    (BATCH, col_tiles, n, n), lambda i, s: (first // BATCH + i, 0, 0, 0)
                ),
                whole_spec(col2),
                whole_spec(col1),
                *[pl.BlockSpec(memory_space=pl.ANY) for _ in after],
            ],
            out_specs=pl.BlockSpec((BATCH, col_tiles, n, n), lambda i, s: (i, 0, 0, 0)),
        ),
        out_shape=jax.ShapeDtypeStruct((count, col_tiles, n, n), BF16),
        compiler_params=pltpu.CompilerParams(vmem_limit_bytes=VMEM),
        cost_estimate=pl.CostEstimate(
            flops=count * col_tiles * 8 * 2 * n**3,
            bytes_accessed=count * col_tiles * n * n * 12,
            transcendentals=0,
        ),
        name="climb_middle",
    )(
        pick,
        *[leaf_rows] * BATCH,
        *[mid_rows] * BATCH,
        *[row2] * BATCH,
        *[row1] * BATCH,
        got,
        col2,
        col1,
        *after,
    )


def split2(value):
    high = value.astype(BF16)
    return high, (value - high.astype(F32)).astype(BF16)


def tiles_a_step(col_tiles):
    return 2 if col_tiles % 2 == 0 else 1


def raw_specs(raw, first, count):
    _, col_tiles, n, _ = raw[0].shape
    batch = tiles_a_step(col_tiles)
    steps = col_tiles // batch

    def own_index(i, s):
        return (first // count, jnp.minimum(i, steps - 1), 0, 0)

    def row_index(which, came):
        def index(i, s):
            at = jnp.clip(i - (which + 1) * steps, 0, steps - 1)
            return (first // count, jnp.where(s[1] == came, at, 0), 0, 0)

        return index

    indices = [own_index] + [row_index(w, c) for w in (0, 1) for c in (0, 1)]
    return [pl.BlockSpec((count, batch, n, n), index) for index in indices]


def raw_tile(pick, refs, k, b):
    own, stayed_a, came_a, stayed_b, came_b = (ref[k, b] for ref in refs)
    i, steps, came = pl.program_id(0), pl.num_programs(0) // 3, pick[1] != 0
    first = jnp.where(came, came_a, stayed_a)
    second = jnp.where(came, came_b, stayed_b)
    return jnp.where(i < steps, own, jnp.where(i < 2 * steps, first, second))


def tile_spec(x, batch):
    return pl.BlockSpec((x.shape[0], batch, *x.shape[2:]), lambda i, s: (0, i, 0, 0))


def solved(inverse_ref, at, rows):
    high, low = inverse_ref[at, 0], inverse_ref[at, 1]
    total = mxu(high, rows[0]) + mxu(low, rows[0])
    if len(rows) > 1:
        total += mxu(high, rows[1])
    return total.astype(BF16)


def leaf_local_kernel(pick, inverse_ref, place_ref, *refs):
    raw, out_ref = refs[:5], refs[-1]
    fronts, batch, n, _ = out_ref.shape
    for b in range(batch):
        for f in range(fronts):
            factor = solved(inverse_ref, f, [raw_tile(pick, raw, f, b)])
            out_ref[f, b] = mxu_t(one_hot(place_ref[f, b], n), factor).astype(BF16)


def middle_local_kernel(pick, inverse_ref, place_ref, pivot_ref, leaf_ref, *refs):
    raw, out_ref = refs[:5], refs[-1]
    _, batch, n, _ = out_ref.shape
    for b in range(batch):
        for p in range(2):
            rows = raw_tile(pick, raw, p, b).astype(F32)
            for f in (p, p + 2):
                rows -= mxu_t(pivot_ref[f], leaf_ref[f, b])
            hot = one_hot(place_ref[p, b], n)
            factor = solved(inverse_ref, p, split2(rows))
            out_ref[4 + p, b] = mxu_t(hot, factor).astype(BF16)
            for f in (p, p + 2):
                out_ref[f, b] = mxu(hot, leaf_ref[f, b]).astype(BF16)


def root_local_kernel(pick, inverse_ref, place_ref, pivot_ref, panel_ref, *refs):
    raw, out_ref = refs[:5], refs[-1]
    _, batch, n, _ = out_ref.shape
    for b in range(batch):
        rows = raw_tile(pick, raw, 0, b).astype(F32)
        for k in range(panel_ref.shape[0]):
            rows -= mxu_t(pivot_ref[k], panel_ref[k, b])
        factor = solved(inverse_ref, 0, split2(rows))
        out_ref[0, b] = mxu_t(one_hot(place_ref[0, b], n), factor).astype(BF16)


def local(kernel, name, pick, inverse, places, constants, tiled, raw, first, count, panels, *after):
    _, col_tiles, n, _ = raw[0].shape
    tiles = 3 * col_tiles
    batch = tiles_a_step(col_tiles)
    return pl.pallas_call(
        kernel,
        grid_spec=pltpu.PrefetchScalarGridSpec(
            num_scalar_prefetch=1,
            grid=(tiles // batch,),
            in_specs=[
                whole_spec(inverse),
                tile_spec(places, batch),
                *[whole_spec(x) for x in constants],
                *[tile_spec(x, batch) for x in tiled],
                *raw_specs(raw, first, count),
                *[pl.BlockSpec(memory_space=pl.ANY) for _ in after],
            ],
            out_specs=pl.BlockSpec((panels, batch, n, n), lambda i, s: (0, i, 0, 0)),
        ),
        out_shape=jax.ShapeDtypeStruct((panels, tiles, n, n), BF16),
        compiler_params=pltpu.CompilerParams(vmem_limit_bytes=VMEM),
        cost_estimate=pl.CostEstimate(
            flops=tiles * panels * 5 * 2 * n**3,
            bytes_accessed=tiles * panels * n * n * 6,
            transcendentals=0,
        ),
        name=name,
    )(pick, inverse, places, *constants, *tiled, *raw, *after)


def finish_kernel(levels, counts, pick, root_ref, *refs):
    part_refs = refs[: sum(counts)]
    panels = refs[sum(counts) : sum(counts) + 3 * levels]
    out_ref = refs[sum(counts) + 3 * levels]
    scratch, *part_bufs, part_sem = refs[sum(counts) + 3 * levels + 1 :]
    step = pl.program_id(0)
    tiles, col_tiles, n, _ = part_bufs[0].shape
    halves = n // LANES
    rows = n * col_tiles * halves
    spread = tiles // col_tiles

    part_copies = []
    for which, count in enumerate(counts):
        size = tiles // count
        for q in range(count):
            at = len(part_copies)
            target = part_bufs[which].at[pl.ds(q * size, size)]
            part_copies.append(
                pltpu.make_async_copy(part_refs[at], target, part_sem.at[at])
            )

    @pl.when(step == 0)
    def _():
        for copy in part_copies:
            copy.start()
        for copy in part_copies:
            copy.wait()

    for which in range(spread):
        j = pick[0] ^ which
        for c in range(col_tiles):
            total = tile_of(
                root_ref, c, col_tiles, n, pl.multiple_of(j * rows, rows)
            )
            for part_buf in part_bufs:
                total += part_buf[step * spread + j, c].astype(F32)
            update = None
            for level in range(levels):
                col_ref, *row_refs = panels[3 * level : 3 * level + 3]
                for k in range(col_ref.shape[0]):
                    term = mxu_t(row_refs[which][k, 0], col_ref[k, c])
                    update = term if update is None else update + term
            total -= update
            for h in range(halves):
                scratch[
                    which, pl.ds(h * col_tiles + c, n, stride=col_tiles * halves), :
                ] = total[:, h * LANES : (h + 1) * LANES]
        out_ref[pl.ds(pl.multiple_of(j * rows, rows), rows), :] = scratch[which].astype(BF16)


def finish(pick, root_rows, parts, panels):
    tiles = sum(x.shape[0] for x in parts[0])
    _, col_tiles, n, _ = parts[0][0].shape
    spread = tiles // col_tiles
    lane_rows = root_rows.shape[0] // col_tiles
    lanes = pl.BlockSpec((lane_rows, LANES), lambda c, s: (c, 0))
    flat = [x for part in parts for x in part]
    count = sum(x.shape[0] for x in panels)

    def panel_specs(x):
        k = x.shape[0]
        return [
            pl.BlockSpec((k, col_tiles, n, n), lambda c, s: (0, 0, 0, 0)),
            pl.BlockSpec((k, 1, n, n), lambda c, s: (0, col_tiles + c, 0, 0)),
            pl.BlockSpec((k, 1, n, n), lambda c, s: (0, 2 * col_tiles + c, 0, 0)),
        ]

    return pl.pallas_call(
        functools.partial(finish_kernel, len(panels), [len(x) for x in parts]),
        grid_spec=pltpu.PrefetchScalarGridSpec(
            num_scalar_prefetch=1,
            grid=(col_tiles,),
            in_specs=[
                lanes,
                *[pl.BlockSpec(memory_space=pl.ANY) for _ in flat],
                *[spec for x in panels for spec in panel_specs(x)],
            ],
            out_specs=lanes,
            scratch_shapes=[
                pltpu.VMEM((spread, lane_rows // spread, LANES), F32),
                *[pltpu.VMEM((tiles, col_tiles, n, n), BF16) for _ in parts],
                pltpu.SemaphoreType.DMA((len(flat),)),
            ],
        ),
        out_shape=jax.ShapeDtypeStruct(root_rows.shape, BF16),
        compiler_params=pltpu.CompilerParams(vmem_limit_bytes=VMEM),
        cost_estimate=pl.CostEstimate(
            flops=tiles * col_tiles * (count + 3) * 2 * n**3,
            bytes_accessed=tiles * col_tiles * n * n * 10,
            transcendentals=0,
        ),
        name="finish_root",
    )(pick, root_rows, *flat, *[x for x in panels for _ in range(3)])


def strip(front, tile_row, groups, member, bits):
    piece = jnp.transpose(front[tile_row // groups], (1, 0, 2))
    if groups > 1:
        piece = jnp.where(member == tile_row % groups, piece, 0.0)
    return group_sum(piece, bits)


def solve(inverse, rows):
    return jnp.einsum("ks,csj->cjk", inverse, rows, precision=HIGHEST)


def placed(hot, panels):
    return jnp.einsum(
        "cqj,cjk->cqk", hot, panels, preferred_element_type=F32
    ).astype(BF16)


def moved(row_hot, block, col_hot):
    out = jnp.einsum("qs,csj->cqj", row_hot, block, precision=HIGHEST)
    return jnp.einsum("cqj,cpj->cqp", out, col_hot, precision=HIGHEST)


def product(rows, cols):
    return jnp.einsum("fsk,fcjk->csj", rows, cols, preferred_element_type=F32)


def hots(places, n):
    slots = jnp.arange(n, dtype=jnp.int32)
    return (places[:, None, :] == slots[None, :, None]).astype(BF16)


def places_of(scatter, order, pivot):
    _, tiles, n = scatter.shape
    tile_ids = jnp.arange(tiles, dtype=jnp.int32)[:, None]
    rows = tile_ids * n + jnp.arange(n, dtype=jnp.int32)[None, :]
    keep = (rows < order[:, None, None]) & (tile_ids != pivot)
    return jnp.where(keep, scatter, -1)


def panel_slices(panel_pair, sizes, members):
    n_tile = lax.axis_size("tile")
    stacked = jnp.stack(panel_pair)
    count, col_tiles, n, width = stacked.shape
    cut = stacked.reshape(count, col_tiles, n_tile, n // n_tile, width)
    cut = jnp.transpose(cut, (2, 0, 1, 3, 4))
    got = lax.all_to_all(cut, "tile", 0, 0, tiled=True)
    out = []
    for at in range(count):
        tiles = jnp.transpose(got[:, at], (1, 0, 2, 3))
        tiles = tiles.reshape(-1, sizes[at], n // n_tile, width)
        out.append(lax.dynamic_index_in_dim(tiles, members[at], 1, keepdims=True))
    return out


def per_device(
    leaf_fronts, middle_fronts, root_front, leaf_scatter, middle_scatter, leaf_orders, middle_orders
):
    n_cube, n_tile = lax.axis_size("cube"), lax.axis_size("tile")
    cube, tile = lax.axis_index("cube"), lax.axis_index("tile")
    g2, g1 = n_cube // 4, n_cube // 2
    bit2, bit1 = g2.bit_length() - 1, g1.bit_length() - 1
    f, p = cube // g2, cube // g1
    m2, m1 = cube % g2, cube % g1
    leaf_tiles, n, col_tiles, _ = leaf_fronts.shape
    mid_tiles = middle_fronts.shape[0]
    col_ids = jnp.arange(col_tiles, dtype=jnp.int32) * n_tile + tile
    spread = n_tile // n_cube
    front_ids = jnp.stack([f, f ^ 2, f ^ 1, f ^ 3])
    middle_ids = jnp.stack([p, p ^ 1])
    all2 = jnp.take(places_of(leaf_scatter, leaf_orders, 0), front_ids, axis=0)
    all1 = jnp.take(places_of(middle_scatter, middle_orders, 1), middle_ids, axis=0)
    high = tile // n_cube
    cols = jnp.arange(col_tiles, dtype=jnp.int32) * n_tile
    tile_ids = jnp.concatenate(
        [cols + tile, cols + cube + n_cube * high, cols + cube + n_cube * (high ^ 1)]
    )
    local2 = jnp.take(all2, tile_ids, axis=1)[:, :, None]
    local1 = jnp.take(all1, tile_ids, axis=1)[:, :, None]
    straight = jnp.arange(n, dtype=jnp.int32)
    local0 = jnp.where((tile_ids == 2)[:, None], -1, straight)[None, :, None]
    places2, places1 = all2[0], all1[0]
    cols2, cols1 = local2[0, :col_tiles, 0], local1[0, :col_tiles, 0]
    hot2, hot1 = hots(cols2, n), hots(cols1, n)
    top2, top1 = hots(places2[1:3], n), hots(all1[:, 2], n)
    slots = jnp.arange(n, dtype=jnp.int32)
    turned2 = (cols2[:, :, None] == slots).astype(BF16)
    turned1 = (cols1[:, :, None] == slots).astype(BF16)

    def at_tile(strips, tile_id):
        return strips[tile_id // n_tile]

    leaf0 = strip(leaf_fronts, 0, g2, m2, bit2)
    corner2, ahead_1, ahead_2 = tile_spread(at_tile(leaf0, 0))

    rows2 = places2.reshape(-1, g2, 1, n)[:, m2]
    rows1 = places1.reshape(-1, g1, 1, n)[:, m1]
    parity2, parity1 = f % 2, p % 2
    leaf_lanes, mid_lanes, root_lanes = map(
        lane_rows, (leaf_fronts, middle_fronts, root_front)
    )
    got2 = []
    for half in (1 - parity1, parity1):
        pick = jnp.stack([1 - parity2, half])
        sent = lift(pick, leaf_lanes, leaf_tiles, rows2, turned2)
        got2.append(partner(sent, bit2))

    def climbed(half, first, count, got, *after):
        pick = jnp.stack([parity2, half])
        return climb(
            pick, first, count, leaf_lanes, mid_lanes, got, mid_tiles, rows2, rows1, turned2, turned1, *after
        )

    count = mid_tiles // 2
    part = max(count // 2, BATCH)
    sent1 = []
    for first in range(0, count, part):
        before = sent1[-1:]
        sent1.append(climbed(1 - parity1, first, part, got2[0], *before))
    got1 = [partner(x[at : at + BATCH], bit1) for x in sent1 for at in range(0, part, BATCH)]

    pieces = [strip(leaf_fronts, r, g2, m2, bit2) for r in (1, 2)]
    lifted = jnp.stack(
        [
            moved(top2[r - 1].astype(F32), pieces[r - 1], hot2.astype(F32))
            + strip(middle_fronts, r, g1, m1, bit2)
            for r in (1, 2)
        ]
    )
    base1 = lifted + partner(lifted, bit2)
    raised = moved(top1[0].astype(F32), base1[1], hot1.astype(F32))
    raised = raised + strip(root_front, 2, n_cube, cube, bit1)
    even = cube % 2 == 0
    rows1_, raised_ = base1[0].astype(BF16), raised.astype(BF16)
    mixed = partner(jnp.where(even, rows1_, raised_), bit1)
    mixed = gate(mixed, sent1[0])
    mixed_too = partner(mixed, 0)
    far_rows1 = jnp.where(even, mixed, mixed_too)
    far_raised = jnp.where(even, mixed_too, mixed)
    base0 = raised + far_raised.astype(F32)
    both0 = (raised_.astype(F32) + far_raised.astype(F32)).astype(BF16)
    raw1 = jnp.stack([rows1_, far_rows1, both0])
    raw1 = [raw1, *row_spread(raw1)]
    is_one = tile % n_tile == 1
    ends = jnp.stack(
        [jnp.where(is_one, at_tile(base1[0], 1), at_tile(base1[0], 2)), at_tile(raised, 2)]
    )
    _, ends1, ends2 = tile_spread(ends)
    end0 = ends2[1] + partner(ends2[1], bit1)

    near = leaf0.astype(BF16)
    near = jnp.stack([near, partner(near, bit1)])
    raw2 = jnp.concatenate([near, partner(near, bit2)])
    raw2 = [raw2, *row_spread(raw2, sent1[0])]
    picks = jnp.stack([high, (tile ^ cube) & 1])

    upper2, inverse2, parts2 = cholesky(corner2, sent1[0])
    ahead2 = solve(inverse2, jnp.stack([ahead_1, ahead_2])).astype(BF16)
    pay2 = jnp.concatenate([parts2, placed(top2, ahead2)])
    pair2 = partner(pay2, bit2)
    across2 = partner(pay2, bit1)
    all_pay2 = jnp.stack([pay2, across2, pair2, partner(across2, bit2)])
    kept1 = [climbed(parity1, 0, part, got2[1], pay2, sent1[-1])]

    one2 = jnp.stack([pay2[2], pair2[2]])
    two2 = jnp.stack([pay2[3], pair2[3]])
    ends = product(one2, jnp.stack([one2, two2], axis=1))
    upper1, inverse1, parts1 = cholesky(ends1[0] - ends[0], kept1[-1])
    two1 = solve(inverse1, (ends2[0] - ends[1])[None]).astype(BF16)
    pay1 = jnp.concatenate([parts1, placed(top1[:1], two1)])
    both1 = jnp.stack([pay1, partner(pay1, bit1)])
    leaf_tiles_ = local(
        leaf_local_kernel, "leaf_rows", picks, all_pay2[:, :2], local2, [], [], raw2, 0, 4, 4,
    )
    if part < count:
        kept1.append(climbed(parity1, part, part, got2[1], pay1))
    middle_tiles_ = local(
        middle_local_kernel, "middle_rows", picks, both1[:, :2], local1,
        [all_pay2[:, 2]], [leaf_tiles_], raw1, 0, 2, 6, kept1[-1], *got1[1:2],
    )

    two2 = placed(jnp.concatenate([top1, top1]), all_pay2[:, 3])
    six = jnp.concatenate([two2, both1[:, 2]])
    ends = product(six, six[:, None])
    upper0, inverse0, parts0 = cholesky(end0 - ends[0], kept1[-1])
    root_tiles_ = local(
        root_local_kernel, "root_rows", picks, parts0[None], local0,
        [six], [middle_tiles_], raw1, 2, 1, 1, *got1[2:3],
    )

    schur = finish(picks, root_lanes, [kept1, got1], [middle_tiles_, root_tiles_])
    schur = schur.reshape(root_front.shape[0], n, n // LANES, col_tiles, LANES)
    schur = schur.transpose(0, 1, 3, 2, 4).reshape(root_front.shape)

    panel2 = solve(inverse2, leaf0).astype(BF16)
    front1 = base1[0] - product(one2, leaf_tiles_[0::2, :col_tiles])
    panel1 = solve(inverse1, front1).astype(BF16)

    def with_corner(panel, upper, pivot):
        return jnp.where((col_ids == pivot)[:, None, None], upper.T.astype(BF16), panel)

    front0 = base0 - product(six, middle_tiles_[:, :col_tiles])
    panel0 = solve(inverse0, front0).astype(BF16)
    leaf_panel, middle_panel = panel_slices(
        (with_corner(panel2, upper2, 0), with_corner(panel1, upper1, 1)),
        (g2, g1),
        (m2, m1),
    )
    [root_panel] = panel_slices([with_corner(panel0, upper0, 2)], [n_cube], [cube])
    return leaf_panel, middle_panel, root_panel, schur


def solution(mesh):
    front = P(None, "cube", None, "tile")
    panel = P(None, "cube", "tile", None)
    return jax.shard_map(
        per_device,
        mesh=mesh,
        in_specs=(front, front, front, P(), P(), P(), P()),
        out_specs=(panel, panel, panel, front),
        check_vma=False,
    )
```

```python
import functools

import jax
import jax.numpy as jnp
from jax import lax
from jax.experimental import pallas as pl
from jax.experimental.pallas import tpu as pltpu
from jax.sharding import PartitionSpec as P

HIGHEST = lax.Precision.HIGHEST
F32 = jnp.float32
BF16 = jnp.bfloat16
LANES = 128
BLOCK = 32
WIDTH = 8
BATCH = 2
VMEM = 50 << 20


def partner(block, apart):
    count = lax.axis_size("cube")
    route = [(low, low ^ 1 << apart) for low in range(count)]
    return lax.ppermute(block, "cube", route)


def group_sum(value, bits):
    for bit in range(bits):
        value = value + partner(value, bit)
    return value


def tile_spread(value):
    count = lax.axis_size("tile")
    me = lax.axis_index("tile")
    bit, filled = count >> 1, 1
    while bit >= 4:
        route = [
            (base + t, base + t + bit)
            for base in range(0, count, 2 * bit)
            if base % (2 * bit) == 0 and base // (2 * bit) < filled
            for t in range(3)
        ]
        moved = lax.ppermute(value, "tile", route)
        value = jnp.where(me & bit != 0, moved, value)
        filled *= 2
        bit >>= 1
    early = value
    other = lax.ppermute(
        value, "tile", [(t, t ^ 1) for t in range(count) if t % 4 != 3]
    )
    even = me & 1 == 0
    pair = jnp.stack([jnp.where(even, value, other), jnp.where(even, other, value)])
    across = lax.ppermute(pair, "tile", [(t, t ^ 2) for t in range(count)])
    front = me & 2 == 0
    low = jnp.where(front, pair, across)
    return low[0], low[1], jnp.where(front, across[0], pair[0]), early


def gate(value, after):
    token = after[(0,) * after.ndim]
    return jnp.where(token == token, value, jnp.zeros_like(value))


def row_spread(value, after_first, after_second):
    n_cube, n_tile = lax.axis_size("cube"), lax.axis_size("tile")
    cube, tile = lax.axis_index("cube"), lax.axis_index("tile")
    missing = tile % n_cube ^ cube
    bits = [1 << b for b in range(n_cube.bit_length() - 2, -1, -1)]

    def moved(block, bit, done):
        route = []
        for m in range(n_cube):
            for t in range(n_tile):
                if ((t % n_cube) ^ m) & ~done == 0:
                    route.append((m * n_tile + t, m * n_tile + (t ^ bit)))
        return lax.ppermute(block, ("cube", "tile"), route)

    def step(block, bit, done):
        return jnp.where(missing & bit != 0, moved(block, bit, done), block)

    own = gate(step(value, bits[0], 0), after_first)
    done = bits[0]
    other = gate(moved(own, n_cube, done), after_second)
    for bit in bits[1:-1]:
        own, other = step(own, bit, done), step(other, bit, done)
        done |= bit
    last = bits[-1]
    return [own, moved(own, last, done), other, moved(other, last, done)]


def split3(value):
    high = value.astype(BF16)
    rest = value - high.astype(F32)
    middle = rest.astype(BF16)
    low = (rest - middle.astype(F32)).astype(BF16)
    return high, middle, low


def newton_rsqrt(value):
    guess = lax.rsqrt(value)
    return guess * (1.5 - 0.5 * value * guess * guess)


def newton_reciprocal(value):
    guess = pl.reciprocal(value, approx=True)
    return guess * (2.0 - value * guess)


def cholesky_kernel(a_ref, *refs):
    upper_ref, inverse_ref, pair_ref, work = refs[-4:]
    n = a_ref.shape[0]
    rows = lax.broadcasted_iota(jnp.int32, (n, n), 0)
    cols = lax.broadcasted_iota(jnp.int32, (n, n), 1)
    work[:, :n] = a_ref[...]
    work[:, n:] = jnp.where(rows == cols, 1.0, 0.0)
    for start in range(0, n, BLOCK):
        stop = start + BLOCK
        low = start // LANES * LANES
        high = n + -(-stop // LANES) * LANES
        parts = [
            work[start:stop, at : at + LANES] for at in range(low, high, LANES)
        ]
        for first in range(0, BLOCK, WIDTH):
            lane = start - low + first
            wide = [
                jnp.broadcast_to(parts[0][:, lane + i : lane + i + 1], (BLOCK, LANES))
                for i in range(WIDTH)
            ]
            for i in range(0, WIDTH, 2):
                j = first + i
                c0, c1 = wide[i], wide[i + 1]
                a = c0[j : j + 1, :]
                b = c0[j + 1 : j + 2, :]
                c = c1[j + 1 : j + 2, :]
                over = newton_reciprocal(a * c - b * b)
                g0 = (c * c0 - b * c1) * over
                g1 = (a * c1 - b * c0) * over
                for later in range(i + 2, WIDTH):
                    at = first + later
                    wide[later] = (
                        wide[later] - g0 * c0[at : at + 1, :] - g1 * c1[at : at + 1, :]
                    )
                inv_a = newton_rsqrt(a)
                below = b * inv_a
                inv_c = newton_rsqrt(c - below * below)
                for at, part in enumerate(parts):
                    r0 = part[j : j + 1, :]
                    r1 = part[j + 1 : j + 2, :]
                    u0 = r0 * inv_a
                    u1 = (r1 - below * u0) * inv_c
                    lanes = slice(low + at * LANES, low + (at + 1) * LANES)
                    work[start + j : start + j + 1, lanes] = u0
                    work[start + j + 1 : start + j + 2, lanes] = u1
                    parts[at] = part - g0 * r0 - g1 * r1
        if stop < n:
            block = work[start:stop, low:high]
            h, m, l = split3(block)
            right = jnp.concatenate([h, m, h, l, m, h], axis=0)
            keep = stop // LANES * LANES
            hl, ml, ll = (x[:, keep - low : n - low] for x in (h, m, l))
            left = jnp.concatenate([hl, hl, ml, hl, ml, ll], axis=0)
            update = lax.dot_general(
                left, right, (((0,), (0,)), ((), ())), preferred_element_type=F32
            )
            work[stop:, low:high] -= update[stop - keep :]
    upper_ref[...] = jnp.where(rows <= cols, work[:, :n], 0.0)
    inverse = jnp.where(rows >= cols, work[:, n:], 0.0)
    inverse_ref[...] = inverse
    high = inverse.astype(BF16)
    pair_ref[0] = high
    pair_ref[1] = (inverse - high.astype(F32)).astype(BF16)


def cholesky(corner, *after):
    n = corner.shape[0]
    shape = jax.ShapeDtypeStruct((n, n), F32)
    return pl.pallas_call(
        cholesky_kernel,
        out_shape=(shape, shape, jax.ShapeDtypeStruct((2, n, n), BF16)),
        in_specs=[
            pl.BlockSpec(memory_space=pltpu.VMEM),
            *[pl.BlockSpec(memory_space=pl.ANY) for _ in after],
        ],
        scratch_shapes=[pltpu.VMEM((n, 2 * n), F32)],
        compiler_params=pltpu.CompilerParams(vmem_limit_bytes=VMEM),
        cost_estimate=pl.CostEstimate(
            flops=20_000_000, bytes_accessed=12 * n * n, transcendentals=0
        ),
        name="cholesky_and_inverse",
    )(corner, *after)


def lane_rows(front):
    tiles, n, col_tiles, _ = front.shape
    halves = n // LANES
    split = front.reshape(tiles, n, col_tiles, halves, LANES)
    return split.transpose(0, 1, 3, 2, 4).reshape(-1, LANES)


def tile_of(ref, at, col_tiles, n, base=0):
    halves = n // LANES
    step = col_tiles * halves
    return jnp.concatenate(
        [
            ref[pl.ds(base + h * col_tiles + at, n, stride=step), :]
            for h in range(halves)
        ],
        axis=1,
    )


def one_hot(places, n):
    slots = lax.broadcasted_iota(jnp.int32, (n, n), 0)
    return jnp.where(slots == places, 1.0, 0.0).astype(BF16)


def mxu(left, right):
    return jnp.dot(left, right, preferred_element_type=F32)


def mxu_t(left, right):
    return lax.dot_general(
        left, right, (((1,), (1,)), ((), ())), preferred_element_type=F32
    )


def lift_kernel(pick, *refs):
    x_refs, row_refs = refs[:BATCH], refs[BATCH : 2 * BATCH]
    col_ref, out_ref = refs[2 * BATCH], refs[-1]
    col_tiles, n = out_ref.shape[1], out_ref.shape[2]
    for b in range(BATCH):
        row_hot = one_hot(row_refs[b][0], n)
        for c in range(col_tiles):
            tile = tile_of(x_refs[b], c, col_tiles, n).astype(BF16)
            half = mxu(row_hot, tile).astype(BF16)
            out_ref[b, c] = mxu(half, col_ref[c]).astype(BF16)


def whole_spec(x):
    return pl.BlockSpec(x.shape, lambda *_: (0,) * x.ndim)


def lane_spec(rows, index):
    return pl.BlockSpec((rows, LANES), lambda i, s: (index(i, s), 0))


def place_spec(n, index):
    return pl.BlockSpec((1, 1, n), lambda i, s: (index(i, s), 0, 0))


def lift(pick, front_rows, tiles, row_places, col_hot, *after):
    col_tiles, n, _ = col_hot.shape
    rows = front_rows.shape[0] // tiles
    count = tiles // 4

    def leaf(b):
        return lambda i, s: 2 * (2 * (BATCH * i + b) + s[1]) + s[0]

    return pl.pallas_call(
        lift_kernel,
        grid_spec=pltpu.PrefetchScalarGridSpec(
            num_scalar_prefetch=1,
            grid=(count // BATCH,),
            in_specs=[
                *[lane_spec(rows, leaf(b)) for b in range(BATCH)],
                *[place_spec(n, leaf(b)) for b in range(BATCH)],
                whole_spec(col_hot),
                *[pl.BlockSpec(memory_space=pl.ANY) for _ in after],
            ],
            out_specs=pl.BlockSpec((BATCH, col_tiles, n, n), lambda i, s: (i, 0, 0, 0)),
        ),
        out_shape=jax.ShapeDtypeStruct((count, col_tiles, n, n), BF16),
        compiler_params=pltpu.CompilerParams(vmem_limit_bytes=VMEM),
        cost_estimate=pl.CostEstimate(
            flops=count * col_tiles * 4 * 2 * n**3,
            bytes_accessed=count * col_tiles * n * n * 6,
            transcendentals=0,
        ),
        name="lift_leaf",
    )(pick, *[front_rows] * BATCH, *[row_places] * BATCH, col_hot, *after)


def climb_kernel(pick, *refs):
    batch = BATCH
    x_refs, mid_refs, row2_refs, row1_refs = (
        refs[k * batch : (k + 1) * batch] for k in range(4)
    )
    got_ref, col2_ref, col1_ref = refs[4 * batch : 4 * batch + 3]
    out_ref = refs[-1]
    col_tiles, n = out_ref.shape[1], out_ref.shape[2]
    for b in range(batch):
        hot2 = one_hot(row2_refs[b][0], n)
        hot1 = one_hot(row1_refs[b][0], n)
        for c in range(col_tiles):
            tile = tile_of(x_refs[b], c, col_tiles, n).astype(BF16)
            half = mxu(hot2, tile).astype(BF16)
            whole = mxu(half, col2_ref[c]) + got_ref[b, c].astype(F32)
            whole = (whole + tile_of(mid_refs[b], c, col_tiles, n)).astype(BF16)
            half = mxu(hot1, whole).astype(BF16)
            out_ref[b, c] = mxu(half, col1_ref[c]).astype(BF16)


def climb(pick, first, count, leaf_rows, mid_rows, got, tiles, row2, row1, col2, col1, *after):
    _, col_tiles, n, _ = got.shape
    rows = mid_rows.shape[0] // tiles

    def mid(b):
        return lambda i, s: 2 * (first + BATCH * i + b) + s[1]

    def leaf(b):
        return lambda i, s: 2 * mid(b)(i, s) + s[0]

    batch = range(BATCH)
    return pl.pallas_call(
        climb_kernel,
        grid_spec=pltpu.PrefetchScalarGridSpec(
            num_scalar_prefetch=1,
            grid=(count // BATCH,),
            in_specs=[
                *[lane_spec(rows, leaf(b)) for b in batch],
                *[lane_spec(rows, mid(b)) for b in batch],
                *[place_spec(n, leaf(b)) for b in batch],
                *[place_spec(n, mid(b)) for b in batch],
                pl.BlockSpec(
                    (BATCH, col_tiles, n, n), lambda i, s: (first // BATCH + i, 0, 0, 0)
                ),
                whole_spec(col2),
                whole_spec(col1),
                *[pl.BlockSpec(memory_space=pl.ANY) for _ in after],
            ],
            out_specs=pl.BlockSpec((BATCH, col_tiles, n, n), lambda i, s: (i, 0, 0, 0)),
        ),
        out_shape=jax.ShapeDtypeStruct((count, col_tiles, n, n), BF16),
        compiler_params=pltpu.CompilerParams(vmem_limit_bytes=VMEM),
        cost_estimate=pl.CostEstimate(
            flops=count * col_tiles * 8 * 2 * n**3,
            bytes_accessed=count * col_tiles * n * n * 12,
            transcendentals=0,
        ),
        name="climb_middle",
    )(
        pick,
        *[leaf_rows] * BATCH,
        *[mid_rows] * BATCH,
        *[row2] * BATCH,
        *[row1] * BATCH,
        got,
        col2,
        col1,
        *after,
    )


def split2(value):
    high = value.astype(BF16)
    return high, (value - high.astype(F32)).astype(BF16)


def tiles_a_step(col_tiles):
    return 2 if col_tiles % 2 == 0 else 1


def raw_specs(raw, first, count):
    _, col_tiles, n, _ = raw[0].shape
    batch = tiles_a_step(col_tiles)
    steps = col_tiles // batch

    def own_index(i, s):
        return (first // count, jnp.minimum(i, steps - 1), 0, 0)

    def row_index(which, came):
        def index(i, s):
            at = jnp.clip(i - (which + 1) * steps, 0, steps - 1)
            return (first // count, jnp.where(s[1] == came, at, 0), 0, 0)

        return index

    indices = [own_index] + [row_index(w, c) for w in (0, 1) for c in (0, 1)]
    return [pl.BlockSpec((count, batch, n, n), index) for index in indices]


def take_raw(pick, refs, buffer):
    i, steps = pl.program_id(0), pl.num_programs(0) // 3
    came = pick[1] != 0
    stayed = jnp.logical_not(came)
    first = jnp.logical_and(i >= steps, i < 2 * steps)
    second = i >= 2 * steps
    holds = [
        i < steps,
        jnp.logical_and(first, stayed),
        jnp.logical_and(first, came),
        jnp.logical_and(second, stayed),
        jnp.logical_and(second, came),
    ]
    for hold, ref in zip(holds, refs):

        @pl.when(hold)
        def _():
            buffer[...] = ref[...]


def tile_spec(x, batch):
    return pl.BlockSpec((x.shape[0], batch, *x.shape[2:]), lambda i, s: (0, i, 0, 0))


def solved(inverse_ref, at, rows):
    high, low = inverse_ref[at, 0], inverse_ref[at, 1]
    total = mxu(high, rows[0]) + mxu(low, rows[0])
    if len(rows) > 1:
        total += mxu(high, rows[1])
    return total.astype(BF16)


def leaf_local_kernel(pick, inverse_ref, place_ref, *refs):
    raw, out_ref, buffer = refs[:5], *refs[-2:]
    take_raw(pick, raw, buffer)
    fronts, batch, n, _ = out_ref.shape
    for b in range(batch):
        for f in range(fronts):
            factor = solved(inverse_ref, f, [buffer[f, b]])
            out_ref[f, b] = mxu_t(one_hot(place_ref[f, b], n), factor).astype(BF16)


def middle_local_kernel(pick, inverse_ref, place_ref, pivot_ref, leaf_ref, *refs):
    raw, out_ref, buffer = refs[:5], *refs[-2:]
    take_raw(pick, raw, buffer)
    _, batch, n, _ = out_ref.shape
    for b in range(batch):
        for p in range(2):
            rows = buffer[p, b].astype(F32)
            for f in (p, p + 2):
                rows -= mxu_t(pivot_ref[f], leaf_ref[f, b])
            hot = one_hot(place_ref[p, b], n)
            factor = solved(inverse_ref, p, split2(rows))
            out_ref[4 + p, b] = mxu_t(hot, factor).astype(BF16)
            for f in (p, p + 2):
                out_ref[f, b] = mxu(hot, leaf_ref[f, b]).astype(BF16)


def root_local_kernel(pick, inverse_ref, place_ref, pivot_ref, panel_ref, *refs):
    raw, out_ref, buffer = refs[:5], *refs[-2:]
    take_raw(pick, raw, buffer)
    _, batch, n, _ = out_ref.shape
    for b in range(batch):
        rows = buffer[0, b].astype(F32)
        for k in range(panel_ref.shape[0]):
            rows -= mxu_t(pivot_ref[k], panel_ref[k, b])
        factor = solved(inverse_ref, 0, split2(rows))
        out_ref[0, b] = mxu_t(one_hot(place_ref[0, b], n), factor).astype(BF16)


def local(kernel, name, pick, inverse, places, constants, tiled, raw, first, count, panels, *after):
    _, col_tiles, n, _ = raw[0].shape
    tiles = 3 * col_tiles
    batch = tiles_a_step(col_tiles)
    return pl.pallas_call(
        kernel,
        grid_spec=pltpu.PrefetchScalarGridSpec(
            num_scalar_prefetch=1,
            grid=(tiles // batch,),
            in_specs=[
                whole_spec(inverse),
                tile_spec(places, batch),
                *[whole_spec(x) for x in constants],
                *[tile_spec(x, batch) for x in tiled],
                *raw_specs(raw, first, count),
                *[pl.BlockSpec(memory_space=pl.ANY) for _ in after],
            ],
            out_specs=pl.BlockSpec((panels, batch, n, n), lambda i, s: (0, i, 0, 0)),
            scratch_shapes=[pltpu.VMEM((count, batch, n, n), BF16)],
        ),
        out_shape=jax.ShapeDtypeStruct((panels, tiles, n, n), BF16),
        compiler_params=pltpu.CompilerParams(vmem_limit_bytes=VMEM),
        cost_estimate=pl.CostEstimate(
            flops=tiles * panels * 5 * 2 * n**3,
            bytes_accessed=tiles * panels * n * n * 6,
            transcendentals=0,
        ),
        name=name,
    )(pick, inverse, places, *constants, *tiled, *raw, *after)


def finish_kernel(levels, counts, pick, root_ref, *refs):
    part_refs = refs[: sum(counts)]
    panels = refs[sum(counts) : sum(counts) + 3 * levels]
    out_ref = refs[sum(counts) + 3 * levels]
    scratch, *part_bufs, part_sem = refs[sum(counts) + 3 * levels + 1 :]
    step = pl.program_id(0)
    tiles, col_tiles, n, _ = part_bufs[0].shape
    halves = n // LANES
    rows = n * col_tiles * halves
    spread = tiles // col_tiles

    part_copies = []
    for which, count in enumerate(counts):
        size = tiles // count
        for q in range(count):
            at = len(part_copies)
            target = part_bufs[which].at[pl.ds(q * size, size)]
            part_copies.append(
                pltpu.make_async_copy(part_refs[at], target, part_sem.at[at])
            )

    @pl.when(step == 0)
    def _():
        for copy in part_copies:
            copy.start()
        for copy in part_copies:
            copy.wait()

    for which in range(spread):
        j = pick[0] ^ which
        for c in range(col_tiles):
            total = tile_of(
                root_ref, c, col_tiles, n, pl.multiple_of(j * rows, rows)
            )
            for part_buf in part_bufs:
                total += part_buf[step * spread + j, c].astype(F32)
            update = None
            for level in range(levels):
                col_ref, *row_refs = panels[3 * level : 3 * level + 3]
                for k in range(col_ref.shape[0]):
                    term = mxu_t(row_refs[which][k, 0], col_ref[k, c])
                    update = term if update is None else update + term
            total -= update
            for h in range(halves):
                scratch[
                    which, pl.ds(h * col_tiles + c, n, stride=col_tiles * halves), :
                ] = total[:, h * LANES : (h + 1) * LANES]
        out_ref[pl.ds(pl.multiple_of(j * rows, rows), rows), :] = scratch[which].astype(BF16)


def finish(pick, root_rows, parts, panels):
    tiles = sum(x.shape[0] for x in parts[0])
    _, col_tiles, n, _ = parts[0][0].shape
    spread = tiles // col_tiles
    lane_rows = root_rows.shape[0] // col_tiles
    lanes = pl.BlockSpec((lane_rows, LANES), lambda c, s: (c, 0))
    flat = [x for part in parts for x in part]
    count = sum(x.shape[0] for x in panels)

    def panel_specs(x):
        k = x.shape[0]
        return [
            pl.BlockSpec((k, col_tiles, n, n), lambda c, s: (0, 0, 0, 0)),
            pl.BlockSpec((k, 1, n, n), lambda c, s: (0, col_tiles + c, 0, 0)),
            pl.BlockSpec((k, 1, n, n), lambda c, s: (0, 2 * col_tiles + c, 0, 0)),
        ]

    return pl.pallas_call(
        functools.partial(finish_kernel, len(panels), [len(x) for x in parts]),
        grid_spec=pltpu.PrefetchScalarGridSpec(
            num_scalar_prefetch=1,
            grid=(col_tiles,),
            in_specs=[
                lanes,
                *[pl.BlockSpec(memory_space=pl.ANY) for _ in flat],
                *[spec for x in panels for spec in panel_specs(x)],
            ],
            out_specs=lanes,
            scratch_shapes=[
                pltpu.VMEM((spread, lane_rows // spread, LANES), F32),
                *[pltpu.VMEM((tiles, col_tiles, n, n), BF16) for _ in parts],
                pltpu.SemaphoreType.DMA((len(flat),)),
            ],
        ),
        out_shape=jax.ShapeDtypeStruct(root_rows.shape, BF16),
        compiler_params=pltpu.CompilerParams(vmem_limit_bytes=VMEM),
        cost_estimate=pl.CostEstimate(
            flops=tiles * col_tiles * (count + 3) * 2 * n**3,
            bytes_accessed=tiles * col_tiles * n * n * 10,
            transcendentals=0,
        ),
        name="finish_root",
    )(pick, root_rows, *flat, *[x for x in panels for _ in range(3)])


def strip(front, tile_row, groups, member, bits):
    piece = jnp.transpose(front[tile_row // groups], (1, 0, 2))
    if groups > 1:
        piece = jnp.where(member == tile_row % groups, piece, 0.0)
    return group_sum(piece, bits)


def solve(inverse, rows):
    return jnp.einsum("ks,csj->cjk", inverse, rows, precision=HIGHEST)


def placed(hot, panels):
    return jnp.einsum(
        "cqj,cjk->cqk", hot, panels, preferred_element_type=F32
    ).astype(BF16)


def moved(row_hot, block, col_hot):
    out = jnp.einsum("qs,csj->cqj", row_hot, block, precision=HIGHEST)
    return jnp.einsum("cqj,cpj->cqp", out, col_hot, precision=HIGHEST)


def product(rows, cols):
    return jnp.einsum("fsk,fcjk->csj", rows, cols, preferred_element_type=F32)


def hots(places, n):
    slots = jnp.arange(n, dtype=jnp.int32)
    return (places[:, None, :] == slots[None, :, None]).astype(BF16)


def places_of(scatter, order, pivot):
    _, tiles, n = scatter.shape
    tile_ids = jnp.arange(tiles, dtype=jnp.int32)[:, None]
    rows = tile_ids * n + jnp.arange(n, dtype=jnp.int32)[None, :]
    keep = (rows < order[:, None, None]) & (tile_ids != pivot)
    return jnp.where(keep, scatter, -1)


def panel_slices(panel_pair, sizes, members):
    n_tile = lax.axis_size("tile")
    stacked = jnp.stack(panel_pair)
    count, col_tiles, n, width = stacked.shape
    cut = stacked.reshape(count, col_tiles, n_tile, n // n_tile, width)
    cut = jnp.transpose(cut, (2, 0, 1, 3, 4))
    got = lax.all_to_all(cut, "tile", 0, 0, tiled=True)
    out = []
    for at in range(count):
        tiles = jnp.transpose(got[:, at], (1, 0, 2, 3))
        tiles = tiles.reshape(-1, sizes[at], n // n_tile, width)
        out.append(lax.dynamic_index_in_dim(tiles, members[at], 1, keepdims=True))
    return out


def per_device(
    leaf_fronts, middle_fronts, root_front, leaf_scatter, middle_scatter, leaf_orders, middle_orders
):
    n_cube, n_tile = lax.axis_size("cube"), lax.axis_size("tile")
    cube, tile = lax.axis_index("cube"), lax.axis_index("tile")
    g2, g1 = n_cube // 4, n_cube // 2
    bit2, bit1 = g2.bit_length() - 1, g1.bit_length() - 1
    f, p = cube // g2, cube // g1
    m2, m1 = cube % g2, cube % g1
    leaf_tiles, n, col_tiles, _ = leaf_fronts.shape
    mid_tiles = middle_fronts.shape[0]
    col_ids = jnp.arange(col_tiles, dtype=jnp.int32) * n_tile + tile
    spread = n_tile // n_cube
    front_ids = jnp.stack([f, f ^ 2, f ^ 1, f ^ 3])
    middle_ids = jnp.stack([p, p ^ 1])
    all2 = jnp.take(places_of(leaf_scatter, leaf_orders, 0), front_ids, axis=0)
    all1 = jnp.take(places_of(middle_scatter, middle_orders, 1), middle_ids, axis=0)
    high = tile // n_cube
    cols = jnp.arange(col_tiles, dtype=jnp.int32) * n_tile
    tile_ids = jnp.concatenate(
        [cols + tile, cols + cube + n_cube * high, cols + cube + n_cube * (high ^ 1)]
    )
    local2 = jnp.take(all2, tile_ids, axis=1)[:, :, None]
    local1 = jnp.take(all1, tile_ids, axis=1)[:, :, None]
    straight = jnp.arange(n, dtype=jnp.int32)
    local0 = jnp.where((tile_ids == 2)[:, None], -1, straight)[None, :, None]
    places2, places1 = all2[0], all1[0]
    cols2, cols1 = local2[0, :col_tiles, 0], local1[0, :col_tiles, 0]
    hot2, hot1 = hots(cols2, n), hots(cols1, n)
    top2, top1 = hots(places2[1:3], n), hots(all1[:, 2], n)
    slots = jnp.arange(n, dtype=jnp.int32)
    turned2 = (cols2[:, :, None] == slots).astype(BF16)
    turned1 = (cols1[:, :, None] == slots).astype(BF16)

    def at_tile(strips, tile_id):
        return strips[tile_id // n_tile]

    leaf0 = strip(leaf_fronts, 0, g2, m2, bit2)
    corner2, ahead_1, ahead_2, early = tile_spread(at_tile(leaf0, 0))

    rows2 = places2.reshape(-1, g2, 1, n)[:, m2]
    rows1 = places1.reshape(-1, g1, 1, n)[:, m1]
    parity2, parity1 = f % 2, p % 2
    leaf_lanes, mid_lanes, root_lanes = map(
        lane_rows, (leaf_fronts, middle_fronts, root_front)
    )
    got2, before = [], []
    for half in (1 - parity1, parity1):
        pick = jnp.stack([1 - parity2, half])
        sent = lift(pick, leaf_lanes, leaf_tiles, rows2, turned2, *before)
        before = [early]
        got2.append(partner(sent, bit2))

    def climbed(half, first, count, got, *after):
        pick = jnp.stack([parity2, half])
        return climb(
            pick, first, count, leaf_lanes, mid_lanes, got, mid_tiles, rows2, rows1, turned2, turned1, *after
        )

    count = mid_tiles // 2
    part = max(count // 2, BATCH)
    sent1 = []
    for first in range(0, count, part):
        before = sent1[-1:]
        sent1.append(climbed(1 - parity1, first, part, got2[0], *before))
    got1 = [partner(x, bit1) for x in sent1]

    pieces = [strip(leaf_fronts, r, g2, m2, bit2) for r in (1, 2)]
    lifted = jnp.stack(
        [
            moved(top2[r - 1].astype(F32), pieces[r - 1], hot2.astype(F32))
            + strip(middle_fronts, r, g1, m1, bit2)
            for r in (1, 2)
        ]
    )
    base1 = lifted + partner(lifted, bit2)
    raised = moved(top1[0].astype(F32), base1[1], hot1.astype(F32))
    raised = raised + strip(root_front, 2, n_cube, cube, bit1)
    even = cube % 2 == 0
    rows1_, raised_ = base1[0].astype(BF16), raised.astype(BF16)
    rows1_, raised_ = gate(rows1_, sent), gate(raised_, sent)
    mixed = partner(jnp.where(even, rows1_, raised_), bit1)
    mixed_too = partner(mixed, 0)
    far_rows1 = jnp.where(even, mixed, mixed_too)
    far_raised = jnp.where(even, mixed_too, mixed)
    base0 = raised + far_raised.astype(F32)
    both0 = (raised_.astype(F32) + far_raised.astype(F32)).astype(BF16)
    raw1 = jnp.stack([rows1_, far_rows1, both0])
    is_one = tile % n_tile == 1
    ends = jnp.stack(
        [jnp.where(is_one, at_tile(base1[0], 1), at_tile(base1[0], 2)), at_tile(raised, 2)]
    )
    _, ends1, ends2, _ = tile_spread(ends)
    end0 = ends2[1] + partner(ends2[1], bit1)

    near = leaf0.astype(BF16)
    near = jnp.stack([near, partner(near, bit1)])
    raw = jnp.concatenate([near, partner(near, bit2), raw1])
    picks = jnp.stack([high, (tile ^ cube) & 1])

    upper2, inverse2, parts2 = cholesky(corner2, sent)
    ahead2 = solve(inverse2, jnp.stack([ahead_1, ahead_2])).astype(BF16)
    pay2 = jnp.concatenate([parts2, placed(top2, ahead2)])
    pair2 = partner(pay2, bit2)
    across2 = partner(pay2, bit1)
    all_pay2 = jnp.stack([pay2, across2, pair2, partner(across2, bit2)])
    kept1 = [climbed(parity1, 0, part, got2[1], pay2, sent1[-1])]

    one2 = jnp.stack([pay2[2], pair2[2]])
    two2 = jnp.stack([pay2[3], pair2[3]])
    ends = product(one2, jnp.stack([one2, two2], axis=1))
    upper1, inverse1, parts1 = cholesky(ends1[0] - ends[0], kept1[-1])
    two1 = solve(inverse1, (ends2[0] - ends[1])[None]).astype(BF16)
    pay1 = jnp.concatenate([parts1, placed(top1[:1], two1)])
    both1 = jnp.stack([pay1, partner(pay1, bit1)])
    raw = [raw, *row_spread(raw, sent1[-1], pay1)]
    leaf_tiles_ = local(
        leaf_local_kernel, "leaf_rows", picks, all_pay2[:, :2], local2, [], [], raw, 0, 4, 4,
    )
    if part < count:
        kept1.append(climbed(parity1, part, part, got2[1], pay1, got1[0]))
    middle_tiles_ = local(
        middle_local_kernel, "middle_rows", picks, both1[:, :2], local1,
        [all_pay2[:, 2]], [leaf_tiles_], raw, 4, 2, 6, kept1[-1], *got1[1:],
    )

    two2 = placed(jnp.concatenate([top1, top1]), all_pay2[:, 3])
    six = jnp.concatenate([two2, both1[:, 2]])
    ends = product(six, six[:, None])
    upper0, inverse0, parts0 = cholesky(end0 - ends[0], kept1[-1])
    root_tiles_ = local(
        root_local_kernel, "root_rows", picks, parts0[None], local0,
        [six], [middle_tiles_], raw, 6, 1, 1,
    )

    schur = finish(picks, root_lanes, [kept1, got1], [middle_tiles_, root_tiles_])
    schur = schur.reshape(root_front.shape[0], n, n // LANES, col_tiles, LANES)
    schur = schur.transpose(0, 1, 3, 2, 4).reshape(root_front.shape)

    panel2 = solve(inverse2, leaf0).astype(BF16)
    front1 = base1[0] - product(one2, leaf_tiles_[0::2, :col_tiles])
    panel1 = solve(inverse1, front1).astype(BF16)

    def with_corner(panel, upper, pivot):
        return jnp.where((col_ids == pivot)[:, None, None], upper.T.astype(BF16), panel)

    front0 = base0 - product(six, middle_tiles_[:, :col_tiles])
    panel0 = solve(inverse0, front0).astype(BF16)
    leaf_panel, middle_panel, root_panel = panel_slices(
        [
            with_corner(panel2, upper2, 0),
            with_corner(panel1, upper1, 1),
            with_corner(panel0, upper0, 2),
        ],
        [g2, g1, n_cube],
        [m2, m1, cube],
    )
    return leaf_panel, middle_panel, root_panel, schur


def solution(mesh):
    front = P(None, "cube", None, "tile")
    panel = P(None, "cube", "tile", None)
    return jax.shard_map(
        per_device,
        mesh=mesh,
        in_specs=(front, front, front, P(), P(), P(), P()),
        out_specs=(panel, panel, panel, front),
        check_vma=False,
    )
```

```python
import functools

import jax
import jax.numpy as jnp
from jax import lax
from jax.experimental import pallas as pl
from jax.experimental.pallas import tpu as pltpu
from jax.sharding import PartitionSpec as P

HIGHEST = lax.Precision.HIGHEST
F32 = jnp.float32
BF16 = jnp.bfloat16
LANES = 128
BLOCK = 32
WIDTH = 8
BATCH = 2
VMEM = 50 << 20


def partner(block, apart):
    count = lax.axis_size("cube")
    route = [(low, low ^ 1 << apart) for low in range(count)]
    return lax.ppermute(block, "cube", route)


def group_sum(value, bits):
    for bit in range(bits):
        value = value + partner(value, bit)
    return value


def tile_spread(value):
    stages = []
    count = lax.axis_size("tile")
    me = lax.axis_index("tile")
    bit, filled = count >> 1, 1
    while bit >= 4:
        route = [
            (base + t, base + t + bit)
            for base in range(0, count, 2 * bit)
            if base % (2 * bit) == 0 and base // (2 * bit) < filled
            for t in range(3)
        ]
        moved = lax.ppermute(value, "tile", route)
        value = jnp.where(me & bit != 0, moved, value)
        stages.append(value)
        filled *= 2
        bit >>= 1
    other = lax.ppermute(
        value, "tile", [(t, t ^ 1) for t in range(count) if t % 4 != 3]
    )
    even = me & 1 == 0
    pair = jnp.stack([jnp.where(even, value, other), jnp.where(even, other, value)])
    stages.append(pair)
    across = lax.ppermute(pair, "tile", [(t, t ^ 2) for t in range(count)])
    front = me & 2 == 0
    low = jnp.where(front, pair, across)
    return (low[0], low[1], jnp.where(front, across[0], pair[0])), stages


def gate(value, *after):
    for x in after:
        token = x[(0,) * x.ndim]
        value = jnp.where(token == token, value, jnp.zeros_like(value))
    return value


def row_spread(value):
    n_cube, n_tile = lax.axis_size("cube"), lax.axis_size("tile")
    cube, tile = lax.axis_index("cube"), lax.axis_index("tile")
    missing = tile % n_cube ^ cube
    bits = [1 << b for b in range(n_cube.bit_length() - 2, -1, -1)]

    def moved(block, bit, done):
        route = []
        for m in range(n_cube):
            for t in range(n_tile):
                if ((t % n_cube) ^ m) & ~done == 0:
                    route.append((m * n_tile + t, m * n_tile + (t ^ bit)))
        return lax.ppermute(block, ("cube", "tile"), route)

    def step(block, bit, done):
        return jnp.where(missing & bit != 0, moved(block, bit, done), block)

    own = step(value, bits[0], 0)
    done = bits[0]
    other = moved(own, n_cube, done)
    for bit in bits[1:-1]:
        own, other = step(own, bit, done), step(other, bit, done)
        done |= bit
    last = bits[-1]
    return [own, moved(own, last, done), other, moved(other, last, done)]


def split3(value):
    high = value.astype(BF16)
    rest = value - high.astype(F32)
    middle = rest.astype(BF16)
    low = (rest - middle.astype(F32)).astype(BF16)
    return high, middle, low


def newton_rsqrt(value):
    guess = lax.rsqrt(value)
    return guess * (1.5 - 0.5 * value * guess * guess)


def newton_reciprocal(value):
    guess = pl.reciprocal(value, approx=True)
    return guess * (2.0 - value * guess)


def cholesky_kernel(a_ref, *refs):
    upper_ref, inverse_ref, pair_ref, work = refs[-4:]
    n = a_ref.shape[0]
    rows = lax.broadcasted_iota(jnp.int32, (n, n), 0)
    cols = lax.broadcasted_iota(jnp.int32, (n, n), 1)
    work[:, :n] = a_ref[...]
    work[:, n:] = jnp.where(rows == cols, 1.0, 0.0)
    for start in range(0, n, BLOCK):
        stop = start + BLOCK
        low = start // LANES * LANES
        high = n + -(-stop // LANES) * LANES
        parts = [
            work[start:stop, at : at + LANES] for at in range(low, high, LANES)
        ]
        for first in range(0, BLOCK, WIDTH):
            lane = start - low + first
            wide = [
                jnp.broadcast_to(parts[0][:, lane + i : lane + i + 1], (BLOCK, LANES))
                for i in range(WIDTH)
            ]
            for i in range(0, WIDTH, 2):
                j = first + i
                c0, c1 = wide[i], wide[i + 1]
                a = c0[j : j + 1, :]
                b = c0[j + 1 : j + 2, :]
                c = c1[j + 1 : j + 2, :]
                over = newton_reciprocal(a * c - b * b)
                g0 = (c * c0 - b * c1) * over
                g1 = (a * c1 - b * c0) * over
                for later in range(i + 2, WIDTH):
                    at = first + later
                    wide[later] = (
                        wide[later] - g0 * c0[at : at + 1, :] - g1 * c1[at : at + 1, :]
                    )
                inv_a = newton_rsqrt(a)
                below = b * inv_a
                inv_c = newton_rsqrt(c - below * below)
                for at, part in enumerate(parts):
                    r0 = part[j : j + 1, :]
                    r1 = part[j + 1 : j + 2, :]
                    u0 = r0 * inv_a
                    u1 = (r1 - below * u0) * inv_c
                    lanes = slice(low + at * LANES, low + (at + 1) * LANES)
                    work[start + j : start + j + 1, lanes] = u0
                    work[start + j + 1 : start + j + 2, lanes] = u1
                    parts[at] = part - g0 * r0 - g1 * r1
        if stop < n:
            block = work[start:stop, low:high]
            h, m, l = split3(block)
            right = jnp.concatenate([h, m, h, l, m, h], axis=0)
            keep = stop // LANES * LANES
            hl, ml, ll = (x[:, keep - low : n - low] for x in (h, m, l))
            left = jnp.concatenate([hl, hl, ml, hl, ml, ll], axis=0)
            update = lax.dot_general(
                left, right, (((0,), (0,)), ((), ())), preferred_element_type=F32
            )
            work[stop:, low:high] -= update[stop - keep :]
    upper_ref[...] = jnp.where(rows <= cols, work[:, :n], 0.0)
    inverse = jnp.where(rows >= cols, work[:, n:], 0.0)
    inverse_ref[...] = inverse
    high = inverse.astype(BF16)
    pair_ref[0] = high
    pair_ref[1] = (inverse - high.astype(F32)).astype(BF16)


def cholesky(corner, *after):
    n = corner.shape[0]
    shape = jax.ShapeDtypeStruct((n, n), F32)
    return pl.pallas_call(
        cholesky_kernel,
        out_shape=(shape, shape, jax.ShapeDtypeStruct((2, n, n), BF16)),
        in_specs=[
            pl.BlockSpec(memory_space=pltpu.VMEM),
            *[pl.BlockSpec(memory_space=pl.ANY) for _ in after],
        ],
        scratch_shapes=[pltpu.VMEM((n, 2 * n), F32)],
        compiler_params=pltpu.CompilerParams(vmem_limit_bytes=VMEM),
        cost_estimate=pl.CostEstimate(
            flops=20_000_000, bytes_accessed=12 * n * n, transcendentals=0
        ),
        name="cholesky_and_inverse",
    )(corner, *after)


def lane_rows(front):
    tiles, n, col_tiles, _ = front.shape
    halves = n // LANES
    split = front.reshape(tiles, n, col_tiles, halves, LANES)
    return split.transpose(0, 1, 3, 2, 4).reshape(-1, LANES)


def tile_of(ref, at, col_tiles, n, base=0):
    halves = n // LANES
    step = col_tiles * halves
    return jnp.concatenate(
        [
            ref[pl.ds(base + h * col_tiles + at, n, stride=step), :]
            for h in range(halves)
        ],
        axis=1,
    )


def one_hot(places, n):
    slots = lax.broadcasted_iota(jnp.int32, (n, n), 0)
    return jnp.where(slots == places, 1.0, 0.0).astype(BF16)


def mxu(left, right):
    return jnp.dot(left, right, preferred_element_type=F32)


def mxu_t(left, right):
    return lax.dot_general(
        left, right, (((1,), (1,)), ((), ())), preferred_element_type=F32
    )


def lift_kernel(pick, *refs):
    x_refs, row_refs = refs[:BATCH], refs[BATCH : 2 * BATCH]
    col_ref, out_ref = refs[2 * BATCH], refs[-1]
    col_tiles, n = out_ref.shape[1], out_ref.shape[2]
    for b in range(BATCH):
        row_hot = one_hot(row_refs[b][0], n)
        for c in range(col_tiles):
            tile = tile_of(x_refs[b], c, col_tiles, n).astype(BF16)
            half = mxu(row_hot, tile).astype(BF16)
            out_ref[b, c] = mxu(half, col_ref[c]).astype(BF16)


def whole_spec(x):
    return pl.BlockSpec(x.shape, lambda *_: (0,) * x.ndim)


def lane_spec(rows, index):
    return pl.BlockSpec((rows, LANES), lambda i, s: (index(i, s), 0))


def place_spec(n, index):
    return pl.BlockSpec((1, 1, n), lambda i, s: (index(i, s), 0, 0))


def lift(pick, front_rows, tiles, row_places, col_hot, *after):
    col_tiles, n, _ = col_hot.shape
    rows = front_rows.shape[0] // tiles
    count = tiles // 4

    def leaf(b):
        return lambda i, s: 2 * (2 * (BATCH * i + b) + s[1]) + s[0]

    return pl.pallas_call(
        lift_kernel,
        grid_spec=pltpu.PrefetchScalarGridSpec(
            num_scalar_prefetch=1,
            grid=(count // BATCH,),
            in_specs=[
                *[lane_spec(rows, leaf(b)) for b in range(BATCH)],
                *[place_spec(n, leaf(b)) for b in range(BATCH)],
                whole_spec(col_hot),
                *[pl.BlockSpec(memory_space=pl.ANY) for _ in after],
            ],
            out_specs=pl.BlockSpec((BATCH, col_tiles, n, n), lambda i, s: (i, 0, 0, 0)),
        ),
        out_shape=jax.ShapeDtypeStruct((count, col_tiles, n, n), BF16),
        compiler_params=pltpu.CompilerParams(vmem_limit_bytes=VMEM),
        cost_estimate=pl.CostEstimate(
            flops=count * col_tiles * 4 * 2 * n**3,
            bytes_accessed=count * col_tiles * n * n * 6,
            transcendentals=0,
        ),
        name="lift_leaf",
    )(pick, *[front_rows] * BATCH, *[row_places] * BATCH, col_hot, *after)


def climb_kernel(pick, *refs):
    batch = BATCH
    x_refs, mid_refs, row2_refs, row1_refs = (
        refs[k * batch : (k + 1) * batch] for k in range(4)
    )
    got_ref, col2_ref, col1_ref = refs[4 * batch : 4 * batch + 3]
    out_ref = refs[-1]
    col_tiles, n = out_ref.shape[1], out_ref.shape[2]
    for b in range(batch):
        hot2 = one_hot(row2_refs[b][0], n)
        hot1 = one_hot(row1_refs[b][0], n)
        for c in range(col_tiles):
            tile = tile_of(x_refs[b], c, col_tiles, n).astype(BF16)
            half = mxu(hot2, tile).astype(BF16)
            whole = mxu(half, col2_ref[c]) + got_ref[b, c].astype(F32)
            whole = (whole + tile_of(mid_refs[b], c, col_tiles, n)).astype(BF16)
            half = mxu(hot1, whole).astype(BF16)
            out_ref[b, c] = mxu(half, col1_ref[c]).astype(BF16)


def climb(pick, first, count, leaf_rows, mid_rows, got, tiles, row2, row1, col2, col1, *after):
    _, col_tiles, n, _ = got.shape
    rows = mid_rows.shape[0] // tiles

    def mid(b):
        return lambda i, s: 2 * (first + BATCH * i + b) + s[1]

    def leaf(b):
        return lambda i, s: 2 * mid(b)(i, s) + s[0]

    batch = range(BATCH)
    return pl.pallas_call(
        climb_kernel,
        grid_spec=pltpu.PrefetchScalarGridSpec(
            num_scalar_prefetch=1,
            grid=(count // BATCH,),
            in_specs=[
                *[lane_spec(rows, leaf(b)) for b in batch],
                *[lane_spec(rows, mid(b)) for b in batch],
                *[place_spec(n, leaf(b)) for b in batch],
                *[place_spec(n, mid(b)) for b in batch],
                pl.BlockSpec(
                    (BATCH, col_tiles, n, n), lambda i, s: (first // BATCH + i, 0, 0, 0)
                ),
                whole_spec(col2),
                whole_spec(col1),
                *[pl.BlockSpec(memory_space=pl.ANY) for _ in after],
            ],
            out_specs=pl.BlockSpec((BATCH, col_tiles, n, n), lambda i, s: (i, 0, 0, 0)),
        ),
        out_shape=jax.ShapeDtypeStruct((count, col_tiles, n, n), BF16),
        compiler_params=pltpu.CompilerParams(vmem_limit_bytes=VMEM),
        cost_estimate=pl.CostEstimate(
            flops=count * col_tiles * 8 * 2 * n**3,
            bytes_accessed=count * col_tiles * n * n * 12,
            transcendentals=0,
        ),
        name="climb_middle",
    )(
        pick,
        *[leaf_rows] * BATCH,
        *[mid_rows] * BATCH,
        *[row2] * BATCH,
        *[row1] * BATCH,
        got,
        col2,
        col1,
        *after,
    )


def split2(value):
    high = value.astype(BF16)
    return high, (value - high.astype(F32)).astype(BF16)


def tiles_a_step(col_tiles):
    return 2 if col_tiles % 2 == 0 else 1


def raw_specs(raw, first, count):
    _, col_tiles, n, _ = raw[0].shape
    batch = tiles_a_step(col_tiles)
    steps = col_tiles // batch

    def own_index(i, s):
        return (first // count, jnp.minimum(i, steps - 1), 0, 0)

    def row_index(which, came):
        def index(i, s):
            at = jnp.clip(i - (which + 1) * steps, 0, steps - 1)
            return (first // count, jnp.where(s[1] == came, at, 0), 0, 0)

        return index

    indices = [own_index] + [row_index(w, c) for w in (0, 1) for c in (0, 1)]
    return [pl.BlockSpec((count, batch, n, n), index) for index in indices]


def raw_tile(pick, refs, k, b):
    own, stayed_a, came_a, stayed_b, came_b = (ref[k, b] for ref in refs)
    i, steps, came = pl.program_id(0), pl.num_programs(0) // 3, pick[1] != 0
    first = jnp.where(came, came_a, stayed_a)
    second = jnp.where(came, came_b, stayed_b)
    return jnp.where(i < steps, own, jnp.where(i < 2 * steps, first, second))


def tile_spec(x, batch):
    return pl.BlockSpec((x.shape[0], batch, *x.shape[2:]), lambda i, s: (0, i, 0, 0))


def solved(inverse_ref, at, rows):
    high, low = inverse_ref[at, 0], inverse_ref[at, 1]
    total = mxu(high, rows[0]) + mxu(low, rows[0])
    if len(rows) > 1:
        total += mxu(high, rows[1])
    return total.astype(BF16)


def leaf_local_kernel(pick, inverse_ref, place_ref, *refs):
    raw, out_ref = refs[:5], refs[-1]
    fronts, batch, n, _ = out_ref.shape
    for b in range(batch):
        for f in range(fronts):
            factor = solved(inverse_ref, f, [raw_tile(pick, raw, f, b)])
            out_ref[f, b] = mxu_t(one_hot(place_ref[f, b], n), factor).astype(BF16)


def middle_local_kernel(pick, inverse_ref, place_ref, pivot_ref, leaf_ref, *refs):
    raw, out_ref = refs[:5], refs[-1]
    _, batch, n, _ = out_ref.shape
    for b in range(batch):
        for p in range(2):
            rows = raw_tile(pick, raw, p, b).astype(F32)
            for f in (p, p + 2):
                rows -= mxu_t(pivot_ref[f], leaf_ref[f, b])
            hot = one_hot(place_ref[p, b], n)
            factor = solved(inverse_ref, p, split2(rows))
            out_ref[4 + p, b] = mxu_t(hot, factor).astype(BF16)
            for f in (p, p + 2):
                out_ref[f, b] = mxu(hot, leaf_ref[f, b]).astype(BF16)


def root_local_kernel(pick, inverse_ref, place_ref, pivot_ref, panel_ref, *refs):
    raw, out_ref = refs[:5], refs[-1]
    _, batch, n, _ = out_ref.shape
    for b in range(batch):
        rows = raw_tile(pick, raw, 0, b).astype(F32)
        for k in range(panel_ref.shape[0]):
            rows -= mxu_t(pivot_ref[k], panel_ref[k, b])
        factor = solved(inverse_ref, 0, split2(rows))
        out_ref[0, b] = mxu_t(one_hot(place_ref[0, b], n), factor).astype(BF16)


def local(kernel, name, pick, inverse, places, constants, tiled, raw, first, count, panels, *after):
    _, col_tiles, n, _ = raw[0].shape
    tiles = 3 * col_tiles
    batch = tiles_a_step(col_tiles)
    return pl.pallas_call(
        kernel,
        grid_spec=pltpu.PrefetchScalarGridSpec(
            num_scalar_prefetch=1,
            grid=(tiles // batch,),
            in_specs=[
                whole_spec(inverse),
                tile_spec(places, batch),
                *[whole_spec(x) for x in constants],
                *[tile_spec(x, batch) for x in tiled],
                *raw_specs(raw, first, count),
                *[pl.BlockSpec(memory_space=pl.ANY) for _ in after],
            ],
            out_specs=pl.BlockSpec((panels, batch, n, n), lambda i, s: (0, i, 0, 0)),
        ),
        out_shape=jax.ShapeDtypeStruct((panels, tiles, n, n), BF16),
        compiler_params=pltpu.CompilerParams(vmem_limit_bytes=VMEM),
        cost_estimate=pl.CostEstimate(
            flops=tiles * panels * 5 * 2 * n**3,
            bytes_accessed=tiles * panels * n * n * 6,
            transcendentals=0,
        ),
        name=name,
    )(pick, inverse, places, *constants, *tiled, *raw, *after)


def finish_kernel(levels, counts, pick, root_ref, *refs):
    part_refs = refs[: sum(counts)]
    panels = refs[sum(counts) : sum(counts) + 3 * levels]
    out_ref = refs[sum(counts) + 3 * levels]
    scratch, *part_bufs, part_sem = refs[sum(counts) + 3 * levels + 1 :]
    step = pl.program_id(0)
    tiles, col_tiles, n, _ = part_bufs[0].shape
    halves = n // LANES
    rows = n * col_tiles * halves
    spread = tiles // col_tiles

    part_copies = []
    for which, count in enumerate(counts):
        size = tiles // count
        for q in range(count):
            at = len(part_copies)
            target = part_bufs[which].at[pl.ds(q * size, size)]
            part_copies.append(
                pltpu.make_async_copy(part_refs[at], target, part_sem.at[at])
            )

    @pl.when(step == 0)
    def _():
        for copy in part_copies:
            copy.start()
        for copy in part_copies:
            copy.wait()

    for which in range(spread):
        j = pick[0] ^ which
        for c in range(col_tiles):
            total = tile_of(
                root_ref, c, col_tiles, n, pl.multiple_of(j * rows, rows)
            )
            for part_buf in part_bufs:
                total += part_buf[step * spread + j, c].astype(F32)
            update = None
            for level in range(levels):
                col_ref, *row_refs = panels[3 * level : 3 * level + 3]
                for k in range(col_ref.shape[0]):
                    term = mxu_t(row_refs[which][k, 0], col_ref[k, c])
                    update = term if update is None else update + term
            total -= update
            for h in range(halves):
                scratch[
                    which, pl.ds(h * col_tiles + c, n, stride=col_tiles * halves), :
                ] = total[:, h * LANES : (h + 1) * LANES]
        out_ref[pl.ds(pl.multiple_of(j * rows, rows), rows), :] = scratch[which].astype(BF16)


def finish(pick, root_rows, parts, panels):
    tiles = sum(x.shape[0] for x in parts[0])
    _, col_tiles, n, _ = parts[0][0].shape
    spread = tiles // col_tiles
    lane_rows = root_rows.shape[0] // col_tiles
    lanes = pl.BlockSpec((lane_rows, LANES), lambda c, s: (c, 0))
    flat = [x for part in parts for x in part]
    count = sum(x.shape[0] for x in panels)

    def panel_specs(x):
        k = x.shape[0]
        return [
            pl.BlockSpec((k, col_tiles, n, n), lambda c, s: (0, 0, 0, 0)),
            pl.BlockSpec((k, 1, n, n), lambda c, s: (0, col_tiles + c, 0, 0)),
            pl.BlockSpec((k, 1, n, n), lambda c, s: (0, 2 * col_tiles + c, 0, 0)),
        ]

    return pl.pallas_call(
        functools.partial(finish_kernel, len(panels), [len(x) for x in parts]),
        grid_spec=pltpu.PrefetchScalarGridSpec(
            num_scalar_prefetch=1,
            grid=(col_tiles,),
            in_specs=[
                lanes,
                *[pl.BlockSpec(memory_space=pl.ANY) for _ in flat],
                *[spec for x in panels for spec in panel_specs(x)],
            ],
            out_specs=lanes,
            scratch_shapes=[
                pltpu.VMEM((spread, lane_rows // spread, LANES), F32),
                *[pltpu.VMEM((tiles, col_tiles, n, n), BF16) for _ in parts],
                pltpu.SemaphoreType.DMA((len(flat),)),
            ],
        ),
        out_shape=jax.ShapeDtypeStruct(root_rows.shape, BF16),
        compiler_params=pltpu.CompilerParams(vmem_limit_bytes=VMEM),
        cost_estimate=pl.CostEstimate(
            flops=tiles * col_tiles * (count + 3) * 2 * n**3,
            bytes_accessed=tiles * col_tiles * n * n * 10,
            transcendentals=0,
        ),
        name="finish_root",
    )(pick, root_rows, *flat, *[x for x in panels for _ in range(3)])


def strip(front, tile_row, groups, member, bits):
    piece = jnp.transpose(front[tile_row // groups], (1, 0, 2))
    if groups > 1:
        piece = jnp.where(member == tile_row % groups, piece, 0.0)
    return group_sum(piece, bits)


def solve(inverse, rows):
    return jnp.einsum("ks,csj->cjk", inverse, rows, precision=HIGHEST)


def placed(hot, panels):
    return jnp.einsum(
        "cqj,cjk->cqk", hot, panels, preferred_element_type=F32
    ).astype(BF16)


def moved(row_hot, block, col_hot):
    out = jnp.einsum("qs,csj->cqj", row_hot, block, precision=HIGHEST)
    return jnp.einsum("cqj,cpj->cqp", out, col_hot, precision=HIGHEST)


def product(rows, cols):
    return jnp.einsum("fsk,fcjk->csj", rows, cols, preferred_element_type=F32)


def hots(places, n):
    slots = jnp.arange(n, dtype=jnp.int32)
    return (places[:, None, :] == slots[None, :, None]).astype(BF16)


def places_of(scatter, order, pivot):
    _, tiles, n = scatter.shape
    tile_ids = jnp.arange(tiles, dtype=jnp.int32)[:, None]
    rows = tile_ids * n + jnp.arange(n, dtype=jnp.int32)[None, :]
    keep = (rows < order[:, None, None]) & (tile_ids != pivot)
    return jnp.where(keep, scatter, -1)


def panel_slices(panel_pair, sizes, members):
    n_tile = lax.axis_size("tile")
    stacked = jnp.stack(panel_pair)
    count, col_tiles, n, width = stacked.shape
    cut = stacked.reshape(count, col_tiles, n_tile, n // n_tile, width)
    cut = jnp.transpose(cut, (2, 0, 1, 3, 4))
    got = lax.all_to_all(cut, "tile", 0, 0, tiled=True)
    out = []
    for at in range(count):
        tiles = jnp.transpose(got[:, at], (1, 0, 2, 3))
        tiles = tiles.reshape(-1, sizes[at], n // n_tile, width)
        out.append(lax.dynamic_index_in_dim(tiles, members[at], 1, keepdims=True))
    return out


def per_device(
    leaf_fronts, middle_fronts, root_front, leaf_scatter, middle_scatter, leaf_orders, middle_orders
):
    n_cube, n_tile = lax.axis_size("cube"), lax.axis_size("tile")
    cube, tile = lax.axis_index("cube"), lax.axis_index("tile")
    g2, g1 = n_cube // 4, n_cube // 2
    bit2, bit1 = g2.bit_length() - 1, g1.bit_length() - 1
    f, p = cube // g2, cube // g1
    m2, m1 = cube % g2, cube % g1
    leaf_tiles, n, col_tiles, _ = leaf_fronts.shape
    mid_tiles = middle_fronts.shape[0]
    col_ids = jnp.arange(col_tiles, dtype=jnp.int32) * n_tile + tile
    spread = n_tile // n_cube
    front_ids = jnp.stack([f, f ^ 2, f ^ 1, f ^ 3])
    middle_ids = jnp.stack([p, p ^ 1])
    all2 = jnp.take(places_of(leaf_scatter, leaf_orders, 0), front_ids, axis=0)
    all1 = jnp.take(places_of(middle_scatter, middle_orders, 1), middle_ids, axis=0)
    high = tile // n_cube
    cols = jnp.arange(col_tiles, dtype=jnp.int32) * n_tile
    tile_ids = jnp.concatenate(
        [cols + tile, cols + cube + n_cube * high, cols + cube + n_cube * (high ^ 1)]
    )
    local2 = jnp.take(all2, tile_ids, axis=1)[:, :, None]
    local1 = jnp.take(all1, tile_ids, axis=1)[:, :, None]
    straight = jnp.arange(n, dtype=jnp.int32)
    local0 = jnp.where((tile_ids == 2)[:, None], -1, straight)[None, :, None]
    places2, places1 = all2[0], all1[0]
    cols2, cols1 = local2[0, :col_tiles, 0], local1[0, :col_tiles, 0]
    hot2, hot1 = hots(cols2, n), hots(cols1, n)
    top2, top1 = hots(places2[1:3], n), hots(all1[:, 2], n)
    slots = jnp.arange(n, dtype=jnp.int32)
    turned2 = (cols2[:, :, None] == slots).astype(BF16)
    turned1 = (cols1[:, :, None] == slots).astype(BF16)

    def at_tile(strips, tile_id):
        return strips[tile_id // n_tile]

    leaf0 = strip(leaf_fronts, 0, g2, m2, bit2)
    (corner2, ahead_1, ahead_2), stages = tile_spread(at_tile(leaf0, 0))

    rows2 = places2.reshape(-1, g2, 1, n)[:, m2]
    rows1 = places1.reshape(-1, g1, 1, n)[:, m1]
    parity2, parity1 = f % 2, p % 2
    leaf_lanes, mid_lanes, root_lanes = map(
        lane_rows, (leaf_fronts, middle_fronts, root_front)
    )
    got2, before, lifts = [], [], []
    for half in (1 - parity1, parity1):
        pick = jnp.stack([1 - parity2, half])
        sent = lift(pick, leaf_lanes, leaf_tiles, rows2, turned2, *before)
        got2.append(partner(sent, bit2))
        lifts.append(sent)
        before = [sent, stages[-2]] if len(stages) > 1 else [sent]

    def climbed(half, first, count, got, *after):
        pick = jnp.stack([parity2, half])
        return climb(
            pick, first, count, leaf_lanes, mid_lanes, got, mid_tiles, rows2, rows1, turned2, turned1, *after
        )

    count = mid_tiles // 2
    part = max(count // 2, BATCH)
    sent1 = []
    for first in range(0, count, part):
        before = [sent1[-1], corner2] if sent1 else [sent, stages[-1]]
        sent1.append(climbed(1 - parity1, first, part, got2[0], *before))
    got1 = [partner(x[at : at + BATCH], bit1) for x in sent1 for at in range(0, part, BATCH)]

    pieces = [strip(leaf_fronts, r, g2, m2, bit2) for r in (1, 2)]
    pieces = [gate(x, lifts[0]) for x in pieces]
    lifted = jnp.stack(
        [
            moved(top2[r - 1].astype(F32), pieces[r - 1], hot2.astype(F32))
            + strip(middle_fronts, r, g1, m1, bit2)
            for r in (1, 2)
        ]
    )
    base1 = lifted + partner(lifted, bit2)
    raised = moved(top1[0].astype(F32), base1[1], hot1.astype(F32))
    raised = raised + strip(root_front, 2, n_cube, cube, bit1)
    even = cube % 2 == 0
    rows1_, raised_ = base1[0].astype(BF16), raised.astype(BF16)
    mixed = partner(jnp.where(even, rows1_, raised_), bit1)
    mixed_too = partner(mixed, 0)
    far_rows1 = jnp.where(even, mixed, mixed_too)
    far_raised = jnp.where(even, mixed_too, mixed)
    base0 = raised + far_raised.astype(F32)
    both0 = (raised_.astype(F32) + far_raised.astype(F32)).astype(BF16)
    raw1 = jnp.stack([rows1_, far_rows1, both0])
    raw1 = [raw1, *row_spread(raw1)]
    is_one = tile % n_tile == 1
    ends = jnp.stack(
        [jnp.where(is_one, at_tile(base1[0], 1), at_tile(base1[0], 2)), at_tile(raised, 2)]
    )
    (_, ends1, ends2), _ = tile_spread(ends)
    end0 = ends2[1] + partner(ends2[1], bit1)

    near = leaf0.astype(BF16)
    near = jnp.stack([near, partner(near, bit1)])
    raw2 = jnp.concatenate([near, partner(near, bit2)])
    raw2 = [raw2, *row_spread(raw2)]
    picks = jnp.stack([high, (tile ^ cube) & 1])

    upper2, inverse2, parts2 = cholesky(corner2, sent1[-1])
    ahead2 = solve(inverse2, jnp.stack([ahead_1, ahead_2])).astype(BF16)
    pay2 = jnp.concatenate([parts2, placed(top2, ahead2)])
    pair2 = partner(pay2, bit2)
    across2 = partner(pay2, bit1)
    all_pay2 = jnp.stack([pay2, across2, pair2, partner(across2, bit2)])
    kept1 = [climbed(parity1, 0, part, got2[1], pay2)]

    one2 = jnp.stack([pay2[2], pair2[2]])
    two2 = jnp.stack([pay2[3], pair2[3]])
    ends = product(one2, jnp.stack([one2, two2], axis=1))
    upper1, inverse1, parts1 = cholesky(ends1[0] - ends[0], kept1[-1])
    two1 = solve(inverse1, (ends2[0] - ends[1])[None]).astype(BF16)
    pay1 = jnp.concatenate([parts1, placed(top1[:1], two1)])
    both1 = jnp.stack([pay1, partner(pay1, bit1)])
    leaf_tiles_ = local(
        leaf_local_kernel, "leaf_rows", picks, all_pay2[:, :2], local2, [], [], raw2, 0, 4, 4,
        pay1, got1[0],
    )
    if part < count:
        kept1.append(climbed(parity1, part, part, got2[1], pay1))
    middle_tiles_ = local(
        middle_local_kernel, "middle_rows", picks, both1[:, :2], local1,
        [all_pay2[:, 2]], [leaf_tiles_], raw1, 0, 2, 6, kept1[-1], *got1[1:2],
    )

    two2 = placed(jnp.concatenate([top1, top1]), all_pay2[:, 3])
    six = jnp.concatenate([two2, both1[:, 2]])
    ends = product(six, six[:, None])
    upper0, inverse0, parts0 = cholesky(end0 - ends[0], kept1[-1])
    root_tiles_ = local(
        root_local_kernel, "root_rows", picks, parts0[None], local0,
        [six], [middle_tiles_], raw1, 2, 1, 1, *got1[2:3],
    )

    schur = finish(picks, root_lanes, [kept1, got1], [middle_tiles_, root_tiles_])
    schur = schur.reshape(root_front.shape[0], n, n // LANES, col_tiles, LANES)
    schur = schur.transpose(0, 1, 3, 2, 4).reshape(root_front.shape)

    panel2 = solve(inverse2, leaf0).astype(BF16)
    front1 = base1[0] - product(one2, leaf_tiles_[0::2, :col_tiles])
    panel1 = solve(inverse1, front1).astype(BF16)

    def with_corner(panel, upper, pivot):
        return jnp.where((col_ids == pivot)[:, None, None], upper.T.astype(BF16), panel)

    front0 = base0 - product(six, middle_tiles_[:, :col_tiles])
    panel0 = solve(inverse0, front0).astype(BF16)
    leaf_panel, middle_panel = panel_slices(
        (with_corner(panel2, upper2, 0), with_corner(panel1, upper1, 1)),
        (g2, g1),
        (m2, m1),
    )
    [root_panel] = panel_slices([with_corner(panel0, upper0, 2)], [n_cube], [cube])
    return leaf_panel, middle_panel, root_panel, schur


def solution(mesh):
    front = P(None, "cube", None, "tile")
    panel = P(None, "cube", "tile", None)
    return jax.shard_map(
        per_device,
        mesh=mesh,
        in_specs=(front, front, front, P(), P(), P(), P()),
        out_specs=(panel, panel, panel, front),
        check_vma=False,
    )
```
